32 devices in a mesh: gx: 8 (over z, x), gy: 4 (over y, core).
Axes of the slice: x: 2, y: 2, z: 4, core: 2. Of those that a mesh axis runs over, the one named last changes fastest.
Arguments:
- a_blocks: bfloat16 [8, 32, 64, 448], P('gx', 'gy'), may hold values from -0.25 to 0.25
- a_cols: int32 [8, 32, 7], P('gx', 'gy'), may hold values from 0 to 15
- mushy: int32 [8, 32], P('gx', 'gy'), may hold values 0 or 1
- p_blocks: bfloat16 [8, 32, 64, 256], P('gx', 'gy'), may hold values from -0.375 to 0.375
- p_cols: int32 [8, 32, 4], P('gx', 'gy'), may hold values from 0 to 7
- send_rows: int32 [8, 32], P('gx', 'gy'), may hold values from 0 to 7
Outputs:
- coarse_tiles: float32 [8, 512, 1536], P('gx', 'gy')
The draws below stay inside these ranges and needn't reach their ends.
All inputs are finite; a program needn't handle non-finite values. No bound on the sum of `mushy` on one device may be relied on, other than what follows from the above.
Results may differ from the reference program's by a relative error of at most 0.0038.
Values may be sent and summed in bfloat16 or wider, within the bound.
No kernel may reach another device: no remote copies, remote signals or barrier semaphores. Data moves between devices by JAX's collectives and lax.ppermute only.
A program may use at most 64 MiB of HBM per device.

```python
import jax
import jax.numpy as jnp
from jax import lax

BS = 64
KA = 7
KS = 3
KP = 4
NCOL = 8
G = 4
NB = 8
ROWS = 32
N_GX = 8
N_GY = 4


def place_ends(entries, rng, least, largest):
    longest = entries.shape.index(max(entries.shape))
    spots = []
    for shift in (0, 1):
        where = [jax.random.randint(jax.random.fold_in(rng, axis), (), 0, length) for axis, length in enumerate(entries.shape)]
        where[longest] = (where[longest] + shift) % entries.shape[longest]
        spots.append(tuple(where))
    return entries.at[spots[0]].set(least).at[spots[1]].set(largest)


def levels(key, extent, cuts, least, top_value):
    factor_of, own = 1.0, jax.random.fold_in(key, 6)
    for axis_at, shards_of in cuts:
        steps = jnp.exp(jax.random.uniform(jax.random.fold_in(own, axis_at), (shards_of,), jnp.float32, least / len(cuts), top_value / len(cuts)))
        factor_of = factor_of * jnp.repeat(steps, extent[axis_at] // shards_of).reshape([-1 if axis == axis_at else 1 for axis in range(len(extent))])
    return factor_of


def bell_draw(own_key, extent, width, most, cuts=(), kind=jnp.bfloat16):
    array = width * jax.random.normal(own_key, extent, jnp.float32)
    if cuts:
        array = array * levels(own_key, extent, cuts, -0.22, 0.18)
    return jnp.clip(array, -most, most).astype(kind)


def setup_inputs(seed: int = 0) -> dict:
    key_of = jax.random.split(jax.random.key(seed), 7)
    return {
        "a_blocks": bell_draw(key_of[0], (N_GX, ROWS, BS, KA * BS), (KA * BS) ** -0.5, 0.25, ((0, 8), (1, 4))),
        "a_cols": place_ends(jax.random.randint(key_of[1], (N_GX, ROWS, KA), 0, NB + 2 * G), jax.random.fold_in(key_of[1], 1), 0, (NB + 2 * G) - 1).astype(jnp.int32),
        "mushy": place_ends((jax.random.randint(key_of[2], (N_GX, ROWS), 0, 3) < 1).astype(jnp.int32), jax.random.fold_in(key_of[2], 1), 0, 1),
        "p_blocks": bell_draw(key_of[3], (N_GX, ROWS, BS, KP * BS), (4 * BS) ** -0.5, 0.375, ((0, 8), (1, 4))),
        "p_cols": place_ends(jax.random.randint(key_of[4], (N_GX, ROWS, KP), 0, NCOL), jax.random.fold_in(key_of[4], 1), 0, NCOL - 1).astype(jnp.int32),
        "send_rows": place_ends(jax.random.randint(key_of[5], (N_GX, N_GY * 2 * G), 0, NB), jax.random.fold_in(key_of[5], 1), 0, NB - 1).astype(jnp.int32),
    }


def dense_rows(blocks, cols, offset, width_blocks):
    count = blocks.shape[0]
    size = blocks.shape[1]
    slots = cols.shape[1]
    onehot = (cols[:, :, None] + offset == jnp.arange(width_blocks, dtype=jnp.int32)[None, None, :]).astype(jnp.float32)
    parts = blocks.reshape(count, size, slots, size).astype(jnp.float32)
    dense = jnp.einsum('rkc,rbka->rbca', onehot, parts)
    return dense.astype(jnp.bfloat16).reshape(count, size, width_blocks * size)


def device_term(ablk, acol, mush, pblk, pcol, left_blk, left_col, right_blk, right_col):
    extended = jnp.concatenate([
        dense_rows(pblk, pcol, NCOL, 3 * NCOL),
        dense_rows(left_blk, left_col, 0, 3 * NCOL),
        dense_rows(right_blk, right_col, 2 * NCOL, 3 * NCOL)], axis=0)
    limit = jnp.where(mush > 0, KA, KS).astype(jnp.int32)
    total = jnp.zeros((NB, BS, 3 * NCOL * BS), jnp.float32)
    for slot in range(KA):
        live = (slot < limit).astype(jnp.bfloat16)
        ablock = ablk[:, :, slot * BS:(slot + 1) * BS] * live[:, None, None]
        picked = extended[acol[:, slot]]
        total = total + jnp.einsum('nij,njw->niw', ablock.astype(jnp.float32), picked.astype(jnp.float32))
    product = total.astype(jnp.bfloat16)
    own = dense_rows(pblk, pcol, 0, NCOL)
    return jnp.einsum('nbc,nbw->cw', own.astype(jnp.float32), product.astype(jnp.float32))


def reference(a_blocks, a_cols, mushy, p_blocks, p_cols, send_rows):
    a4 = a_blocks.reshape(N_GX, N_GY, NB, BS, KA * BS)
    ac4 = a_cols.reshape(N_GX, N_GY, NB, KA)
    m4 = mushy.reshape(N_GX, N_GY, NB)
    p4 = p_blocks.reshape(N_GX, N_GY, NB, BS, KP * BS)
    pc4 = p_cols.reshape(N_GX, N_GY, NB, KP)
    s4 = send_rows.reshape(N_GX, N_GY, 2 * G)

    def column(col):
        left_g = jnp.maximum(col - 1, 0)
        right_g = jnp.minimum(col + 1, N_GX - 1)
        left_flag = (col > 0).astype(jnp.bfloat16)
        right_flag = (col < N_GX - 1).astype(jnp.bfloat16)

        def device(carry, row):
            left_sel = s4[left_g, row, G:]
            right_sel = s4[right_g, row, :G]
            left_blk = p4[left_g, row][left_sel] * left_flag
            left_col = pc4[left_g, row][left_sel]
            right_blk = p4[right_g, row][right_sel] * right_flag
            right_col = pc4[right_g, row][right_sel]
            term = device_term(a4[col, row], ac4[col, row], m4[col, row], p4[col, row], pc4[col, row],
                               left_blk, left_col, right_blk, right_col)
            return carry + term, None

        start = jnp.zeros((NCOL * BS, 3 * NCOL * BS), jnp.float32)
        summed, unused = lax.scan(device, start, jnp.arange(N_GY, dtype=jnp.int32))
        return summed

    return lax.map(column, jnp.arange(N_GX, dtype=jnp.int32))
```

```python
import functools

import jax
import jax.numpy as jnp
from jax import lax
from jax.experimental import pallas as pl
from jax.experimental.pallas import tpu as pltpu
from jax.sharding import PartitionSpec as P

KA = 7
KS = 3
NCOL = 8
LANES = 128

F32 = jnp.float32
BF16 = jnp.bfloat16
SMEM = pl.BlockSpec(memory_space=pltpu.SMEM)
VMEM = pl.BlockSpec(memory_space=pltpu.VMEM)


def halves(tile):
    low = lax.broadcasted_iota(jnp.int32, tile.shape, 1) < LANES // 2
    swapped = pltpu.roll(tile, LANES // 2, 1)
    return jnp.where(low, tile, swapped), jnp.where(low, swapped, tile)


def place(blocks, cols, slots, tile):
    total = None
    for block, col in zip(blocks, cols):
        term = block * jnp.where(slots == col - 2 * tile, 1.0, 0.0).astype(F32)
        total = term if total is None else total + term
    return total


def pack_kernel(sends, pcol, p_ref, first_ref, second_ref):
    odd = lax.axis_index("gx") % 2
    count = sends.shape[0] // 2
    size = p_ref.shape[1]
    slots = pcol.shape[0]
    for out_ref, start in ((first_ref, (1 - odd) * count), (second_ref, odd * count)):
        tail = out_ref.shape[0] - count * size
        which = lax.broadcasted_iota(jnp.int32, (tail, out_ref.shape[1]), 0)
        cols = jnp.zeros(which.shape, F32)
        for s in range(count):
            row = sends[start + s]
            out_ref[s * size : (s + 1) * size, :] = p_ref[row]
            for j in range(slots):
                cols = jnp.where(which == s * slots + j, pcol[j, row].astype(F32), cols)
        out_ref[count * size :, :] = cols.astype(BF16)


def own_kernel(parts, acol, mush, pcol, a_ref, p_ref, ownt_ref, ghost_ref, ap_ref, own_ref, mid_ref):
    odd = lax.axis_index("gx") % 2
    bit = lax.axis_index("gy") % 2
    rows, size = p_ref.shape[0], p_ref.shape[1]
    width = NCOL * size
    count = ghost_ref.shape[3] // size
    share = width // parts
    half = lax.broadcasted_iota(jnp.int32, (1, LANES), 1) // size

    def build(n, carry):
        at = pl.ds(pl.multiple_of(n * size, size), size)
        blocks, cols = [], []
        for q in range(pcol.shape[0] // 2):
            tile = p_ref[n, :, q * LANES : (q + 1) * LANES].astype(F32)
            blocks += halves(tile)
        cols = [pcol[j, n] for j in range(pcol.shape[0])]
        for c in range(width // LANES):
            own_ref[at, c * LANES : (c + 1) * LANES] = place(blocks, cols, half, c).astype(BF16)
        limit = jnp.where(mush[n] > 0, KA, KS)
        blocks, cols = [], []
        for q in range(KA // 2):
            tile = a_ref[n, :, q * LANES : (q + 1) * LANES].astype(F32)
            blocks += halves(tile)
        last = a_ref[n, :, (KA - 1) * size :].astype(F32)
        blocks.append(jnp.concatenate([last, last], axis=1))
        cols = [jnp.where(k < limit, acol[k, n], -1) for k in range(KA)]
        for c in range((rows + 2 * count) * size // LANES):
            value = place(blocks, cols, half, c)
            high = value.astype(BF16)
            low = (value - high.astype(F32)).astype(BF16)
            if c < rows * size // LANES:
                spot = slice(c * LANES, (c + 1) * LANES)
                mid_ref[0, at, spot] = high
                mid_ref[1, at, spot] = low
            else:
                side, tile = divmod(c - rows * size // LANES, count * size // LANES)
                spot = slice(tile * LANES, (tile + 1) * LANES)
                order = 1 - odd if side == 0 else odd
                ghost_ref[order, 0, at, spot] = high
                ghost_ref[order, 1, at, spot] = low
        return carry

    lax.fori_loop(0, rows, build, 0)
    for c in range(width // LANES):
        flipped = own_ref[:, c * LANES : (c + 1) * LANES].T
        for k in range(LANES // share):
            part = c * (LANES // share) + k
            spot = part // 2 + jnp.where(part % 2 == bit, 0, parts // 2)
            at = pl.ds(pl.multiple_of(spot * share, share), share)
            ownt_ref[at, :] = flipped[k * share : (k + 1) * share, :]
    own = own_ref[...]
    step = width // 2
    for m in range(2):
        at = slice(m * step, (m + 1) * step)
        value = jnp.dot(mid_ref[0, at, :], own, preferred_element_type=F32)
        value += jnp.dot(mid_ref[1, at, :], own, preferred_element_type=F32)
        ap_ref[at, :] = value.astype(BF16)


def ghost_kernel(first_ref, second_ref, ownt_ref, ghost_ref, ap_ref, keep_ref, send_ref, ext_ref, prod_ref):
    odd = lax.axis_index("gx") % 2
    width = ownt_ref.shape[0]
    size = width // NCOL
    count = ghost_ref.shape[3] // size
    half = (lax.broadcasted_iota(jnp.int32, (1, LANES), 1) // size).astype(F32)
    rows = keep_ref.shape[1] * keep_ref.shape[2]

    def finish(third, prod):
        kept = jnp.dot(ownt_ref[:rows, :], prod, preferred_element_type=F32)
        keep_ref[third] = kept.reshape(keep_ref.shape[1:])
        sent = jnp.dot(ownt_ref[rows:, :], prod, preferred_element_type=F32)
        send_ref[third] = sent.astype(BF16).reshape(send_ref.shape[1:])

    finish(1, ap_ref[...])
    for order, in_ref in enumerate((first_ref, second_ref)):
        slots = in_ref.shape[1] // size
        cols = in_ref[count * size :, :LANES].astype(F32)
        for s in range(count):
            blocks = []
            for q in range(slots // 2):
                tile = in_ref[s * size : (s + 1) * size, q * LANES : (q + 1) * LANES].astype(F32)
                blocks += halves(tile)
            mine = [cols[s * slots + j : s * slots + j + 1, :] for j in range(slots)]
            for c in range(width // LANES):
                spot = slice(c * LANES, (c + 1) * LANES)
                ext_ref[s * size : (s + 1) * size, spot] = place(blocks, mine, half, c).astype(BF16)
        ext = ext_ref[...]
        step = width // 2
        for m in range(2):
            at = slice(m * step, (m + 1) * step)
            value = jnp.dot(ghost_ref[order, 0, at, :], ext, preferred_element_type=F32)
            value += jnp.dot(ghost_ref[order, 1, at, :], ext, preferred_element_type=F32)
            prod_ref[at, :] = value.astype(BF16)
        third = 2 * (1 - odd) if order == 0 else 2 * odd
        finish(third, prod_ref[...])


def fold_kernel(stage, keep_ref, recv_ref, next_ref, send_ref):
    bit = (lax.axis_index("gy") >> stage) % 2
    for i in range(next_ref.shape[1]):
        mine, other = 2 * i + bit, 2 * i + 1 - bit
        next_ref[0, i] = keep_ref[0, mine] + recv_ref[0, mine].astype(F32)
        send_ref[0, i] = (keep_ref[0, other] + recv_ref[0, other].astype(F32)).astype(BF16)


def last_kernel(keep_ref, recv_ref, out_ref):
    out_ref[...] = keep_ref[0, 0] + recv_ref[0, 0].astype(F32)


def swapped(value, axis, step):
    length = lax.axis_size(axis)
    return lax.ppermute(value, axis, [(i, i ^ step) for i in range(length) if i ^ step < length])


def body(a_blocks, a_cols, mushy, p_blocks, p_cols, send_rows):
    ablk, pblk = a_blocks[0], p_blocks[0]
    acol, pcol = a_cols[0].T, p_cols[0].T
    mush, sends = mushy[0], send_rows[0]
    rows, size, inner = pblk.shape
    count = sends.shape[0] // 2
    width = NCOL * size
    length = lax.axis_size("gx")
    parts = lax.axis_size("gy")
    share = width // parts
    high = pltpu.CompilerParams(vmem_limit_bytes=32 * 1024 * 1024)

    tail = -(-count * pcol.shape[0] // 16) * 16
    packed = jax.ShapeDtypeStruct((count * size + tail, inner), BF16)
    first, second = pl.pallas_call(
        pack_kernel,
        out_shape=(packed, packed),
        in_specs=[SMEM, SMEM, VMEM],
        out_specs=(VMEM, VMEM),
        compiler_params=high,
        name="pack",
    )(sends, pcol, pblk)
    even = [(i, i + 1) for i in range(0, length - 1, 2)]
    uneven = [(i, i + 1) for i in range(1, length - 1, 2)]
    first = lax.ppermute(first, "gx", even + [(j, i) for i, j in even])
    second = lax.ppermute(second, "gx", uneven + [(j, i) for i, j in uneven])

    own_t, ghost, ap = pl.pallas_call(
        functools.partial(own_kernel, parts),
        out_shape=(
            jax.ShapeDtypeStruct((width, rows * size), BF16),
            jax.ShapeDtypeStruct((2, 2, rows * size, count * size), BF16),
            jax.ShapeDtypeStruct((rows * size, width), BF16),
        ),
        in_specs=[SMEM, SMEM, SMEM, VMEM, VMEM],
        out_specs=(VMEM, VMEM, VMEM),
        scratch_shapes=[
            pltpu.VMEM((rows * size, width), BF16),
            pltpu.VMEM((2, rows * size, rows * size), BF16),
        ],
        compiler_params=high,
        cost_estimate=pl.CostEstimate(flops=600000000, bytes_accessed=3000000, transcendentals=0),
        name="own",
    )(acol, mush, pcol, ablk, pblk)

    keep, send = pl.pallas_call(
        ghost_kernel,
        out_shape=(
            jax.ShapeDtypeStruct((3, parts // 2, share, width), F32),
            jax.ShapeDtypeStruct((3, parts // 2, share, width), BF16),
        ),
        in_specs=[VMEM] * 5,
        out_specs=(VMEM, VMEM),
        scratch_shapes=[
            pltpu.VMEM((count * size, width), BF16),
            pltpu.VMEM((rows * size, width), BF16),
        ],
        compiler_params=high,
        cost_estimate=pl.CostEstimate(flops=1400000000, bytes_accessed=5000000, transcendentals=0),
        name="ghost",
    )(first, second, own_t, ghost, ap)

    stage = 0
    left = parts // 2
    while left > 1:
        recv = swapped(send, "gy", 1 << stage)
        stage += 1
        full = pl.BlockSpec((1, left, share, width), lambda t: (t, 0, 0, 0))
        left //= 2
        part = pl.BlockSpec((1, left, share, width), lambda t: (t, 0, 0, 0))
        keep, send = pl.pallas_call(
            functools.partial(fold_kernel, stage),
            grid=(3,),
            out_shape=(
                jax.ShapeDtypeStruct((3, left, share, width), F32),
                jax.ShapeDtypeStruct((3, left, share, width), BF16),
            ),
            in_specs=[full, full],
            out_specs=(part, part),
            name="fold",
        )(keep, recv)
    recv = swapped(send, "gy", 1 << stage)
    part = pl.BlockSpec((1, 1, share, width), lambda t: (t, 0, 0, 0))
    result = pl.pallas_call(
        last_kernel,
        grid=(3,),
        out_shape=jax.ShapeDtypeStruct((share, 3 * width), F32),
        in_specs=[part, part],
        out_specs=pl.BlockSpec((share, width), lambda t: (0, t)),
        name="last",
    )(keep, recv)
    return result[None]


def solution(mesh):
    placed = (
        P("gx", "gy", None, None),
        P("gx", "gy", None),
        P("gx", "gy"),
        P("gx", "gy", None, None),
        P("gx", "gy", None),
        P("gx", "gy"),
    )
    return jax.shard_map(
        body, mesh=mesh, in_specs=placed, out_specs=P("gx", "gy", None), check_vma=False
    )
```

```python
import functools

import jax
import jax.numpy as jnp
from jax import lax
from jax.experimental import pallas as pl
from jax.experimental.pallas import tpu as pltpu
from jax.sharding import PartitionSpec as P

KA = 7
KS = 3
NCOL = 8
LANES = 128

F32 = jnp.float32
BF16 = jnp.bfloat16
SMEM = pl.BlockSpec(memory_space=pltpu.SMEM)
VMEM = pl.BlockSpec(memory_space=pltpu.VMEM)
HBM = pl.BlockSpec(memory_space=pltpu.HBM)
PARAMS = pltpu.CompilerParams(vmem_limit_bytes=24 * 1024 * 1024)


def halves(tile):
    low = lax.broadcasted_iota(jnp.int32, tile.shape, 1) < LANES // 2
    swapped = pltpu.roll(tile, LANES // 2, 1)
    return jnp.where(low, tile, swapped), jnp.where(low, swapped, tile)


def blocks_of(ref, at, slots):
    blocks = []
    for q in range(slots // 2):
        blocks += halves(ref[at + (slice(q * LANES, (q + 1) * LANES),)].astype(F32))
    if slots % 2:
        last = ref[at + (slice((slots - 1) * LANES // 2, slots * LANES // 2),)].astype(F32)
        blocks.append(jnp.concatenate([last, last], axis=1))
    return blocks


def place(blocks, cols, slots, tile):
    total = None
    for block, col in zip(blocks, cols):
        term = block * jnp.where(slots == col - 2 * tile, 1.0, 0.0).astype(F32)
        total = term if total is None else total + term
    return total


def scatter_rows(acol, mush, a_ref, base, high_ref, low_ref):
    rows, size = a_ref.shape[0], a_ref.shape[1]
    half = lax.broadcasted_iota(jnp.int32, (1, LANES), 1) // size

    def build(n, carry):
        at = pl.ds(pl.multiple_of(n * size, size), size)
        limit = jnp.where(mush[n] > 0, KA, KS)
        blocks = blocks_of(a_ref, (n, slice(None)), KA)
        cols = [jnp.where(k < limit, acol[k, 0, n] - base, -1) for k in range(KA)]
        for c in range(high_ref.shape[1] // LANES):
            value = place(blocks, cols, half, c)
            high = value.astype(BF16)
            spot = slice(c * LANES, (c + 1) * LANES)
            high_ref[at, spot] = high
            low_ref[at, spot] = (value - high.astype(F32)).astype(BF16)
        return carry

    lax.fori_loop(0, rows, build, 0)


def multiply(high_ref, low_ref, ext, prod_ref):
    step = prod_ref.shape[0] // 2
    for m in range(2):
        at = slice(m * step, (m + 1) * step)
        value = jnp.dot(high_ref[at, :], ext, preferred_element_type=F32)
        value += jnp.dot(low_ref[at, :], ext, preferred_element_type=F32)
        prod_ref[at, :] = value.astype(BF16)


def finish(ownt_ref, prod, keep_ref, send_ref):
    rows = ownt_ref.shape[0] // 2
    sent = jnp.dot(ownt_ref[rows:, :], prod, preferred_element_type=F32)
    send_ref[...] = sent.astype(BF16).reshape(send_ref.shape)
    kept = jnp.dot(ownt_ref[:rows, :], prod, preferred_element_type=F32)
    keep_ref[...] = kept.reshape(keep_ref.shape)


def pack_kernel(
    sends_in, pcol_in, acol_in, mush_in, a_in, p_in,
    first_ref, second_ref, a_ref, p_ref, pcol, acol, mush, sends, sems,
):
    copies = [
        pltpu.make_async_copy(src, dst, sems.at[i])
        for i, (src, dst) in enumerate(
            (
                (sends_in, sends),
                (pcol_in, pcol),
                (p_in, p_ref),
                (acol_in, acol),
                (mush_in, mush),
                (a_in, a_ref),
            )
        )
    ]
    for copy in copies:
        copy.start()
    for copy in copies[:3]:
        copy.wait()
    odd = lax.axis_index("gx") % 2
    count = sends.shape[0] // 2
    size = p_ref.shape[1]
    slots = pcol.shape[0]
    for out_ref, start in ((first_ref, (1 - odd) * count), (second_ref, odd * count)):
        tail = out_ref.shape[0] - count * size
        which = lax.broadcasted_iota(jnp.int32, (tail, out_ref.shape[1]), 0)
        cols = jnp.zeros(which.shape, F32)
        for s in range(count):
            row = sends[start + s]
            out_ref[s * size : (s + 1) * size, :] = p_ref[row]
            for j in range(slots):
                cols = jnp.where(which == s * slots + j, pcol[j, row].astype(F32), cols)
        out_ref[count * size :, :] = cols.astype(BF16)
    for copy in copies[3:]:
        copy.wait()


def own_kernel(
    parts, acol, mush, pcol, a_ref, p_ref, ownt_ref, keep_ref, send_ref, own_ref, high_ref, low_ref, prod_ref
):
    bit = lax.axis_index("gy") % 2
    rows, size = p_ref.shape[0], p_ref.shape[1]
    width = NCOL * size
    share = width // parts
    half = lax.broadcasted_iota(jnp.int32, (1, LANES), 1) // size

    def build(n, carry):
        at = pl.ds(pl.multiple_of(n * size, size), size)
        blocks = blocks_of(p_ref, (n, slice(None)), pcol.shape[0])
        cols = [pcol[j, n] for j in range(pcol.shape[0])]
        for c in range(width // LANES):
            own_ref[at, c * LANES : (c + 1) * LANES] = place(blocks, cols, half, c).astype(BF16)
        return carry

    lax.fori_loop(0, rows, build, 0)
    scatter_rows(acol, mush, a_ref, 0, high_ref, low_ref)
    for c in range(width // LANES):
        flipped = own_ref[:, c * LANES : (c + 1) * LANES].T
        for k in range(LANES // share):
            part = c * (LANES // share) + k
            spot = part // 2 + jnp.where(part % 2 == bit, 0, parts // 2)
            at = pl.ds(pl.multiple_of(spot * share, share), share)
            ownt_ref[at, :] = flipped[k * share : (k + 1) * share, :]
    multiply(high_ref, low_ref, own_ref[...], prod_ref)
    finish(ownt_ref, prod_ref[...], keep_ref, send_ref)


def ghost_kernel(
    order, acol, mush, a_ref, in_ref, ownt_ref, keep_ref, send_ref, ext_ref, high_ref, low_ref, prod_ref
):
    odd = lax.axis_index("gx") % 2
    right = odd if order else 1 - odd
    rows, size = a_ref.shape[0], a_ref.shape[1]
    width = NCOL * size
    slots = in_ref.shape[1] // size
    count = ext_ref.shape[0] // size
    half = (lax.broadcasted_iota(jnp.int32, (1, LANES), 1) // size).astype(F32)
    scatter_rows(acol, mush, a_ref, rows + right * count, high_ref, low_ref)
    cols = in_ref[count * size :, :LANES].astype(F32)
    for s in range(count):
        blocks = blocks_of(in_ref, (slice(s * size, (s + 1) * size),), slots)
        mine = [cols[s * slots + j : s * slots + j + 1, :] for j in range(slots)]
        for c in range(width // LANES):
            spot = slice(c * LANES, (c + 1) * LANES)
            ext_ref[s * size : (s + 1) * size, spot] = place(blocks, mine, half, c).astype(BF16)
    multiply(high_ref, low_ref, ext_ref[...], prod_ref)
    finish(ownt_ref, prod_ref[...], keep_ref, send_ref)


def fold_kernel(stage, keep_ref, recv_ref, next_ref, send_ref):
    bit = (lax.axis_index("gy") >> stage) % 2
    for i in range(next_ref.shape[0]):
        mine, other = 2 * i + bit, 2 * i + 1 - bit
        send_ref[i] = (keep_ref[other] + recv_ref[other].astype(F32)).astype(BF16)
        next_ref[i] = keep_ref[mine] + recv_ref[mine].astype(F32)


def write_kernel(orders, *refs):
    count = len(orders)
    keeps, recvs = refs[:count], refs[count : 2 * count]
    out_ref, sum_ref, sems = refs[-3:]
    odd = lax.axis_index("gx") % 2
    width = keeps[0].shape[2]
    copies = []
    for i, order in enumerate(orders):
        third = 1 if order is None else 2 * odd if order else 2 - 2 * odd
        sum_ref[i] = keeps[i][0] + recvs[i][0].astype(F32)
        spot = pl.ds(pl.multiple_of(third * width, width), width)
        copies.append(pltpu.make_async_copy(sum_ref.at[i], out_ref.at[:, spot], sems.at[i]))
        copies[-1].start()
    for copy in copies:
        copy.wait()


def swapped(value, axis, step):
    length = lax.axis_size(axis)
    return lax.ppermute(value, axis, [(i, i ^ step) for i in range(length) if i ^ step < length])


def reduced(keep, send, parts):
    left, share, width = keep.shape
    stage = 0
    while left > 1:
        recv = swapped(send, "gy", 1 << stage)
        stage += 1
        left //= 2
        keep, send = pl.pallas_call(
            functools.partial(fold_kernel, stage),
            out_shape=(
                jax.ShapeDtypeStruct((left, share, width), F32),
                jax.ShapeDtypeStruct((left, share, width), BF16),
            ),
            in_specs=[VMEM, VMEM],
            out_specs=(VMEM, VMEM),
            compiler_params=PARAMS,
            name="fold",
        )(keep, recv)
    return keep, swapped(send, "gy", 1 << stage)


def body(a_blocks, a_cols, mushy, p_blocks, p_cols, send_rows):
    rows, size, inner = p_blocks.shape[1:]
    acol, pcol = a_cols.transpose(2, 0, 1), p_cols[0].T
    mush, sends = mushy[0], send_rows[0]
    count = sends.shape[0] // 2
    width = NCOL * size
    length = lax.axis_size("gx")
    parts = lax.axis_size("gy")
    share = width // parts

    tail = -(-count * pcol.shape[0] // 16) * 16
    packed = jax.ShapeDtypeStruct((count * size + tail, inner), BF16)

    def same(array):
        return jax.ShapeDtypeStruct(array.shape, array.dtype)

    first, second, ablk, pblk, pcol, acol, mush = pl.pallas_call(
        pack_kernel,
        out_shape=(packed, packed, same(a_blocks[0]), same(p_blocks[0]), same(pcol), same(acol), same(mush)),
        in_specs=[HBM] * 6,
        out_specs=(VMEM, VMEM, VMEM, VMEM, SMEM, SMEM, SMEM),
        scratch_shapes=[pltpu.SMEM(sends.shape, sends.dtype), pltpu.SemaphoreType.DMA((6,))],
        compiler_params=PARAMS,
        name="pack",
    )(sends, pcol, acol, mush, a_blocks[0], p_blocks[0])
    even = [(i, i + 1) for i in range(0, length - 1, 2)]
    uneven = [(i, i + 1) for i in range(1, length - 1, 2)]
    first = lax.ppermute(first, "gx", even + [(j, i) for i, j in even])
    second = lax.ppermute(second, "gx", uneven + [(j, i) for i, j in uneven])

    partial = (
        jax.ShapeDtypeStruct((parts // 2, share, width), F32),
        jax.ShapeDtypeStruct((parts // 2, share, width), BF16),
    )
    cost = pl.CostEstimate(flops=600000000, bytes_accessed=3000000, transcendentals=0)
    own_t, keep, send = pl.pallas_call(
        functools.partial(own_kernel, parts),
        out_shape=(jax.ShapeDtypeStruct((width, rows * size), BF16),) + partial,
        in_specs=[SMEM, SMEM, SMEM, VMEM, VMEM],
        out_specs=(VMEM, VMEM, VMEM),
        scratch_shapes=[pltpu.VMEM((rows * size, width), BF16)]
        + [pltpu.VMEM((rows * size, rows * size), BF16)] * 2
        + [pltpu.VMEM((rows * size, width), BF16)],
        compiler_params=PARAMS,
        cost_estimate=cost,
        name="own",
    )(acol, mush, pcol, ablk, pblk)
    chunks = [reduced(keep, send, parts)]
    for order, ghosts in enumerate((first, second)):
        keep, send = pl.pallas_call(
            functools.partial(ghost_kernel, order),
            out_shape=partial,
            in_specs=[SMEM, SMEM, VMEM, VMEM, VMEM],
            out_specs=(VMEM, VMEM),
            scratch_shapes=[pltpu.VMEM((count * size, width), BF16)]
            + [pltpu.VMEM((rows * size, count * size), BF16)] * 2
            + [pltpu.VMEM((rows * size, width), BF16)],
            compiler_params=PARAMS,
            cost_estimate=cost,
            name="ghost",
        )(acol, mush, ablk, ghosts, own_t)
        chunks.append(reduced(keep, send, parts))

    result = None
    for orders, some in (((None, 0), chunks[:2]), ((1,), chunks[2:])):
        values = [keep for keep, recv in some] + [recv for keep, recv in some]
        given = [] if result is None else [result]
        result = pl.pallas_call(
            functools.partial(write_kernel, orders),
            out_shape=jax.ShapeDtypeStruct((share, 3 * width), F32),
            in_specs=[VMEM] * len(values) + [HBM] * len(given),
            out_specs=HBM,
            input_output_aliases={len(values): 0} if given else {},
            scratch_shapes=[
                pltpu.VMEM((len(some), share, width), F32),
                pltpu.SemaphoreType.DMA((len(some),)),
            ],
            compiler_params=PARAMS,
            name="write",
        )(*values, *given)
    return result[None]


def solution(mesh):
    placed = (
        P("gx", "gy", None, None),
        P("gx", "gy", None),
        P("gx", "gy"),
        P("gx", "gy", None, None),
        P("gx", "gy", None),
        P("gx", "gy"),
    )
    return jax.shard_map(
        body, mesh=mesh, in_specs=placed, out_specs=P("gx", "gy", None), check_vma=False
    )
```

```python
import functools

import jax
import jax.numpy as jnp
from jax import lax
from jax.experimental import pallas as pl
from jax.experimental.pallas import tpu as pltpu
from jax.sharding import PartitionSpec as P

KA = 7
KS = 3
NCOL = 8
LANES = 128

F32 = jnp.float32
BF16 = jnp.bfloat16
SMEM = pl.BlockSpec(memory_space=pltpu.SMEM)
VMEM = pl.BlockSpec(memory_space=pltpu.VMEM)
HBM = pl.BlockSpec(memory_space=pltpu.HBM)
PARAMS = pltpu.CompilerParams(vmem_limit_bytes=24 * 1024 * 1024)


def halves(tile):
    low = lax.broadcasted_iota(jnp.int32, tile.shape, 1) < LANES // 2
    swapped = pltpu.roll(tile, LANES // 2, 1)
    return jnp.where(low, tile, swapped), jnp.where(low, swapped, tile)


def blocks_of(ref, at, slots):
    blocks = []
    for q in range(slots // 2):
        blocks += halves(ref[at + (slice(q * LANES, (q + 1) * LANES),)].astype(F32))
    if slots % 2:
        last = ref[at + (slice((slots - 1) * LANES // 2, slots * LANES // 2),)].astype(F32)
        blocks.append(jnp.concatenate([last, last], axis=1))
    return blocks


def place(blocks, cols, slots, tile):
    total = None
    for block, col in zip(blocks, cols):
        term = block * jnp.where(slots == col - 2 * tile, 1.0, 0.0).astype(F32)
        total = term if total is None else total + term
    return total


def multiply(acol, mush, a_ref, base, ext_ref, prod_ref):
    rows, size = a_ref.shape[0], a_ref.shape[1]
    ext_ref[ext_ref.shape[0] - 1] = jnp.zeros(ext_ref.shape[1:], BF16)
    none = ext_ref.shape[0] - 1
    for n in range(rows):
        limit = jnp.where(mush[n] > 0, KA, KS)
        picks = []
        for k in range(KA):
            spot = acol[k, 0, n] - base
            good = (k < limit) & (spot >= 0) & (spot < none)
            picks.append(jnp.where(good, spot, none))
        picked = jnp.concatenate([ext_ref[spot] for spot in picks], axis=0)
        value = jnp.dot(a_ref[n], picked, preferred_element_type=F32)
        prod_ref[n * size : (n + 1) * size, :] = value.astype(BF16)


def finish(ownt_ref, prod, keep_ref, send_ref):
    rows = ownt_ref.shape[0] // 2
    sent = jnp.dot(ownt_ref[rows:, :], prod, preferred_element_type=F32)
    send_ref[...] = sent.astype(BF16).reshape(send_ref.shape)
    kept = jnp.dot(ownt_ref[:rows, :], prod, preferred_element_type=F32)
    keep_ref[...] = kept.reshape(keep_ref.shape)


def pack_kernel(sends_in, pcol_in, p_in, first_ref, second_ref, sends, pcol, tail_ref, sems):
    copies = [
        pltpu.make_async_copy(sends_in, sends, sems.at[0]),
        pltpu.make_async_copy(pcol_in, pcol, sems.at[1]),
    ]
    for copy in copies:
        copy.start()
    for copy in copies:
        copy.wait()
    odd = lax.axis_index("gx") % 2
    count = sends.shape[0] // 2
    size = p_in.shape[1]
    slots = pcol.shape[0]
    sides = ((first_ref, (1 - odd) * count), (second_ref, odd * count))
    copies = []
    for i, (out_ref, start) in enumerate(sides):
        for s in range(count):
            sem = sems.at[i * count + s]
            into = out_ref.at[s * size : (s + 1) * size]
            copies.append(pltpu.make_async_copy(p_in.at[sends[start + s]], into, sem))
            copies[-1].start()
    which = lax.broadcasted_iota(jnp.int32, tail_ref.shape[1:], 0)
    for i, (out_ref, start) in enumerate(sides):
        cols = jnp.zeros(which.shape, F32)
        for s in range(count):
            row = sends[start + s]
            for j in range(slots):
                cols = jnp.where(which == s * slots + j, pcol[j, row].astype(F32), cols)
        tail_ref[i] = cols.astype(BF16)
        into = out_ref.at[count * size :]
        copies.append(pltpu.make_async_copy(tail_ref.at[i], into, sems.at[2 * count + i]))
        copies[-1].start()
    for copy in copies:
        copy.wait()


def own_kernel(parts, acol, mush, pcol, a_ref, p_ref, after, ownt_ref, keep_ref, send_ref, own_ref, prod_ref):
    bit = lax.axis_index("gy") % 2
    rows, size = p_ref.shape[0], p_ref.shape[1]
    width = NCOL * size
    share = width // parts
    half = lax.broadcasted_iota(jnp.int32, (1, LANES), 1) // size

    def build(n, carry):
        blocks = blocks_of(p_ref, (n, slice(None)), pcol.shape[0])
        cols = [pcol[j, n] for j in range(pcol.shape[0])]
        for c in range(width // LANES):
            own_ref[n, :, c * LANES : (c + 1) * LANES] = place(blocks, cols, half, c).astype(BF16)
        return carry

    lax.fori_loop(0, rows, build, 0)
    for c in range(width // LANES):
        column = own_ref[:rows, :, c * LANES : (c + 1) * LANES]
        flipped = column.reshape(rows * size, LANES).T
        for k in range(LANES // share):
            part = c * (LANES // share) + k
            spot = part // 2 + jnp.where(part % 2 == bit, 0, parts // 2)
            at = pl.ds(pl.multiple_of(spot * share, share), share)
            ownt_ref[at, :] = flipped[k * share : (k + 1) * share, :]
    multiply(acol, mush, a_ref, 0, own_ref, prod_ref)
    finish(ownt_ref, prod_ref[...], keep_ref, send_ref)


def ghost_kernel(order, acol, mush, a_ref, in_ref, ownt_ref, keep_ref, send_ref, ext_ref, prod_ref):
    odd = lax.axis_index("gx") % 2
    right = odd if order else 1 - odd
    rows, size = a_ref.shape[0], a_ref.shape[1]
    width = NCOL * size
    slots = in_ref.shape[1] // size
    count = ext_ref.shape[0] - 1
    half = (lax.broadcasted_iota(jnp.int32, (1, LANES), 1) // size).astype(F32)
    cols = in_ref[count * size :, :LANES].astype(F32)
    for s in range(count):
        blocks = blocks_of(in_ref, (slice(s * size, (s + 1) * size),), slots)
        mine = [cols[s * slots + j : s * slots + j + 1, :] for j in range(slots)]
        for c in range(width // LANES):
            spot = slice(c * LANES, (c + 1) * LANES)
            ext_ref[s, :, spot] = place(blocks, mine, half, c).astype(BF16)
    multiply(acol, mush, a_ref, rows + right * count, ext_ref, prod_ref)
    finish(ownt_ref, prod_ref[...], keep_ref, send_ref)


def fold_kernel(stage, keep_ref, recv_ref, next_ref, send_ref):
    bit = (lax.axis_index("gy") >> stage) % 2
    for i in range(next_ref.shape[0]):
        mine, other = 2 * i + bit, 2 * i + 1 - bit
        send_ref[i] = (keep_ref[other] + recv_ref[other].astype(F32)).astype(BF16)
        next_ref[i] = keep_ref[mine] + recv_ref[mine].astype(F32)


def write_kernel(orders, *refs):
    count = len(orders)
    keeps, recvs = refs[:count], refs[count : 2 * count]
    out_ref, sum_ref, sems = refs[-3:]
    odd = lax.axis_index("gx") % 2
    width = keeps[0].shape[2]
    copies = []
    for i, order in enumerate(orders):
        third = 1 if order is None else 2 * odd if order else 2 - 2 * odd
        sum_ref[i] = keeps[i][0] + recvs[i][0].astype(F32)
        spot = pl.ds(pl.multiple_of(third * width, width), width)
        copies.append(pltpu.make_async_copy(sum_ref.at[i], out_ref.at[:, spot], sems.at[i]))
        copies[-1].start()
    for copy in copies:
        copy.wait()


def swapped(value, axis, step):
    length = lax.axis_size(axis)
    return lax.ppermute(value, axis, [(i, i ^ step) for i in range(length) if i ^ step < length])


def folded(keep, send, parts):
    left, share, width = keep.shape
    stage = 0
    while left > 1:
        recv = swapped(send, "gy", 1 << stage)
        stage += 1
        left //= 2
        keep, send = pl.pallas_call(
            functools.partial(fold_kernel, stage),
            out_shape=(
                jax.ShapeDtypeStruct((left, share, width), F32),
                jax.ShapeDtypeStruct((left, share, width), BF16),
            ),
            in_specs=[VMEM, VMEM],
            out_specs=(VMEM, VMEM),
            compiler_params=PARAMS,
            name="fold",
        )(keep, recv)
    return keep, send, 1 << stage


def body(a_blocks, a_cols, mushy, p_blocks, p_cols, send_rows):
    rows, size, inner = p_blocks.shape[1:]
    acol, pcol = a_cols.transpose(2, 0, 1), p_cols[0].T
    mush, sends = mushy[0], send_rows[0]
    ablk, pblk = a_blocks[0], p_blocks[0]
    count = sends.shape[0] // 2
    width = NCOL * size
    length = lax.axis_size("gx")
    parts = lax.axis_size("gy")
    share = width // parts

    tail = -(-count * pcol.shape[0] // 16) * 16
    packed = jax.ShapeDtypeStruct((count * size + tail, inner), BF16)
    after_pack = jax.ShapeDtypeStruct(sends.shape, sends.dtype)

    first, second, token = pl.pallas_call(
        pack_kernel,
        out_shape=(packed, packed, after_pack),
        in_specs=[HBM] * 3,
        out_specs=(HBM, HBM, SMEM),
        scratch_shapes=[
            pltpu.SMEM(pcol.shape, pcol.dtype),
            pltpu.VMEM((2, tail, inner), BF16),
            pltpu.SemaphoreType.DMA((2 * count + 2,)),
        ],
        compiler_params=pltpu.CompilerParams(vmem_limit_bytes=56 * 1024 * 1024),
        cost_estimate=pl.CostEstimate(flops=10000000000, bytes_accessed=3000000, transcendentals=0),
        name="pack",
    )(sends, pcol, pblk)
    even = [(i, i + 1) for i in range(0, length - 1, 2)]
    uneven = [(i, i + 1) for i in range(1, length - 1, 2)]
    first = lax.ppermute(first, "gx", even + [(j, i) for i, j in even])
    second = lax.ppermute(second, "gx", uneven + [(j, i) for i, j in uneven])

    partial = (
        jax.ShapeDtypeStruct((parts // 2, share, width), F32),
        jax.ShapeDtypeStruct((parts // 2, share, width), BF16),
    )
    cost = pl.CostEstimate(flops=600000000, bytes_accessed=3000000, transcendentals=0)
    own_t, keep, send = pl.pallas_call(
        functools.partial(own_kernel, parts),
        out_shape=(jax.ShapeDtypeStruct((width, rows * size), BF16),) + partial,
        in_specs=[SMEM, SMEM, SMEM, VMEM, VMEM, HBM],
        out_specs=(VMEM, VMEM, VMEM),
        scratch_shapes=[
            pltpu.VMEM((rows + 1, size, width), BF16),
            pltpu.VMEM((rows * size, width), BF16),
        ],
        compiler_params=PARAMS,
        cost_estimate=cost,
        name="own",
    )(acol, mush, pcol, ablk, pblk, token)
    chunks = [folded(keep, send, parts)]
    for order, ghosts in enumerate((first, second)):
        keep, send = pl.pallas_call(
            functools.partial(ghost_kernel, order),
            out_shape=partial,
            in_specs=[SMEM, SMEM, VMEM, VMEM, VMEM],
            out_specs=(VMEM, VMEM),
            scratch_shapes=[
                pltpu.VMEM((count + 1, size, width), BF16),
                pltpu.VMEM((rows * size, width), BF16),
            ],
            compiler_params=PARAMS,
            cost_estimate=cost,
            name="ghost",
        )(acol, mush, ablk, ghosts, own_t)
        chunks.append(folded(keep, send, parts))
    chunks = [(keep, swapped(send, "gy", step)) for keep, send, step in chunks]

    result = None
    for orders, some in (((None, 0), chunks[:2]), ((1,), chunks[2:])):
        values = [keep for keep, recv in some] + [recv for keep, recv in some]
        given = [] if result is None else [result]
        result = pl.pallas_call(
            functools.partial(write_kernel, orders),
            out_shape=jax.ShapeDtypeStruct((share, 3 * width), F32),
            in_specs=[VMEM] * len(values) + [HBM] * len(given),
            out_specs=HBM,
            input_output_aliases={len(values): 0} if given else {},
            scratch_shapes=[
                pltpu.VMEM((len(some), share, width), F32),
                pltpu.SemaphoreType.DMA((len(some),)),
            ],
            compiler_params=PARAMS,
            name="write",
        )(*values, *given)
    return result[None]


def solution(mesh):
    placed = (
        P("gx", "gy", None, None),
        P("gx", "gy", None),
        P("gx", "gy"),
        P("gx", "gy", None, None),
        P("gx", "gy", None),
        P("gx", "gy"),
    )
    return jax.shard_map(
        body, mesh=mesh, in_specs=placed, out_specs=P("gx", "gy", None), check_vma=False
    )
```

```python
import functools

import jax
import jax.numpy as jnp
from jax import lax
from jax.experimental import pallas as pl
from jax.experimental.pallas import tpu as pltpu
from jax.sharding import PartitionSpec as P

KA = 7
KS = 3
NCOL = 8
LANES = 128

F32 = jnp.float32
BF16 = jnp.bfloat16
SMEM = pl.BlockSpec(memory_space=pltpu.SMEM)
VMEM = pl.BlockSpec(memory_space=pltpu.VMEM)
HBM = pl.BlockSpec(memory_space=pltpu.HBM)
LONG = pl.CostEstimate(flops=10000000000, bytes_accessed=3000000, transcendentals=0)
PARAMS = pltpu.CompilerParams(vmem_limit_bytes=24 * 1024 * 1024)


def dense_rows(rows, masks_of, out_ref, width):
    size = rows[0].shape[0]
    row = lax.broadcasted_iota(jnp.int32, (size, LANES), 0)
    lane = lax.broadcasted_iota(jnp.int32, (size, LANES), 1)
    unit = jnp.where(row == lane % size, 1.0, 0.0).astype(BF16)
    for n, value in enumerate(rows):
        for c in range(width // LANES):
            moves = jnp.concatenate([unit * mask for mask in masks_of(n, c)], axis=0)
            spot = slice(c * LANES, (c + 1) * LANES)
            out_ref[n, :, spot] = jnp.dot(value, moves, preferred_element_type=F32).astype(BF16)


def multiply(acol, mush, a_ref, base, ext_ref, prod_ref):
    rows, size = a_ref.shape[0], a_ref.shape[1]
    ext_ref[ext_ref.shape[0] - 1] = jnp.zeros(ext_ref.shape[1:], BF16)
    none = ext_ref.shape[0] - 1
    for n in range(rows):
        limit = jnp.where(mush[n] > 0, KA, KS)
        picks = []
        for k in range(KA):
            spot = acol[k, 0, n] - base
            good = (k < limit) & (spot >= 0) & (spot < none)
            picks.append(jnp.where(good, spot, none))
        picked = jnp.concatenate([ext_ref[spot] for spot in picks], axis=0)
        value = jnp.dot(a_ref[n], picked, preferred_element_type=F32)
        prod_ref[n * size : (n + 1) * size, :] = value.astype(BF16)


def finish(ownt_ref, prod, keep_ref, send_ref):
    rows = ownt_ref.shape[0] // 2
    sent = jnp.dot(ownt_ref[rows:, :], prod, preferred_element_type=F32)
    send_ref[...] = sent.astype(BF16).reshape(send_ref.shape)
    kept = jnp.dot(ownt_ref[:rows, :], prod, preferred_element_type=F32)
    keep_ref[...] = kept.reshape(keep_ref.shape)


def pack_kernel(
    sends_in, pcol_in, acol_in, p_in, first_ref, second_ref, acol, sends, pcol, p_ref, tail_ref, sems
):
    copies = [
        pltpu.make_async_copy(src, dst, sems.at[i])
        for i, (src, dst) in enumerate(
            ((sends_in, sends), (pcol_in, pcol), (p_in, p_ref), (acol_in, acol))
        )
    ]
    for copy in copies:
        copy.start()
    for copy in copies:
        copy.wait()
    odd = lax.axis_index("gx") % 2
    count = sends.shape[0] // 2
    size = p_ref.shape[1]
    slots = pcol.shape[0]
    sides = ((first_ref, (1 - odd) * count), (second_ref, odd * count))
    copies = []
    for i, (out_ref, start) in enumerate(sides):
        for s in range(count):
            into = out_ref.at[s * size : (s + 1) * size]
            copies.append(pltpu.make_async_copy(p_ref.at[sends[start + s]], into, sems.at[len(copies)]))
            copies[-1].start()
    which = lax.broadcasted_iota(jnp.int32, tail_ref.shape[1:], 0)
    for i, (out_ref, start) in enumerate(sides):
        cols = jnp.zeros(which.shape, F32)
        for s in range(count):
            row = sends[start + s]
            for j in range(slots):
                cols = jnp.where(which == s * slots + j, pcol[j, row].astype(F32), cols)
        tail_ref[i] = cols.astype(BF16)
        into = out_ref.at[count * size :]
        copies.append(pltpu.make_async_copy(tail_ref.at[i], into, sems.at[len(copies)]))
        copies[-1].start()
    for copy in copies:
        copy.wait()


def own_kernel(parts, acol, mush, pcol, a_ref, p_ref, ownt_ref, keep_ref, send_ref, own_ref, prod_ref):
    bit = lax.axis_index("gy") % 2
    rows, size = p_ref.shape[0], p_ref.shape[1]
    width = NCOL * size
    share = width // parts
    half = lax.broadcasted_iota(jnp.int32, (1, LANES), 1) // size

    def masks(n, c):
        return [
            jnp.where(half == pcol[j, n] - 2 * c, 1.0, 0.0).astype(BF16) for j in range(pcol.shape[0])
        ]

    dense_rows([p_ref[n] for n in range(rows)], masks, own_ref, width)
    for c in range(width // LANES):
        column = own_ref[:rows, :, c * LANES : (c + 1) * LANES]
        flipped = column.reshape(rows * size, LANES).T
        for k in range(LANES // share):
            part = c * (LANES // share) + k
            spot = part // 2 + jnp.where(part % 2 == bit, 0, parts // 2)
            at = pl.ds(pl.multiple_of(spot * share, share), share)
            ownt_ref[at, :] = flipped[k * share : (k + 1) * share, :]
    multiply(acol, mush, a_ref, 0, own_ref, prod_ref)
    finish(ownt_ref, prod_ref[...], keep_ref, send_ref)


def ghost_kernel(order, acol, mush, a_ref, in_ref, ownt_ref, keep_ref, send_ref, ext_ref, prod_ref):
    odd = lax.axis_index("gx") % 2
    right = odd if order else 1 - odd
    rows, size = a_ref.shape[0], a_ref.shape[1]
    width = NCOL * size
    slots = in_ref.shape[1] // size
    count = ext_ref.shape[0] - 1
    half = (lax.broadcasted_iota(jnp.int32, (1, LANES), 1) // size).astype(F32)
    cols = in_ref[count * size :, :LANES].astype(F32)

    def masks(n, c):
        mine = [cols[n * slots + j : n * slots + j + 1, :] for j in range(slots)]
        return [jnp.where(half == col - 2 * c, 1.0, 0.0).astype(BF16) for col in mine]

    dense_rows([in_ref[n * size : (n + 1) * size, :] for n in range(count)], masks, ext_ref, width)
    multiply(acol, mush, a_ref, rows + right * count, ext_ref, prod_ref)
    finish(ownt_ref, prod_ref[...], keep_ref, send_ref)


def fold_kernel(stage, keep_ref, recv_ref, *refs):
    next_ref, send_ref = refs[-2:]
    bit = (lax.axis_index("gy") >> stage) % 2
    for i in range(next_ref.shape[0]):
        mine, other = 2 * i + bit, 2 * i + 1 - bit
        send_ref[i] = (keep_ref[other] + recv_ref[other].astype(F32)).astype(BF16)
        next_ref[i] = keep_ref[mine] + recv_ref[mine].astype(F32)


def write_kernel(order, keep_ref, recv_ref, *refs):
    out_ref, token_ref, sum_ref, sem = refs[-4:]
    odd = lax.axis_index("gx") % 2
    third = 1 if order is None else 2 * odd if order else 2 - 2 * odd
    width = sum_ref.shape[1]
    sum_ref[...] = keep_ref[0] + recv_ref[0].astype(F32)
    spot = pl.ds(pl.multiple_of(third * width, width), width)
    copy = pltpu.make_async_copy(sum_ref, out_ref.at[:, spot], sem)
    copy.start()
    token_ref[...] = jnp.zeros(token_ref.shape, F32)
    copy.wait()


def swapped(value, axis, step):
    length = lax.axis_size(axis)
    return lax.ppermute(value, axis, [(i, i ^ step) for i in range(length) if i ^ step < length])


def folded(keep, send, parts, after=()):
    left, share, width = keep.shape
    stage = 0
    while left > 1:
        recv = swapped(send, "gy", 1 << stage)
        stage += 1
        left //= 2
        keep, send = pl.pallas_call(
            functools.partial(fold_kernel, stage),
            out_shape=(
                jax.ShapeDtypeStruct((left, share, width), F32),
                jax.ShapeDtypeStruct((left, share, width), BF16),
            ),
            in_specs=[VMEM] * (2 + len(after)),
            out_specs=(VMEM, VMEM),
            compiler_params=PARAMS,
            name="fold",
        )(keep, recv, *after)
        after = ()
    return keep, swapped(send, "gy", 1 << stage)


def written(order, keep, recv, result):
    share, width = keep.shape[1:]
    given = [] if result is None else [result]
    return pl.pallas_call(
        functools.partial(write_kernel, order),
        out_shape=(
            jax.ShapeDtypeStruct((share, 3 * width), F32),
            jax.ShapeDtypeStruct((8, LANES), F32),
        ),
        in_specs=[VMEM, VMEM] + [HBM] * len(given),
        out_specs=(HBM, VMEM),
        input_output_aliases={2: 0} if given else {},
        scratch_shapes=[pltpu.VMEM((share, width), F32), pltpu.SemaphoreType.DMA],
        compiler_params=PARAMS,
        cost_estimate=LONG,
        name="write",
    )(keep, recv, *given)


def body(a_blocks, a_cols, mushy, p_blocks, p_cols, send_rows):
    rows, size, inner = p_blocks.shape[1:]
    acol, pcol = a_cols.transpose(2, 0, 1), p_cols[0].T
    mush, sends = mushy[0], send_rows[0]
    ablk, pblk = a_blocks[0], p_blocks[0]
    count = sends.shape[0] // 2
    width = NCOL * size
    length = lax.axis_size("gx")
    parts = lax.axis_size("gy")
    share = width // parts

    tail = -(-count * pcol.shape[0] // 16) * 16
    packed = jax.ShapeDtypeStruct((count * size + tail, inner), BF16)

    first, second, acol = pl.pallas_call(
        pack_kernel,
        out_shape=(packed, packed, jax.ShapeDtypeStruct(acol.shape, acol.dtype)),
        in_specs=[HBM] * 4,
        out_specs=(HBM, HBM, SMEM),
        scratch_shapes=[
            pltpu.SMEM(sends.shape, sends.dtype),
            pltpu.SMEM(pcol.shape, pcol.dtype),
            pltpu.VMEM(pblk.shape, BF16),
            pltpu.VMEM((2, tail, inner), BF16),
            pltpu.SemaphoreType.DMA((2 * count + 2,)),
        ],
        compiler_params=pltpu.CompilerParams(vmem_limit_bytes=56 * 1024 * 1024),
        cost_estimate=pl.CostEstimate(flops=10000000000, bytes_accessed=3000000, transcendentals=0),
        name="pack",
    )(sends, pcol, acol, pblk)
    even = [(i, i + 1) for i in range(0, length - 1, 2)]
    uneven = [(i, i + 1) for i in range(1, length - 1, 2)]
    first = lax.ppermute(first, "gx", even + [(j, i) for i, j in even])
    second = lax.ppermute(second, "gx", uneven + [(j, i) for i, j in uneven])

    partial = (
        jax.ShapeDtypeStruct((parts // 2, share, width), F32),
        jax.ShapeDtypeStruct((parts // 2, share, width), BF16),
    )
    own_t, keep, send = pl.pallas_call(
        functools.partial(own_kernel, parts),
        out_shape=(jax.ShapeDtypeStruct((width, rows * size), BF16),) + partial,
        in_specs=[SMEM, SMEM, SMEM, VMEM, VMEM],
        out_specs=(VMEM, VMEM, VMEM),
        scratch_shapes=[
            pltpu.VMEM((rows + 1, size, width), BF16),
            pltpu.VMEM((rows * size, width), BF16),
        ],
        compiler_params=PARAMS,
        cost_estimate=LONG,
        name="own",
    )(acol, mush, pcol, ablk, pblk)
    keep, recv = folded(keep, send, parts)
    pieces = []
    for order, ghosts in enumerate((first, second)):
        pieces.append(
            pl.pallas_call(
                functools.partial(ghost_kernel, order),
                out_shape=partial,
                in_specs=[SMEM, SMEM, VMEM, VMEM, VMEM],
                out_specs=(VMEM, VMEM),
                scratch_shapes=[
                    pltpu.VMEM((count + 1, size, width), BF16),
                    pltpu.VMEM((rows * size, width), BF16),
                ],
                compiler_params=PARAMS,
                cost_estimate=LONG,
                name="ghost",
            )(acol, mush, ablk, ghosts, own_t)
        )
    result, token = written(None, keep, recv, None)
    sides = [folded(*pieces[0], parts), folded(*pieces[1], parts, (token,))]
    for order, (keep, recv) in enumerate(sides):
        result, token = written(order, keep, recv, result)
    return result[None]


def solution(mesh):
    placed = (
        P("gx", "gy", None, None),
        P("gx", "gy", None),
        P("gx", "gy"),
        P("gx", "gy", None, None),
        P("gx", "gy", None),
        P("gx", "gy"),
    )
    return jax.shard_map(
        body, mesh=mesh, in_specs=placed, out_specs=P("gx", "gy", None), check_vma=False
    )
```

```python
import functools

import jax
import jax.numpy as jnp
from jax import lax
from jax.experimental import pallas as pl
from jax.experimental.pallas import tpu as pltpu
from jax.sharding import PartitionSpec as P

KA = 7
KS = 3
NCOL = 8
LANES = 128
WIDE = 256

F32 = jnp.float32
BF16 = jnp.bfloat16
SMEM = pl.BlockSpec(memory_space=pltpu.SMEM)
VMEM = pl.BlockSpec(memory_space=pltpu.VMEM)
HBM = pl.BlockSpec(memory_space=pltpu.HBM)
LONG = pl.CostEstimate(flops=10000000000, bytes_accessed=1000000, transcendentals=0)
SHORT = pl.CostEstimate(flops=1000000000, bytes_accessed=1000000, transcendentals=0)
PARAMS = pltpu.CompilerParams(vmem_limit_bytes=24 * 1024 * 1024)


def spread(value, masks_of, width):
    size = value.shape[0]
    row = lax.broadcasted_iota(jnp.int32, (size, WIDE), 0)
    lane = lax.broadcasted_iota(jnp.int32, (size, WIDE), 1)
    unit = jnp.where(row == lane % size, 1.0, 0.0).astype(BF16)
    tiles = []
    for c in range(width // WIDE):
        moves = jnp.concatenate([unit * mask for mask in masks_of(c * WIDE // size)], axis=0)
        tiles.append(jnp.dot(value, moves, preferred_element_type=F32))
    return tiles


def masks_at(cols, size, dtype):
    slots = (lax.broadcasted_iota(jnp.int32, (1, WIDE), 1) // size).astype(dtype)
    return lambda first: [
        jnp.where(slots == col - first, 1.0, 0.0).astype(BF16) for col in cols
    ]


def multiply(acol, mush, a_ref, base, ext_ref, prod_ref):
    rows, size = a_ref.shape[0], a_ref.shape[1]
    ext_ref[ext_ref.shape[0] - 1] = jnp.zeros(ext_ref.shape[1:], BF16)
    none = ext_ref.shape[0] - 1
    for n in range(rows):
        limit = jnp.where(mush[n] > 0, KA, KS)
        picks = []
        for k in range(KA):
            spot = acol[k, 0, n] - base
            good = (k < limit) & (spot >= 0) & (spot < none)
            picks.append(jnp.where(good, spot, none))
        picked = jnp.concatenate([ext_ref[spot] for spot in picks], axis=0)
        value = jnp.dot(a_ref[n], picked, preferred_element_type=F32)
        prod_ref[n * size : (n + 1) * size, :] = value.astype(BF16)


def finish(ownt_ref, prod, keep_ref, send_ref):
    rows = ownt_ref.shape[0] // 2
    sent = jnp.dot(ownt_ref[rows:, :], prod, preferred_element_type=F32)
    send_ref[...] = sent.astype(BF16).reshape(send_ref.shape)
    kept = jnp.dot(ownt_ref[:rows, :], prod, preferred_element_type=F32)
    keep_ref[...] = kept.reshape(keep_ref.shape)


def pack_kernel(sends_in, pcol_in, p_in, first_ref, second_ref, sends, pcol, p_ref, packed_ref, sems):
    copies = [
        pltpu.make_async_copy(src, dst, sems.at[i])
        for i, (src, dst) in enumerate(((sends_in, sends), (pcol_in, pcol), (p_in, p_ref)))
    ]
    for copy in copies:
        copy.start()
    for copy in copies[:2]:
        copy.wait()
    odd = lax.axis_index("gx") % 2
    count = sends.shape[0] // 2
    size = p_ref.shape[1]
    slots = pcol.shape[0]
    starts = ((1 - odd) * count, odd * count)
    tail = packed_ref.shape[1] - count * size
    which = lax.broadcasted_iota(jnp.int32, (tail, packed_ref.shape[2]), 0)
    for i, start in enumerate(starts):
        cols = jnp.zeros(which.shape, F32)
        for s in range(count):
            row = sends[start + s]
            for j in range(slots):
                cols = jnp.where(which == s * slots + j, pcol[j, row].astype(F32), cols)
        packed_ref[i, count * size :, :] = cols.astype(BF16)
    copies[2].wait()
    copies = []
    for i, (out_ref, start) in enumerate(zip((first_ref, second_ref), starts)):
        for s in range(count):
            packed_ref[i, s * size : (s + 1) * size, :] = p_ref[sends[start + s]]
        copies.append(pltpu.make_async_copy(packed_ref.at[i], out_ref, sems.at[i]))
        copies[-1].start()
    for copy in copies:
        copy.wait()


def own_kernel(parts, acol, mush, pcol, a_ref, p_ref, passed, ownt_ref, keep_ref, send_ref, *refs):
    own_ref, prod_ref = refs[-2:]
    bit = lax.axis_index("gy") % 2
    rows, size = p_ref.shape[0], p_ref.shape[1]
    width = NCOL * size
    share = width // parts
    for n in range(rows):
        masks = masks_at([pcol[j, n] for j in range(pcol.shape[0])], size, jnp.int32)
        for c, tile in enumerate(spread(p_ref[n], masks, width)):
            own_ref[n, :, c * WIDE : (c + 1) * WIDE] = tile.astype(BF16)
    for c in range(width // LANES):
        column = own_ref[:rows, :, c * LANES : (c + 1) * LANES]
        flipped = column.reshape(rows * size, LANES).T
        for k in range(LANES // share):
            part = c * (LANES // share) + k
            spot = part // 2 + jnp.where(part % 2 == bit, 0, parts // 2)
            at = pl.ds(pl.multiple_of(spot * share, share), share)
            ownt_ref[at, :] = flipped[k * share : (k + 1) * share, :]
    multiply(acol, mush, a_ref, 0, own_ref, prod_ref)
    finish(ownt_ref, prod_ref[...], keep_ref, send_ref)


def scatter_kernel(acol, mush, a_ref, high_ref, low_ref):
    odd = lax.axis_index("gx") % 2
    rows, size = a_ref.shape[0], a_ref.shape[1]
    width = high_ref.shape[2]
    for n in range(rows):
        limit = jnp.where(mush[n] > 0, KA, KS)
        at = slice(n * size, (n + 1) * size)
        for order in range(2):
            right = odd if order else 1 - odd
            base = rows + right * (width // size)
            cols = [jnp.where(k < limit, acol[k, 0, n] - base, -1) for k in range(KA)]
            masks = masks_at(cols, size, jnp.int32)
            for c, tile in enumerate(spread(a_ref[n], masks, width)):
                spot = slice(c * WIDE, (c + 1) * WIDE)
                high = tile.astype(BF16)
                high_ref[order, at, spot] = high
                low_ref[order, at, spot] = (tile - high.astype(F32)).astype(BF16)


def ghost_kernel(order, high_ref, low_ref, in_ref, ownt_ref, *refs):
    keep_ref, send_ref, ext_ref, prod_ref = refs[-4:]
    width = ownt_ref.shape[0]
    size = width // NCOL
    slots = in_ref.shape[1] // size
    count = ext_ref.shape[0] // size
    cols = in_ref[count * size :, :].astype(F32)
    for n in range(count):
        at = slice(n * size, (n + 1) * size)
        masks = masks_at([cols[n * slots + j : n * slots + j + 1, :] for j in range(slots)], size, F32)
        for c, tile in enumerate(spread(in_ref[at, :], masks, width)):
            ext_ref[at, c * WIDE : (c + 1) * WIDE] = tile.astype(BF16)
    ext = ext_ref[...]
    step = prod_ref.shape[0] // 2
    for m in range(2):
        at = slice(m * step, (m + 1) * step)
        value = jnp.dot(high_ref[order, at, :], ext, preferred_element_type=F32)
        value += jnp.dot(low_ref[order, at, :], ext, preferred_element_type=F32)
        prod_ref[at, :] = value.astype(BF16)
    finish(ownt_ref, prod_ref[...], keep_ref, send_ref)


def fold_kernel(stage, keep_ref, recv_ref, *refs):
    next_ref, send_ref = refs[-2:]
    bit = (lax.axis_index("gy") >> stage) % 2
    for i in range(next_ref.shape[0]):
        mine, other = 2 * i + bit, 2 * i + 1 - bit
        send_ref[i] = (keep_ref[other] + recv_ref[other].astype(F32)).astype(BF16)
        next_ref[i] = keep_ref[mine] + recv_ref[mine].astype(F32)


def write_kernel(order, keep_ref, recv_ref, *refs):
    sum_ref, sem = refs[-2:]
    out_ref = refs[0 if order is None else 1]
    odd = lax.axis_index("gx") % 2
    third = 1 if order is None else 2 * odd if order else 2 - 2 * odd
    width = sum_ref.shape[1]
    sum_ref[...] = keep_ref[0] + recv_ref[0].astype(F32)
    spot = pl.ds(pl.multiple_of(third * width, width), width)
    copy = pltpu.make_async_copy(sum_ref, out_ref.at[:, spot], sem)
    copy.start()
    if order is None:
        refs[1][...] = jnp.zeros(refs[1].shape, F32)
    copy.wait()


def swapped(value, axis, step):
    length = lax.axis_size(axis)
    return lax.ppermute(value, axis, [(i, i ^ step) for i in range(length) if i ^ step < length])


def folded(keep, send, parts, after=()):
    left, share, width = keep.shape
    stage = 0
    while left > 1:
        recv = swapped(send, "gy", 1 << stage)
        stage += 1
        left //= 2
        keep, send = pl.pallas_call(
            functools.partial(fold_kernel, stage),
            out_shape=(
                jax.ShapeDtypeStruct((left, share, width), F32),
                jax.ShapeDtypeStruct((left, share, width), BF16),
            ),
            in_specs=[VMEM] * (2 + len(after)),
            out_specs=(VMEM, VMEM),
            compiler_params=PARAMS,
            name="fold",
        )(keep, recv, *after)
        after = ()
    return keep, swapped(send, "gy", 1 << stage), keep


def written(order, keep, recv, result):
    share, width = keep.shape[1:]
    start = order is None
    whole = jax.ShapeDtypeStruct((share, 3 * width), F32)
    token = jax.ShapeDtypeStruct((8, LANES), F32)
    return pl.pallas_call(
        functools.partial(write_kernel, order),
        out_shape=(whole, token) if start else whole,
        in_specs=[VMEM, VMEM] if start else [VMEM, VMEM, HBM],
        out_specs=(HBM, VMEM) if start else HBM,
        input_output_aliases={} if start else {2: 0},
        scratch_shapes=[pltpu.VMEM((share, width), F32), pltpu.SemaphoreType.DMA],
        compiler_params=PARAMS,
        cost_estimate=LONG,
        name="write",
    )(keep, recv, *([] if start else [result]))


def body(a_blocks, a_cols, mushy, p_blocks, p_cols, send_rows):
    rows, size, inner = p_blocks.shape[1:]
    acol, pcol = a_cols.transpose(2, 0, 1), p_cols[0].T
    mush, sends = mushy[0], send_rows[0]
    ablk, pblk = a_blocks[0], p_blocks[0]
    count = sends.shape[0] // 2
    width = NCOL * size
    length = lax.axis_size("gx")
    parts = lax.axis_size("gy")
    share = width // parts

    tail = -(-count * pcol.shape[0] // 16) * 16
    packed = jax.ShapeDtypeStruct((count * size + tail, inner), BF16)

    first, second = pl.pallas_call(
        pack_kernel,
        out_shape=(packed, packed),
        in_specs=[HBM] * 3,
        out_specs=(HBM, HBM),
        scratch_shapes=[
            pltpu.SMEM(sends.shape, sends.dtype),
            pltpu.SMEM(pcol.shape, pcol.dtype),
            pltpu.VMEM(pblk.shape, BF16),
            pltpu.VMEM((2,) + packed.shape, BF16),
            pltpu.SemaphoreType.DMA((3,)),
        ],
        compiler_params=pltpu.CompilerParams(vmem_limit_bytes=56 * 1024 * 1024),
        cost_estimate=LONG,
        name="pack",
    )(sends, pcol, pblk)
    even = [(i, i + 1) for i in range(0, length - 1, 2)]
    uneven = [(i, i + 1) for i in range(1, length - 1, 2)]
    first = lax.ppermute(first, "gx", even + [(j, i) for i, j in even])

    partial = (
        jax.ShapeDtypeStruct((parts // 2, share, width), F32),
        jax.ShapeDtypeStruct((parts // 2, share, width), BF16),
    )
    own_t, keep, send, second = pl.pallas_call(
        functools.partial(own_kernel, parts),
        out_shape=(jax.ShapeDtypeStruct((width, rows * size), BF16),) + partial + (packed,),
        in_specs=[SMEM, SMEM, SMEM, VMEM, VMEM, HBM],
        out_specs=(VMEM, VMEM, VMEM, HBM),
        input_output_aliases={5: 3},
        scratch_shapes=[
            pltpu.VMEM((rows + 1, size, width), BF16),
            pltpu.VMEM((rows * size, width), BF16),
        ],
        compiler_params=PARAMS,
        cost_estimate=SHORT,
        name="own",
    )(acol, mush, pcol, ablk, pblk, second)
    second = lax.ppermute(second, "gx", uneven + [(j, i) for i, j in uneven])
    keep, recv, folds = folded(keep, send, parts)
    split = jax.ShapeDtypeStruct((2, rows * size, count * size), BF16)
    high, low = pl.pallas_call(
        scatter_kernel,
        out_shape=(split, split),
        in_specs=[SMEM, SMEM, VMEM],
        out_specs=(VMEM, VMEM),
        compiler_params=PARAMS,
        cost_estimate=LONG,
        name="scatter",
    )(acol, mush, ablk)
    pieces = []
    for order, ghosts in enumerate((first, second)):
        after = [] if order else [folds]
        pieces.append(
            pl.pallas_call(
                functools.partial(ghost_kernel, order),
                out_shape=partial,
                in_specs=[VMEM] * (4 + len(after)),
                out_specs=(VMEM, VMEM),
                scratch_shapes=[
                    pltpu.VMEM((count * size, width), BF16),
                    pltpu.VMEM((rows * size, width), BF16),
                ],
                compiler_params=PARAMS,
                cost_estimate=LONG,
                name="ghost",
            )(high, low, ghosts, own_t, *after)
        )
    result, token = written(None, keep, recv, None)
    sides = [folded(*pieces[0], parts), folded(*pieces[1], parts, (token,))]
    for order, (keep, recv, folds) in enumerate(sides):
        result = written(order, keep, recv, result)
    return result[None]


def solution(mesh):
    placed = (
        P("gx", "gy", None, None),
        P("gx", "gy", None),
        P("gx", "gy"),
        P("gx", "gy", None, None),
        P("gx", "gy", None),
        P("gx", "gy"),
    )
    return jax.shard_map(
        body, mesh=mesh, in_specs=placed, out_specs=P("gx", "gy", None), check_vma=False
    )
```

```python
import functools

import jax
import jax.numpy as jnp
from jax import lax
from jax.experimental import pallas as pl
from jax.experimental.pallas import tpu as pltpu
from jax.sharding import PartitionSpec as P

KA = 7
KS = 3
NCOL = 8
LANES = 128
WIDE = 256

F32 = jnp.float32
BF16 = jnp.bfloat16
SMEM = pl.BlockSpec(memory_space=pltpu.SMEM)
VMEM = pl.BlockSpec(memory_space=pltpu.VMEM)
HBM = pl.BlockSpec(memory_space=pltpu.HBM)
LONG = pl.CostEstimate(flops=10000000000, bytes_accessed=1000000, transcendentals=0)
SHORT = pl.CostEstimate(flops=1000000000, bytes_accessed=1000000, transcendentals=0)
PARAMS = pltpu.CompilerParams(vmem_limit_bytes=24 * 1024 * 1024)


def spread(value, masks_of, width):
    size = value.shape[0]
    row = lax.broadcasted_iota(jnp.int32, (size, WIDE), 0)
    lane = lax.broadcasted_iota(jnp.int32, (size, WIDE), 1)
    unit = jnp.where(row == lane % size, 1.0, 0.0).astype(BF16)
    tiles = []
    for c in range(width // WIDE):
        moves = jnp.concatenate([unit * mask for mask in masks_of(c * WIDE // size)], axis=0)
        tiles.append(jnp.dot(value, moves, preferred_element_type=F32))
    return tiles


def masks_at(cols, size, dtype):
    slots = (lax.broadcasted_iota(jnp.int32, (1, WIDE), 1) // size).astype(dtype)
    return lambda first: [
        jnp.where(slots == col - first, 1.0, 0.0).astype(BF16) for col in cols
    ]


def multiply(acol, mush, a_ref, base, ext_ref, prod_ref):
    rows, size = a_ref.shape[0], a_ref.shape[1]
    ext_ref[ext_ref.shape[0] - 1] = jnp.zeros(ext_ref.shape[1:], BF16)
    none = ext_ref.shape[0] - 1
    for n in range(rows):
        limit = jnp.where(mush[n] > 0, KA, KS)
        picks = []
        for k in range(KA):
            spot = acol[k, 0, n] - base
            good = (k < limit) & (spot >= 0) & (spot < none)
            picks.append(jnp.where(good, spot, none))
        picked = jnp.concatenate([ext_ref[spot] for spot in picks], axis=0)
        value = jnp.dot(a_ref[n], picked, preferred_element_type=F32)
        prod_ref[n * size : (n + 1) * size, :] = value.astype(BF16)


def finish(ownt_ref, prod, keep_ref, send_ref):
    rows = ownt_ref.shape[0] // 2
    sent = jnp.dot(ownt_ref[rows:, :], prod, preferred_element_type=F32)
    send_ref[...] = sent.astype(BF16).reshape(send_ref.shape)
    kept = jnp.dot(ownt_ref[:rows, :], prod, preferred_element_type=F32)
    keep_ref[...] = kept.reshape(keep_ref.shape)


def pack_kernel(
    sends_in, pcol_in, mush_in, p_in, first_ref, second_ref, mush, sends, pcol, p_ref, packed_ref, sems
):
    copies = [
        pltpu.make_async_copy(src, dst, sems.at[i])
        for i, (src, dst) in enumerate(
            ((sends_in, sends), (pcol_in, pcol), (mush_in, mush), (p_in, p_ref))
        )
    ]
    for copy in copies:
        copy.start()
    for copy in copies[:3]:
        copy.wait()
    odd = lax.axis_index("gx") % 2
    count = sends.shape[0] // 2
    size = p_ref.shape[1]
    slots = pcol.shape[0]
    starts = ((1 - odd) * count, odd * count)
    tail = packed_ref.shape[1] - count * size
    which = lax.broadcasted_iota(jnp.int32, (tail, packed_ref.shape[2]), 0)
    for i, start in enumerate(starts):
        cols = jnp.zeros(which.shape, F32)
        for s in range(count):
            row = sends[start + s]
            for j in range(slots):
                cols = jnp.where(which == s * slots + j, pcol[j, row].astype(F32), cols)
        packed_ref[i, count * size :, :] = cols.astype(BF16)
    copies[3].wait()
    copies = []
    for i, (out_ref, start) in enumerate(zip((first_ref, second_ref), starts)):
        for s in range(count):
            packed_ref[i, s * size : (s + 1) * size, :] = p_ref[sends[start + s]]
        copies.append(pltpu.make_async_copy(packed_ref.at[i], out_ref, sems.at[i]))
        copies[-1].start()
    for copy in copies:
        copy.wait()


def own_kernel(parts, acol, mush, pcol, a_ref, p_ref, ownt_ref, keep_ref, send_ref, own_ref, prod_ref):
    bit = lax.axis_index("gy") % 2
    rows, size = p_ref.shape[0], p_ref.shape[1]
    width = NCOL * size
    share = width // parts
    for n in range(rows):
        masks = masks_at([pcol[j, n] for j in range(pcol.shape[0])], size, jnp.int32)
        for c, tile in enumerate(spread(p_ref[n], masks, width)):
            own_ref[n, :, c * WIDE : (c + 1) * WIDE] = tile.astype(BF16)
    for c in range(width // LANES):
        column = own_ref[:rows, :, c * LANES : (c + 1) * LANES]
        flipped = column.reshape(rows * size, LANES).T
        for k in range(LANES // share):
            part = c * (LANES // share) + k
            spot = part // 2 + jnp.where(part % 2 == bit, 0, parts // 2)
            at = pl.ds(pl.multiple_of(spot * share, share), share)
            ownt_ref[at, :] = flipped[k * share : (k + 1) * share, :]
    multiply(acol, mush, a_ref, 0, own_ref, prod_ref)
    finish(ownt_ref, prod_ref[...], keep_ref, send_ref)


def scatter_kernel(acol, mush, a_ref, high_ref, low_ref):
    odd = lax.axis_index("gx") % 2
    rows, size = a_ref.shape[0], a_ref.shape[1]
    width = high_ref.shape[2]
    for n in range(rows):
        limit = jnp.where(mush[n] > 0, KA, KS)
        at = slice(n * size, (n + 1) * size)
        for order in range(2):
            right = odd if order else 1 - odd
            base = rows + right * (width // size)
            cols = [jnp.where(k < limit, acol[k, 0, n] - base, -1) for k in range(KA)]
            masks = masks_at(cols, size, jnp.int32)
            for c, tile in enumerate(spread(a_ref[n], masks, width)):
                spot = slice(c * WIDE, (c + 1) * WIDE)
                high = tile.astype(BF16)
                high_ref[order, at, spot] = high
                low_ref[order, at, spot] = (tile - high.astype(F32)).astype(BF16)


def ghost_kernel(order, high_ref, low_ref, in_ref, ownt_ref, *refs):
    keep_ref, send_ref, ext_ref, prod_ref = refs[-4:]
    width = ownt_ref.shape[0]
    size = width // NCOL
    slots = in_ref.shape[1] // size
    count = ext_ref.shape[0] // size
    cols = in_ref[count * size :, :].astype(F32)
    for n in range(count):
        at = slice(n * size, (n + 1) * size)
        masks = masks_at([cols[n * slots + j : n * slots + j + 1, :] for j in range(slots)], size, F32)
        for c, tile in enumerate(spread(in_ref[at, :], masks, width)):
            ext_ref[at, c * WIDE : (c + 1) * WIDE] = tile.astype(BF16)
    ext = ext_ref[...]
    step = prod_ref.shape[0] // 2
    for m in range(2):
        at = slice(m * step, (m + 1) * step)
        value = jnp.dot(high_ref[order, at, :], ext, preferred_element_type=F32)
        value += jnp.dot(low_ref[order, at, :], ext, preferred_element_type=F32)
        prod_ref[at, :] = value.astype(BF16)
    finish(ownt_ref, prod_ref[...], keep_ref, send_ref)


def fold_kernel(stage, keep_ref, recv_ref, *refs):
    next_ref, send_ref = refs[-2:]
    bit = (lax.axis_index("gy") >> stage) % 2
    for i in range(next_ref.shape[0]):
        mine, other = 2 * i + bit, 2 * i + 1 - bit
        send_ref[i] = (keep_ref[other] + recv_ref[other].astype(F32)).astype(BF16)
        next_ref[i] = keep_ref[mine] + recv_ref[mine].astype(F32)


def write_kernel(order, keep_ref, recv_ref, *refs):
    sum_ref, sem = refs[-2:]
    out_ref = refs[0 if order is None else 1]
    odd = lax.axis_index("gx") % 2
    third = 1 if order is None else 2 * odd if order else 2 - 2 * odd
    width = sum_ref.shape[1]
    sum_ref[...] = keep_ref[0] + recv_ref[0].astype(F32)
    spot = pl.ds(pl.multiple_of(third * width, width), width)
    copy = pltpu.make_async_copy(sum_ref, out_ref.at[:, spot], sem)
    copy.start()
    if order is None:
        refs[1][...] = jnp.zeros(refs[1].shape, F32)
    copy.wait()


def swapped(value, axis, step):
    length = lax.axis_size(axis)
    return lax.ppermute(value, axis, [(i, i ^ step) for i in range(length) if i ^ step < length])


def folded(keep, send, parts, after=()):
    left, share, width = keep.shape
    stage = 0
    while left > 1:
        recv = swapped(send, "gy", 1 << stage)
        stage += 1
        left //= 2
        keep, send = pl.pallas_call(
            functools.partial(fold_kernel, stage),
            out_shape=(
                jax.ShapeDtypeStruct((left, share, width), F32),
                jax.ShapeDtypeStruct((left, share, width), BF16),
            ),
            in_specs=[VMEM] * (2 + len(after)),
            out_specs=(VMEM, VMEM),
            compiler_params=PARAMS,
            name="fold",
        )(keep, recv, *after)
        after = ()
    return keep, swapped(send, "gy", 1 << stage), keep


def written(order, keep, recv, result):
    share, width = keep.shape[1:]
    start = order is None
    whole = jax.ShapeDtypeStruct((share, 3 * width), F32)
    token = jax.ShapeDtypeStruct((8, LANES), F32)
    return pl.pallas_call(
        functools.partial(write_kernel, order),
        out_shape=(whole, token) if start else whole,
        in_specs=[VMEM, VMEM] if start else [VMEM, VMEM, HBM],
        out_specs=(HBM, VMEM) if start else HBM,
        input_output_aliases={} if start else {2: 0},
        scratch_shapes=[pltpu.VMEM((share, width), F32), pltpu.SemaphoreType.DMA],
        compiler_params=PARAMS,
        cost_estimate=LONG,
        name="write",
    )(keep, recv, *([] if start else [result]))


def body(a_blocks, a_cols, mushy, p_blocks, p_cols, send_rows):
    rows, size, inner = p_blocks.shape[1:]
    acol, pcol = a_cols.transpose(2, 0, 1), p_cols[0].T
    mush, sends = mushy[0], send_rows[0]
    ablk, pblk = a_blocks[0], p_blocks[0]
    count = sends.shape[0] // 2
    width = NCOL * size
    length = lax.axis_size("gx")
    parts = lax.axis_size("gy")
    share = width // parts

    tail = -(-count * pcol.shape[0] // 16) * 16
    packed = jax.ShapeDtypeStruct((count * size + tail, inner), BF16)

    first, second, mush = pl.pallas_call(
        pack_kernel,
        out_shape=(packed, packed, jax.ShapeDtypeStruct(mush.shape, mush.dtype)),
        in_specs=[HBM] * 4,
        out_specs=(HBM, HBM, SMEM),
        scratch_shapes=[
            pltpu.SMEM(sends.shape, sends.dtype),
            pltpu.SMEM(pcol.shape, pcol.dtype),
            pltpu.VMEM(pblk.shape, BF16),
            pltpu.VMEM((2,) + packed.shape, BF16),
            pltpu.SemaphoreType.DMA((4,)),
        ],
        compiler_params=pltpu.CompilerParams(vmem_limit_bytes=56 * 1024 * 1024),
        cost_estimate=LONG,
        name="pack",
    )(sends, pcol, mush, pblk)
    pairs = [(i, i ^ 1) for i in range(length) if i ^ 1 < length]
    if length % 2:
        uneven = [(i, i + 1) for i in range(1, length - 1, 2)]
        second = lax.ppermute(second, "gx", uneven + [(j, i) for i, j in uneven])
    else:
        second = lax.ppermute(second, "gx", pairs)
    first = lax.ppermute(first, "gx", pairs)

    partial = (
        jax.ShapeDtypeStruct((parts // 2, share, width), F32),
        jax.ShapeDtypeStruct((parts // 2, share, width), BF16),
    )
    own_t, keep, send = pl.pallas_call(
        functools.partial(own_kernel, parts),
        out_shape=(jax.ShapeDtypeStruct((width, rows * size), BF16),) + partial,
        in_specs=[SMEM, SMEM, SMEM, VMEM, VMEM],
        out_specs=(VMEM, VMEM, VMEM),
        scratch_shapes=[
            pltpu.VMEM((rows + 1, size, width), BF16),
            pltpu.VMEM((rows * size, width), BF16),
        ],
        compiler_params=PARAMS,
        cost_estimate=LONG,
        name="own",
    )(acol, mush, pcol, ablk, pblk)
    if length % 2 == 0:
        hops = [(i, i + 2 - 4 * (i % 2)) for i in range(length)]
        second = lax.ppermute(second, "gx", [(i, j) for i, j in hops if 0 <= j < length])
    keep, recv, folds = folded(keep, send, parts)
    split = jax.ShapeDtypeStruct((2, rows * size, count * size), BF16)
    high, low = pl.pallas_call(
        scatter_kernel,
        out_shape=(split, split),
        in_specs=[SMEM, SMEM, VMEM],
        out_specs=(VMEM, VMEM),
        compiler_params=PARAMS,
        cost_estimate=LONG,
        name="scatter",
    )(acol, mush, ablk)
    pieces = []
    for order, ghosts in enumerate((first, second)):
        after = [] if order else [folds]
        pieces.append(
            pl.pallas_call(
                functools.partial(ghost_kernel, order),
                out_shape=partial,
                in_specs=[VMEM] * (4 + len(after)),
                out_specs=(VMEM, VMEM),
                scratch_shapes=[
                    pltpu.VMEM((count * size, width), BF16),
                    pltpu.VMEM((rows * size, width), BF16),
                ],
                compiler_params=PARAMS,
                cost_estimate=LONG if order else SHORT,
                name="ghost",
            )(high, low, ghosts, own_t, *after)
        )
    result, token = written(None, keep, recv, None)
    sides = [folded(*pieces[0], parts), folded(*pieces[1], parts, (token,))]
    for order, (keep, recv, folds) in enumerate(sides):
        result = written(order, keep, recv, result)
    return result[None]


def solution(mesh):
    placed = (
        P("gx", "gy", None, None),
        P("gx", "gy", None),
        P("gx", "gy"),
        P("gx", "gy", None, None),
        P("gx", "gy", None),
        P("gx", "gy"),
    )
    return jax.shard_map(
        body, mesh=mesh, in_specs=placed, out_specs=P("gx", "gy", None), check_vma=False
    )
```

```python
import functools

import jax
import jax.numpy as jnp
from jax import lax
from jax.experimental import pallas as pl
from jax.experimental.pallas import tpu as pltpu
from jax.sharding import PartitionSpec as P

KA = 7
KS = 3
NCOL = 8
LANES = 128
WIDE = 256

F32 = jnp.float32
BF16 = jnp.bfloat16
SMEM = pl.BlockSpec(memory_space=pltpu.SMEM)
VMEM = pl.BlockSpec(memory_space=pltpu.VMEM)
HBM = pl.BlockSpec(memory_space=pltpu.HBM)
LONG = pl.CostEstimate(flops=10000000000, bytes_accessed=1000000, transcendentals=0)
PARAMS = pltpu.CompilerParams(vmem_limit_bytes=24 * 1024 * 1024)


def spread(value, masks_of, width):
    size = value.shape[0]
    row = lax.broadcasted_iota(jnp.int32, (size, WIDE), 0)
    lane = lax.broadcasted_iota(jnp.int32, (size, WIDE), 1)
    unit = jnp.where(row == lane % size, 1.0, 0.0).astype(BF16)
    tiles = []
    for c in range(width // WIDE):
        moves = jnp.concatenate([unit * mask for mask in masks_of(c * WIDE // size)], axis=0)
        tiles.append(jnp.dot(value, moves, preferred_element_type=F32))
    return tiles


def masks_at(cols, size, dtype):
    slots = (lax.broadcasted_iota(jnp.int32, (1, WIDE), 1) // size).astype(dtype)
    return lambda first: [
        jnp.where(slots == col - first, 1.0, 0.0).astype(BF16) for col in cols
    ]


def multiply(acol, mush, a_ref, base, ext_ref, prod_ref):
    rows, size = a_ref.shape[0], a_ref.shape[1]
    ext_ref[ext_ref.shape[0] - 1] = jnp.zeros(ext_ref.shape[1:], BF16)
    none = ext_ref.shape[0] - 1
    for n in range(rows):
        limit = jnp.where(mush[n] > 0, KA, KS)
        picks = []
        for k in range(KA):
            spot = acol[k, 0, n] - base
            good = (k < limit) & (spot >= 0) & (spot < none)
            picks.append(jnp.where(good, spot, none))
        picked = jnp.concatenate([ext_ref[spot] for spot in picks], axis=0)
        value = jnp.dot(a_ref[n], picked, preferred_element_type=F32)
        prod_ref[n * size : (n + 1) * size, :] = value.astype(BF16)


def finish(ownt_ref, prod, keep_ref, send_ref):
    rows = ownt_ref.shape[0] // 2
    sent = jnp.dot(ownt_ref[rows:, :], prod, preferred_element_type=F32)
    send_ref[...] = sent.astype(BF16).reshape(send_ref.shape)
    kept = jnp.dot(ownt_ref[:rows, :], prod, preferred_element_type=F32)
    keep_ref[...] = kept.reshape(keep_ref.shape)


def pack_kernel(
    sends_in, pcol_in, mush_in, p_in, first_ref, second_ref, mush, sends, pcol, p_ref, packed_ref, sems
):
    copies = [
        pltpu.make_async_copy(src, dst, sems.at[i])
        for i, (src, dst) in enumerate(
            ((sends_in, sends), (pcol_in, pcol), (mush_in, mush), (p_in, p_ref))
        )
    ]
    for copy in copies:
        copy.start()
    for copy in copies[:3]:
        copy.wait()
    odd = lax.axis_index("gx") % 2
    count = sends.shape[0] // 2
    size = p_ref.shape[1]
    slots = pcol.shape[0]
    starts = ((1 - odd) * count, odd * count)
    tail = packed_ref.shape[1] - count * size
    which = lax.broadcasted_iota(jnp.int32, (tail, packed_ref.shape[2]), 0)
    for i, start in enumerate(starts):
        cols = jnp.zeros(which.shape, F32)
        for s in range(count):
            row = sends[start + s]
            for j in range(slots):
                cols = jnp.where(which == s * slots + j, pcol[j, row].astype(F32), cols)
        packed_ref[i, count * size :, :] = cols.astype(BF16)
    copies[3].wait()
    copies = []
    for i, (out_ref, start) in enumerate(zip((first_ref, second_ref), starts)):
        for s in range(count):
            packed_ref[i, s * size : (s + 1) * size, :] = p_ref[sends[start + s]]
        copies.append(pltpu.make_async_copy(packed_ref.at[i, : out_ref.shape[0]], out_ref, sems.at[i]))
        copies[-1].start()
    for copy in copies:
        copy.wait()


def own_kernel(parts, acol, mush, pcol, a_ref, p_ref, ownt_ref, keep_ref, send_ref, own_ref, prod_ref):
    bit = lax.axis_index("gy") % 2
    rows, size = p_ref.shape[0], p_ref.shape[1]
    width = NCOL * size
    share = width // parts
    for n in range(rows):
        masks = masks_at([pcol[j, n] for j in range(pcol.shape[0])], size, jnp.int32)
        for c, tile in enumerate(spread(p_ref[n], masks, width)):
            own_ref[n, :, c * WIDE : (c + 1) * WIDE] = tile.astype(BF16)
    for c in range(width // LANES):
        column = own_ref[:rows, :, c * LANES : (c + 1) * LANES]
        flipped = column.reshape(rows * size, LANES).T
        for k in range(LANES // share):
            part = c * (LANES // share) + k
            spot = part // 2 + jnp.where(part % 2 == bit, 0, parts // 2)
            at = pl.ds(pl.multiple_of(spot * share, share), share)
            ownt_ref[at, :] = flipped[k * share : (k + 1) * share, :]
    multiply(acol, mush, a_ref, 0, own_ref, prod_ref)
    finish(ownt_ref, prod_ref[...], keep_ref, send_ref)


def scatter_kernel(acol, mush, a_ref, high_ref, low_ref):
    odd = lax.axis_index("gx") % 2
    rows, size = a_ref.shape[0], a_ref.shape[1]
    width = high_ref.shape[2]
    for n in range(rows):
        limit = jnp.where(mush[n] > 0, KA, KS)
        at = slice(n * size, (n + 1) * size)
        for order in range(2):
            right = odd if order else 1 - odd
            base = rows + right * (width // size)
            cols = [jnp.where(k < limit, acol[k, 0, n] - base, -1) for k in range(KA)]
            masks = masks_at(cols, size, jnp.int32)
            for c, tile in enumerate(spread(a_ref[n], masks, width)):
                spot = slice(c * WIDE, (c + 1) * WIDE)
                high = tile.astype(BF16)
                high_ref[order, at, spot] = high
                low_ref[order, at, spot] = (tile - high.astype(F32)).astype(BF16)


def ghost_kernel(order, high_ref, low_ref, in_ref, ownt_ref, *refs):
    keep_ref, send_ref, ext_ref, prod_ref = refs[-4:]
    width = ownt_ref.shape[0]
    size = width // NCOL
    slots = in_ref.shape[1] // size
    count = ext_ref.shape[0] // size
    cols = in_ref[count * size :, :].astype(F32)
    for n in range(count):
        at = slice(n * size, (n + 1) * size)
        masks = masks_at([cols[n * slots + j : n * slots + j + 1, :] for j in range(slots)], size, F32)
        for c, tile in enumerate(spread(in_ref[at, :], masks, width)):
            ext_ref[at, c * WIDE : (c + 1) * WIDE] = tile.astype(BF16)
    ext = ext_ref[...]
    step = prod_ref.shape[0] // 2
    for m in range(2):
        at = slice(m * step, (m + 1) * step)
        value = jnp.dot(high_ref[order, at, :], ext, preferred_element_type=F32)
        value += jnp.dot(low_ref[order, at, :], ext, preferred_element_type=F32)
        prod_ref[at, :] = value.astype(BF16)
    finish(ownt_ref, prod_ref[...], keep_ref, send_ref)


def fold_kernel(stage, keep_ref, recv_ref, *refs):
    next_ref, send_ref = refs[-2:]
    bit = (lax.axis_index("gy") >> stage) % 2
    for i in range(next_ref.shape[0]):
        mine, other = 2 * i + bit, 2 * i + 1 - bit
        send_ref[i] = (keep_ref[other] + recv_ref[other].astype(F32)).astype(BF16)
        next_ref[i] = keep_ref[mine] + recv_ref[mine].astype(F32)


def write_kernel(order, keep_ref, recv_ref, *refs):
    sum_ref, sem = refs[-2:]
    out_ref = refs[0 if order is None else 1]
    odd = lax.axis_index("gx") % 2
    third = 1 if order is None else 2 * odd if order else 2 - 2 * odd
    width = sum_ref.shape[1]
    sum_ref[...] = keep_ref[0] + recv_ref[0].astype(F32)
    spot = pl.ds(pl.multiple_of(third * width, width), width)
    copy = pltpu.make_async_copy(sum_ref, out_ref.at[:, spot], sem)
    copy.start()
    if order is None:
        refs[1][...] = jnp.zeros(refs[1].shape, F32)
    copy.wait()


def swapped(value, axis, step):
    length = lax.axis_size(axis)
    return lax.ppermute(value, axis, [(i, i ^ step) for i in range(length) if i ^ step < length])


def folded(keep, send, parts, after=()):
    left, share, width = keep.shape
    stage = 0
    while left > 1:
        recv = swapped(send, "gy", 1 << stage)
        stage += 1
        left //= 2
        keep, send = pl.pallas_call(
            functools.partial(fold_kernel, stage),
            out_shape=(
                jax.ShapeDtypeStruct((left, share, width), F32),
                jax.ShapeDtypeStruct((left, share, width), BF16),
            ),
            in_specs=[VMEM] * (2 + len(after)),
            out_specs=(VMEM, VMEM),
            compiler_params=PARAMS,
            name="fold",
        )(keep, recv, *after)
        after = ()
    return keep, swapped(send, "gy", 1 << stage), keep


def written(order, keep, recv, result):
    share, width = keep.shape[1:]
    start = order is None
    whole = jax.ShapeDtypeStruct((share, 3 * width), F32)
    token = jax.ShapeDtypeStruct((8, LANES), F32)
    return pl.pallas_call(
        functools.partial(write_kernel, order),
        out_shape=(whole, token) if start else whole,
        in_specs=[VMEM, VMEM] if start else [VMEM, VMEM, HBM],
        out_specs=(HBM, VMEM) if start else HBM,
        input_output_aliases={} if start else {2: 0},
        scratch_shapes=[pltpu.VMEM((share, width), F32), pltpu.SemaphoreType.DMA],
        compiler_params=PARAMS,
        cost_estimate=LONG,
        name="write",
    )(keep, recv, *([] if start else [result]))


def body(a_blocks, a_cols, mushy, p_blocks, p_cols, send_rows):
    rows, size, inner = p_blocks.shape[1:]
    acol, pcol = a_cols.transpose(2, 0, 1), p_cols[0].T
    mush, sends = mushy[0], send_rows[0]
    ablk, pblk = a_blocks[0], p_blocks[0]
    count = sends.shape[0] // 2
    width = NCOL * size
    length = lax.axis_size("gx")
    parts = lax.axis_size("gy")
    share = width // parts

    tail = -(-count * pcol.shape[0] // 16) * 16
    packed = jax.ShapeDtypeStruct((count * size + tail, inner), BF16)
    longer = jax.ShapeDtypeStruct((count * size + tail + 16, inner), BF16)

    first, second, mush = pl.pallas_call(
        pack_kernel,
        out_shape=(packed, longer, jax.ShapeDtypeStruct(mush.shape, mush.dtype)),
        in_specs=[HBM] * 4,
        out_specs=(HBM, HBM, SMEM),
        scratch_shapes=[
            pltpu.SMEM(sends.shape, sends.dtype),
            pltpu.SMEM(pcol.shape, pcol.dtype),
            pltpu.VMEM(pblk.shape, BF16),
            pltpu.VMEM((2,) + longer.shape, BF16),
            pltpu.SemaphoreType.DMA((4,)),
        ],
        compiler_params=pltpu.CompilerParams(vmem_limit_bytes=56 * 1024 * 1024),
        cost_estimate=LONG,
        name="pack",
    )(sends, pcol, mush, pblk)
    even = [(i, i + 1) for i in range(0, length - 1, 2)]
    uneven = [(i, i + 1) for i in range(1, length - 1, 2)]
    first = lax.ppermute(first, "gx", even + [(j, i) for i, j in even])
    second = lax.ppermute(second, "gx", uneven + [(j, i) for i, j in uneven])

    partial = (
        jax.ShapeDtypeStruct((parts // 2, share, width), F32),
        jax.ShapeDtypeStruct((parts // 2, share, width), BF16),
    )
    own_t, keep, send = pl.pallas_call(
        functools.partial(own_kernel, parts),
        out_shape=(jax.ShapeDtypeStruct((width, rows * size), BF16),) + partial,
        in_specs=[SMEM, SMEM, SMEM, VMEM, VMEM],
        out_specs=(VMEM, VMEM, VMEM),
        scratch_shapes=[
            pltpu.VMEM((rows + 1, size, width), BF16),
            pltpu.VMEM((rows * size, width), BF16),
        ],
        compiler_params=PARAMS,
        cost_estimate=LONG,
        name="own",
    )(acol, mush, pcol, ablk, pblk)
    keep, recv, folds = folded(keep, send, parts)
    split = jax.ShapeDtypeStruct((2, rows * size, count * size), BF16)
    high, low = pl.pallas_call(
        scatter_kernel,
        out_shape=(split, split),
        in_specs=[SMEM, SMEM, VMEM],
        out_specs=(VMEM, VMEM),
        compiler_params=PARAMS,
        cost_estimate=LONG,
        name="scatter",
    )(acol, mush, ablk)
    pieces = []
    for order, ghosts in enumerate((first, second)):
        after = [folds] if order else []
        pieces.append(
            pl.pallas_call(
                functools.partial(ghost_kernel, order),
                out_shape=partial,
                in_specs=[VMEM] * (4 + len(after)),
                out_specs=(VMEM, VMEM),
                scratch_shapes=[
                    pltpu.VMEM((count * size, width), BF16),
                    pltpu.VMEM((rows * size, width), BF16),
                ],
                compiler_params=PARAMS,
                cost_estimate=LONG,
                name="ghost",
            )(high, low, ghosts, own_t, *after)
        )
    result, token = written(None, keep, recv, None)
    sides = [folded(*pieces[0], parts), folded(*pieces[1], parts, (token,))]
    for order, (keep, recv, folds) in enumerate(sides):
        result = written(order, keep, recv, result)
    return result[None]


def solution(mesh):
    placed = (
        P("gx", "gy", None, None),
        P("gx", "gy", None),
        P("gx", "gy"),
        P("gx", "gy", None, None),
        P("gx", "gy", None),
        P("gx", "gy"),
    )
    return jax.shard_map(
        body, mesh=mesh, in_specs=placed, out_specs=P("gx", "gy", None), check_vma=False
    )
```

```python
import functools

import jax
import jax.numpy as jnp
from jax import lax
from jax.experimental import pallas as pl
from jax.experimental.pallas import tpu as pltpu
from jax.sharding import PartitionSpec as P

KA = 7
KS = 3
NCOL = 8
LANES = 128
WIDE = 256

F32 = jnp.float32
BF16 = jnp.bfloat16
SMEM = pl.BlockSpec(memory_space=pltpu.SMEM)
VMEM = pl.BlockSpec(memory_space=pltpu.VMEM)
HBM = pl.BlockSpec(memory_space=pltpu.HBM)
LONG = pl.CostEstimate(flops=10000000000, bytes_accessed=1000000, transcendentals=0)
SHORT = pl.CostEstimate(flops=1000000000, bytes_accessed=1000000, transcendentals=0)
PARAMS = pltpu.CompilerParams(vmem_limit_bytes=24 * 1024 * 1024)


def spread(value, masks_of, width):
    size = value.shape[0]
    row = lax.broadcasted_iota(jnp.int32, (size, WIDE), 0)
    lane = lax.broadcasted_iota(jnp.int32, (size, WIDE), 1)
    unit = jnp.where(row == lane % size, 1.0, 0.0).astype(BF16)
    tiles = []
    for c in range(width // WIDE):
        moves = jnp.concatenate([unit * mask for mask in masks_of(c * WIDE // size)], axis=0)
        tiles.append(jnp.dot(value, moves, preferred_element_type=F32))
    return tiles


def masks_at(cols, size, dtype):
    slots = (lax.broadcasted_iota(jnp.int32, (1, WIDE), 1) // size).astype(dtype)
    return lambda first: [
        jnp.where(slots == col - first, 1.0, 0.0).astype(BF16) for col in cols
    ]


def multiply(acol, mush, a_ref, base, ext_ref, prod_ref):
    rows, size = a_ref.shape[0], a_ref.shape[1]
    ext_ref[ext_ref.shape[0] - 1] = jnp.zeros(ext_ref.shape[1:], BF16)
    none = ext_ref.shape[0] - 1
    for n in range(rows):
        limit = jnp.where(mush[n] > 0, KA, KS)
        picks = []
        for k in range(KA):
            spot = acol[k, 0, n] - base
            good = (k < limit) & (spot >= 0) & (spot < none)
            picks.append(jnp.where(good, spot, none))
        picked = jnp.concatenate([ext_ref[spot] for spot in picks], axis=0)
        value = jnp.dot(a_ref[n], picked, preferred_element_type=F32)
        prod_ref[n * size : (n + 1) * size, :] = value.astype(BF16)


def finish(ownt_ref, prod, keep_ref, send_ref):
    rows = ownt_ref.shape[0] // 2
    sent = jnp.dot(ownt_ref[rows:, :], prod, preferred_element_type=F32)
    send_ref[...] = sent.astype(BF16).reshape(send_ref.shape)
    kept = jnp.dot(ownt_ref[:rows, :], prod, preferred_element_type=F32)
    keep_ref[...] = kept.reshape(keep_ref.shape)


def pack_kernel(sends_in, pcol_in, p_in, first_ref, second_ref, sends, pcol, p_ref, packed_ref, sems):
    copies = [
        pltpu.make_async_copy(src, dst, sems.at[i])
        for i, (src, dst) in enumerate(((sends_in, sends), (pcol_in, pcol), (p_in, p_ref)))
    ]
    for copy in copies:
        copy.start()
    for copy in copies[:2]:
        copy.wait()
    odd = lax.axis_index("gx") % 2
    count = sends.shape[0] // 2
    size = p_ref.shape[1]
    slots = pcol.shape[0]
    starts = (odd * count, (1 - odd) * count)
    tail = packed_ref.shape[1] - count * size
    which = lax.broadcasted_iota(jnp.int32, (tail, packed_ref.shape[2]), 0)
    for i, start in enumerate(starts):
        cols = jnp.zeros(which.shape, F32)
        for s in range(count):
            row = sends[start + s]
            for j in range(slots):
                cols = jnp.where(which == s * slots + j, pcol[j, row].astype(F32), cols)
        packed_ref[i, count * size :, :] = cols.astype(BF16)
    copies[2].wait()
    copies = []
    for i, (out_ref, start) in enumerate(zip((first_ref, second_ref), starts)):
        for s in range(count):
            packed_ref[i, s * size : (s + 1) * size, :] = p_ref[sends[start + s]]
        copies.append(pltpu.make_async_copy(packed_ref.at[i], out_ref, sems.at[i]))
        copies[-1].start()
    for copy in copies:
        copy.wait()


def own_kernel(parts, acol, mush, pcol, a_ref, p_ref, passed, ownt_ref, keep_ref, send_ref, *refs):
    own_ref, prod_ref = refs[-2:]
    bit = lax.axis_index("gy") % 2
    rows, size = p_ref.shape[0], p_ref.shape[1]
    width = NCOL * size
    share = width // parts
    for n in range(rows):
        masks = masks_at([pcol[j, n] for j in range(pcol.shape[0])], size, jnp.int32)
        for c, tile in enumerate(spread(p_ref[n], masks, width)):
            own_ref[n, :, c * WIDE : (c + 1) * WIDE] = tile.astype(BF16)
    for c in range(width // LANES):
        column = own_ref[:rows, :, c * LANES : (c + 1) * LANES]
        flipped = column.reshape(rows * size, LANES).T
        for k in range(LANES // share):
            part = c * (LANES // share) + k
            spot = part // 2 + jnp.where(part % 2 == bit, 0, parts // 2)
            at = pl.ds(pl.multiple_of(spot * share, share), share)
            ownt_ref[at, :] = flipped[k * share : (k + 1) * share, :]
    multiply(acol, mush, a_ref, 0, own_ref, prod_ref)
    finish(ownt_ref, prod_ref[...], keep_ref, send_ref)


def scatter_kernel(acol, mush, a_ref, high_ref, low_ref):
    odd = lax.axis_index("gx") % 2
    rows, size = a_ref.shape[0], a_ref.shape[1]
    width = high_ref.shape[2]
    for n in range(rows):
        limit = jnp.where(mush[n] > 0, KA, KS)
        at = slice(n * size, (n + 1) * size)
        for order in range(2):
            right = 1 - odd if order else odd
            base = rows + right * (width // size)
            cols = [jnp.where(k < limit, acol[k, 0, n] - base, -1) for k in range(KA)]
            masks = masks_at(cols, size, jnp.int32)
            for c, tile in enumerate(spread(a_ref[n], masks, width)):
                spot = slice(c * WIDE, (c + 1) * WIDE)
                high = tile.astype(BF16)
                high_ref[order, at, spot] = high
                low_ref[order, at, spot] = (tile - high.astype(F32)).astype(BF16)


def ghost_kernel(order, high_ref, low_ref, in_ref, ownt_ref, *refs):
    keep_ref, send_ref, ext_ref, prod_ref = refs[-4:]
    width = ownt_ref.shape[0]
    size = width // NCOL
    slots = in_ref.shape[1] // size
    count = ext_ref.shape[0] // size
    cols = in_ref[count * size :, :].astype(F32)
    for n in range(count):
        at = slice(n * size, (n + 1) * size)
        masks = masks_at([cols[n * slots + j : n * slots + j + 1, :] for j in range(slots)], size, F32)
        for c, tile in enumerate(spread(in_ref[at, :], masks, width)):
            ext_ref[at, c * WIDE : (c + 1) * WIDE] = tile.astype(BF16)
    ext = ext_ref[...]
    step = prod_ref.shape[0] // 2
    for m in range(2):
        at = slice(m * step, (m + 1) * step)
        value = jnp.dot(high_ref[order, at, :], ext, preferred_element_type=F32)
        value += jnp.dot(low_ref[order, at, :], ext, preferred_element_type=F32)
        prod_ref[at, :] = value.astype(BF16)
    finish(ownt_ref, prod_ref[...], keep_ref, send_ref)


def fold_kernel(stage, keep_ref, recv_ref, *refs):
    next_ref, send_ref = refs[-2:]
    bit = (lax.axis_index("gy") >> stage) % 2
    for i in range(next_ref.shape[0]):
        mine, other = 2 * i + bit, 2 * i + 1 - bit
        send_ref[i] = (keep_ref[other] + recv_ref[other].astype(F32)).astype(BF16)
        next_ref[i] = keep_ref[mine] + recv_ref[mine].astype(F32)


def write_kernel(order, keep_ref, recv_ref, *refs):
    sum_ref, sem = refs[-2:]
    out_ref = refs[0 if order is None else 1]
    odd = lax.axis_index("gx") % 2
    third = 1 if order is None else 2 - 2 * odd if order else 2 * odd
    width = sum_ref.shape[1]
    sum_ref[...] = keep_ref[0] + recv_ref[0].astype(F32)
    spot = pl.ds(pl.multiple_of(third * width, width), width)
    copy = pltpu.make_async_copy(sum_ref, out_ref.at[:, spot], sem)
    copy.start()
    if order is None:
        refs[1][...] = jnp.zeros(refs[1].shape, F32)
    copy.wait()


def swapped(value, axis, step):
    length = lax.axis_size(axis)
    return lax.ppermute(value, axis, [(i, i ^ step) for i in range(length) if i ^ step < length])


def folded(keep, send, parts, after=()):
    left, share, width = keep.shape
    stage = 0
    while left > 1:
        recv = swapped(send, "gy", 1 << stage)
        stage += 1
        left //= 2
        keep, send = pl.pallas_call(
            functools.partial(fold_kernel, stage),
            out_shape=(
                jax.ShapeDtypeStruct((left, share, width), F32),
                jax.ShapeDtypeStruct((left, share, width), BF16),
            ),
            in_specs=[VMEM] * (2 + len(after)),
            out_specs=(VMEM, VMEM),
            compiler_params=PARAMS,
            name="fold",
        )(keep, recv, *after)
        after = ()
    return keep, swapped(send, "gy", 1 << stage), keep


def written(order, keep, recv, result):
    share, width = keep.shape[1:]
    start = order is None
    whole = jax.ShapeDtypeStruct((share, 3 * width), F32)
    token = jax.ShapeDtypeStruct((8, LANES), F32)
    return pl.pallas_call(
        functools.partial(write_kernel, order),
        out_shape=(whole, token) if start else whole,
        in_specs=[VMEM, VMEM] if start else [VMEM, VMEM, HBM],
        out_specs=(HBM, VMEM) if start else HBM,
        input_output_aliases={} if start else {2: 0},
        scratch_shapes=[pltpu.VMEM((share, width), F32), pltpu.SemaphoreType.DMA],
        compiler_params=PARAMS,
        cost_estimate=LONG,
        name="write",
    )(keep, recv, *([] if start else [result]))


def body(a_blocks, a_cols, mushy, p_blocks, p_cols, send_rows):
    rows, size, inner = p_blocks.shape[1:]
    acol, pcol = a_cols.transpose(2, 0, 1), p_cols[0].T
    mush, sends = mushy[0], send_rows[0]
    ablk, pblk = a_blocks[0], p_blocks[0]
    count = sends.shape[0] // 2
    width = NCOL * size
    length = lax.axis_size("gx")
    parts = lax.axis_size("gy")
    share = width // parts

    tail = -(-count * pcol.shape[0] // 16) * 16
    packed = jax.ShapeDtypeStruct((count * size + tail, inner), BF16)

    first, second = pl.pallas_call(
        pack_kernel,
        out_shape=(packed, packed),
        in_specs=[HBM] * 3,
        out_specs=(HBM, HBM),
        scratch_shapes=[
            pltpu.SMEM(sends.shape, sends.dtype),
            pltpu.SMEM(pcol.shape, pcol.dtype),
            pltpu.VMEM(pblk.shape, BF16),
            pltpu.VMEM((2,) + packed.shape, BF16),
            pltpu.SemaphoreType.DMA((3,)),
        ],
        compiler_params=pltpu.CompilerParams(vmem_limit_bytes=56 * 1024 * 1024),
        cost_estimate=LONG,
        name="pack",
    )(sends, pcol, pblk)
    even = [(i, i + 1) for i in range(0, length - 1, 2)]
    uneven = [(i, i + 1) for i in range(1, length - 1, 2)]
    first = lax.ppermute(first, "gx", uneven + [(j, i) for i, j in uneven])

    partial = (
        jax.ShapeDtypeStruct((parts // 2, share, width), F32),
        jax.ShapeDtypeStruct((parts // 2, share, width), BF16),
    )
    own_t, keep, send, second = pl.pallas_call(
        functools.partial(own_kernel, parts),
        out_shape=(jax.ShapeDtypeStruct((width, rows * size), BF16),) + partial + (packed,),
        in_specs=[SMEM, SMEM, SMEM, VMEM, VMEM, HBM],
        out_specs=(VMEM, VMEM, VMEM, HBM),
        input_output_aliases={5: 3},
        scratch_shapes=[
            pltpu.VMEM((rows + 1, size, width), BF16),
            pltpu.VMEM((rows * size, width), BF16),
        ],
        compiler_params=PARAMS,
        cost_estimate=SHORT,
        name="own",
    )(acol, mush, pcol, ablk, pblk, second)
    second = lax.ppermute(second, "gx", even + [(j, i) for i, j in even])
    keep, recv, folds = folded(keep, send, parts)
    split = jax.ShapeDtypeStruct((2, rows * size, count * size), BF16)
    high, low = pl.pallas_call(
        scatter_kernel,
        out_shape=(split, split),
        in_specs=[SMEM, SMEM, VMEM],
        out_specs=(VMEM, VMEM),
        compiler_params=PARAMS,
        cost_estimate=LONG,
        name="scatter",
    )(acol, mush, ablk)
    pieces = []
    for order, ghosts in enumerate((first, second)):
        after = [] if order else [folds]
        pieces.append(
            pl.pallas_call(
                functools.partial(ghost_kernel, order),
                out_shape=partial,
                in_specs=[VMEM] * (4 + len(after)),
                out_specs=(VMEM, VMEM),
                scratch_shapes=[
                    pltpu.VMEM((count * size, width), BF16),
                    pltpu.VMEM((rows * size, width), BF16),
                ],
                compiler_params=PARAMS,
                cost_estimate=LONG,
                name="ghost",
            )(high, low, ghosts, own_t, *after)
        )
    result, token = written(None, keep, recv, None)
    sides = [folded(*pieces[0], parts), folded(*pieces[1], parts, (token,))]
    for order, (keep, recv, folds) in enumerate(sides):
        result = written(order, keep, recv, result)
    return result[None]


def solution(mesh):
    placed = (
        P("gx", "gy", None, None),
        P("gx", "gy", None),
        P("gx", "gy"),
        P("gx", "gy", None, None),
        P("gx", "gy", None),
        P("gx", "gy"),
    )
    return jax.shard_map(
        body, mesh=mesh, in_specs=placed, out_specs=P("gx", "gy", None), check_vma=False
    )
```

```python
import functools

import jax
import jax.numpy as jnp
from jax import lax
from jax.experimental import pallas as pl
from jax.experimental.pallas import tpu as pltpu
from jax.sharding import PartitionSpec as P

KA = 7
KS = 3
NCOL = 8
LANES = 128
WIDE = 256

F32 = jnp.float32
BF16 = jnp.bfloat16
SMEM = pl.BlockSpec(memory_space=pltpu.SMEM)
VMEM = pl.BlockSpec(memory_space=pltpu.VMEM)
HBM = pl.BlockSpec(memory_space=pltpu.HBM)
LONG = pl.CostEstimate(flops=10000000000, bytes_accessed=1000000, transcendentals=0)
MEDIUM = pl.CostEstimate(flops=1000000000, bytes_accessed=1000000, transcendentals=0)
SHORT = pl.CostEstimate(flops=100000000, bytes_accessed=1000000, transcendentals=0)
PARAMS = pltpu.CompilerParams(vmem_limit_bytes=24 * 1024 * 1024)


def spread(value, masks_of, width):
    size = value.shape[0]
    row = lax.broadcasted_iota(jnp.int32, (size, WIDE), 0)
    lane = lax.broadcasted_iota(jnp.int32, (size, WIDE), 1)
    unit = jnp.where(row == lane % size, 1.0, 0.0).astype(BF16)
    tiles = []
    for c in range(width // WIDE):
        moves = jnp.concatenate([unit * mask for mask in masks_of(c * WIDE // size)], axis=0)
        tiles.append(jnp.dot(value, moves, preferred_element_type=F32))
    return tiles


def masks_at(cols, size, dtype):
    slots = (lax.broadcasted_iota(jnp.int32, (1, WIDE), 1) // size).astype(dtype)
    return lambda first: [
        jnp.where(slots == col - first, 1.0, 0.0).astype(BF16) for col in cols
    ]


def multiply(acol, mush, a_ref, base, ext_ref, prod_ref):
    rows, size = a_ref.shape[0], a_ref.shape[1]
    ext_ref[ext_ref.shape[0] - 1] = jnp.zeros(ext_ref.shape[1:], BF16)
    none = ext_ref.shape[0] - 1
    for n in range(rows):
        limit = jnp.where(mush[n] > 0, KA, KS)
        picks = []
        for k in range(KA):
            spot = acol[k, 0, n] - base
            good = (k < limit) & (spot >= 0) & (spot < none)
            picks.append(jnp.where(good, spot, none))
        picked = jnp.concatenate([ext_ref[spot] for spot in picks], axis=0)
        value = jnp.dot(a_ref[n], picked, preferred_element_type=F32)
        prod_ref[n * size : (n + 1) * size, :] = value.astype(BF16)


def finish(ownt_ref, prod, keep_ref, send_ref):
    rows = ownt_ref.shape[0] // 2
    sent = jnp.dot(ownt_ref[rows:, :], prod, preferred_element_type=F32)
    send_ref[...] = sent.astype(BF16).reshape(send_ref.shape)
    kept = jnp.dot(ownt_ref[:rows, :], prod, preferred_element_type=F32)
    keep_ref[...] = kept.reshape(keep_ref.shape)


def pack_kernel(
    sends_in, pcol_in, mush_in, p_in, first_ref, second_ref, mush, sends, pcol, p_ref, packed_ref, sems
):
    copies = [
        pltpu.make_async_copy(src, dst, sems.at[i])
        for i, (src, dst) in enumerate(
            ((sends_in, sends), (pcol_in, pcol), (p_in, p_ref), (mush_in, mush))
        )
    ]
    for copy in copies:
        copy.start()
    for copy in copies[:2]:
        copy.wait()
    odd = lax.axis_index("gx") % 2
    count = sends.shape[0] // 2
    size = p_ref.shape[1]
    slots = pcol.shape[0]
    starts = ((1 - odd) * count, odd * count)
    tail = packed_ref.shape[1] - count * size
    which = lax.broadcasted_iota(jnp.int32, (tail, packed_ref.shape[2]), 0)
    for i, start in enumerate(starts):
        cols = jnp.zeros(which.shape, F32)
        for s in range(count):
            row = sends[start + s]
            for j in range(slots):
                cols = jnp.where(which == s * slots + j, pcol[j, row].astype(F32), cols)
        packed_ref[i, count * size :, :] = cols.astype(BF16)
    copies[2].wait()
    copies = copies[3:]
    for i, (out_ref, start) in enumerate(zip((first_ref, second_ref), starts)):
        for s in range(count):
            packed_ref[i, s * size : (s + 1) * size, :] = p_ref[sends[start + s]]
        copies.append(pltpu.make_async_copy(packed_ref.at[i], out_ref, sems.at[i]))
        copies[-1].start()
    for copy in copies:
        copy.wait()


def own_kernel(parts, acol, mush, pcol, a_ref, p_ref, ownt_ref, keep_ref, send_ref, own_ref, prod_ref):
    bit = lax.axis_index("gy") % 2
    rows, size = p_ref.shape[0], p_ref.shape[1]
    width = NCOL * size
    share = width // parts
    for n in range(rows):
        masks = masks_at([pcol[j, n] for j in range(pcol.shape[0])], size, jnp.int32)
        for c, tile in enumerate(spread(p_ref[n], masks, width)):
            own_ref[n, :, c * WIDE : (c + 1) * WIDE] = tile.astype(BF16)
    for c in range(width // LANES):
        column = own_ref[:rows, :, c * LANES : (c + 1) * LANES]
        flipped = column.reshape(rows * size, LANES).T
        for k in range(LANES // share):
            part = c * (LANES // share) + k
            spot = part // 2 + jnp.where(part % 2 == bit, 0, parts // 2)
            at = pl.ds(pl.multiple_of(spot * share, share), share)
            ownt_ref[at, :] = flipped[k * share : (k + 1) * share, :]
    multiply(acol, mush, a_ref, 0, own_ref, prod_ref)
    finish(ownt_ref, prod_ref[...], keep_ref, send_ref)


def ghost_kernel(order, acol, mush, a_ref, in_ref, ownt_ref, *refs):
    keep_ref, send_ref, high_ref, low_ref, ext_ref, prod_ref = refs[-6:]
    odd = lax.axis_index("gx") % 2
    right = odd if order else 1 - odd
    rows, size = a_ref.shape[0], a_ref.shape[1]
    width = ownt_ref.shape[0]
    slots = in_ref.shape[1] // size
    count = ext_ref.shape[0] // size
    base = rows + right * count
    for n in range(rows):
        limit = jnp.where(mush[n] > 0, KA, KS)
        at = slice(n * size, (n + 1) * size)
        masks = masks_at([jnp.where(k < limit, acol[k, 0, n] - base, -1) for k in range(KA)], size, jnp.int32)
        for c, tile in enumerate(spread(a_ref[n], masks, count * size)):
            spot = slice(c * WIDE, (c + 1) * WIDE)
            high = tile.astype(BF16)
            high_ref[at, spot] = high
            low_ref[at, spot] = (tile - high.astype(F32)).astype(BF16)
    cols = in_ref[count * size :, :].astype(F32)
    for n in range(count):
        at = slice(n * size, (n + 1) * size)
        masks = masks_at([cols[n * slots + j : n * slots + j + 1, :] for j in range(slots)], size, F32)
        for c, tile in enumerate(spread(in_ref[at, :], masks, width)):
            ext_ref[at, c * WIDE : (c + 1) * WIDE] = tile.astype(BF16)
    ext = ext_ref[...]
    step = prod_ref.shape[0] // 2
    for m in range(2):
        at = slice(m * step, (m + 1) * step)
        value = jnp.dot(high_ref[at, :], ext, preferred_element_type=F32)
        value += jnp.dot(low_ref[at, :], ext, preferred_element_type=F32)
        prod_ref[at, :] = value.astype(BF16)
    finish(ownt_ref, prod_ref[...], keep_ref, send_ref)


def fold_kernel(stage, keep_ref, recv_ref, *refs):
    next_ref, send_ref = refs[-2:]
    bit = (lax.axis_index("gy") >> stage) % 2
    for i in range(next_ref.shape[0]):
        mine, other = 2 * i + bit, 2 * i + 1 - bit
        send_ref[i] = (keep_ref[other] + recv_ref[other].astype(F32)).astype(BF16)
        next_ref[i] = keep_ref[mine] + recv_ref[mine].astype(F32)


def write_kernel(order, keep_ref, recv_ref, *refs):
    out_ref, sum_ref, sem = refs[-3:]
    odd = lax.axis_index("gx") % 2
    third = 1 if order is None else 2 * odd if order else 2 - 2 * odd
    width = sum_ref.shape[1]
    sum_ref[...] = keep_ref[0] + recv_ref[0].astype(F32)
    spot = pl.ds(pl.multiple_of(third * width, width), width)
    copy = pltpu.make_async_copy(sum_ref, out_ref.at[:, spot], sem)
    copy.start()
    copy.wait()


def gate_kernel(recv_ref, token_ref):
    token_ref[...] = jnp.zeros(token_ref.shape, F32)


def swapped(value, axis, step):
    length = lax.axis_size(axis)
    return lax.ppermute(value, axis, [(i, i ^ step) for i in range(length) if i ^ step < length])


def folded(keep, send, parts, after=()):
    left, share, width = keep.shape
    stage = 0
    while left > 1:
        recv = swapped(send, "gy", 1 << stage)
        stage += 1
        left //= 2
        keep, send = pl.pallas_call(
            functools.partial(fold_kernel, stage),
            out_shape=(
                jax.ShapeDtypeStruct((left, share, width), F32),
                jax.ShapeDtypeStruct((left, share, width), BF16),
            ),
            in_specs=[VMEM] * (2 + len(after)),
            out_specs=(VMEM, VMEM),
            compiler_params=PARAMS,
            name="fold",
        )(keep, recv, *after)
        after = ()
    return keep, swapped(send, "gy", 1 << stage), keep


def written(order, keep, recv, result):
    share, width = keep.shape[1:]
    start = order is None
    whole = jax.ShapeDtypeStruct((share, 3 * width), F32)
    return pl.pallas_call(
        functools.partial(write_kernel, order),
        out_shape=whole,
        in_specs=[VMEM, VMEM] if start else [VMEM, VMEM, HBM],
        out_specs=HBM,
        input_output_aliases={} if start else {2: 0},
        scratch_shapes=[pltpu.VMEM((share, width), F32), pltpu.SemaphoreType.DMA],
        compiler_params=PARAMS,
        cost_estimate=SHORT,
        name="write",
    )(keep, recv, *([] if start else [result]))


def body(a_blocks, a_cols, mushy, p_blocks, p_cols, send_rows):
    rows, size, inner = p_blocks.shape[1:]
    acol, pcol = a_cols.transpose(2, 0, 1), p_cols[0].T
    mush, sends = mushy[0], send_rows[0]
    ablk, pblk = a_blocks[0], p_blocks[0]
    count = sends.shape[0] // 2
    width = NCOL * size
    length = lax.axis_size("gx")
    parts = lax.axis_size("gy")
    share = width // parts

    tail = -(-count * pcol.shape[0] // 16) * 16
    packed = jax.ShapeDtypeStruct((count * size + tail, inner), BF16)

    first, second, mush = pl.pallas_call(
        pack_kernel,
        out_shape=(packed, packed, jax.ShapeDtypeStruct(mush.shape, mush.dtype)),
        in_specs=[HBM] * 4,
        out_specs=(HBM, HBM, HBM),
        scratch_shapes=[
            pltpu.SMEM(sends.shape, sends.dtype),
            pltpu.SMEM(pcol.shape, pcol.dtype),
            pltpu.VMEM(pblk.shape, BF16),
            pltpu.VMEM((2,) + packed.shape, BF16),
            pltpu.SemaphoreType.DMA((4,)),
        ],
        compiler_params=pltpu.CompilerParams(vmem_limit_bytes=56 * 1024 * 1024),
        cost_estimate=LONG,
        name="pack",
    )(sends, pcol, mush, pblk)
    even = [(i, i + 1) for i in range(0, length - 1, 2)]
    uneven = [(i, i + 1) for i in range(1, length - 1, 2)]
    first = lax.ppermute(first, "gx", even + [(j, i) for i, j in even])
    second = lax.ppermute(second, "gx", uneven + [(j, i) for i, j in uneven])

    partial = (
        jax.ShapeDtypeStruct((parts // 2, share, width), F32),
        jax.ShapeDtypeStruct((parts // 2, share, width), BF16),
    )
    own_t, keep, send = pl.pallas_call(
        functools.partial(own_kernel, parts),
        out_shape=(jax.ShapeDtypeStruct((width, rows * size), BF16),) + partial,
        in_specs=[SMEM, SMEM, SMEM, VMEM, VMEM],
        out_specs=(VMEM, VMEM, VMEM),
        scratch_shapes=[
            pltpu.VMEM((rows + 1, size, width), BF16),
            pltpu.VMEM((rows * size, width), BF16),
        ],
        compiler_params=PARAMS,
        cost_estimate=MEDIUM,
        name="own",
    )(acol, mush, pcol, ablk, pblk)
    keep, recv, folds = folded(keep, send, parts)
    pieces = []
    for order, ghosts in enumerate((first, second)):
        after = [folds] if order else []
        pieces.append(
            pl.pallas_call(
                functools.partial(ghost_kernel, order),
                out_shape=partial,
                in_specs=[SMEM, SMEM] + [VMEM] * (3 + len(after)),
                out_specs=(VMEM, VMEM),
                scratch_shapes=[
                    pltpu.VMEM((rows * size, count * size), BF16),
                    pltpu.VMEM((rows * size, count * size), BF16),
                    pltpu.VMEM((count * size, width), BF16),
                    pltpu.VMEM((rows * size, width), BF16),
                ],
                compiler_params=PARAMS,
                cost_estimate=LONG,
                name="ghost",
            )(acol, mush, ablk, ghosts, own_t, *after)
        )
    token = pl.pallas_call(
        gate_kernel,
        out_shape=jax.ShapeDtypeStruct((8, LANES), F32),
        in_specs=[HBM],
        out_specs=VMEM,
        compiler_params=PARAMS,
        cost_estimate=LONG,
        name="gate",
    )(recv)
    sides = [folded(*pieces[0], parts), folded(*pieces[1], parts, (token,))]
    result = written(None, keep, recv, None)
    for order, (keep, recv, folds) in enumerate(sides):
        result = written(order, keep, recv, result)
    return result[None]


def solution(mesh):
    placed = (
        P("gx", "gy", None, None),
        P("gx", "gy", None),
        P("gx", "gy"),
        P("gx", "gy", None, None),
        P("gx", "gy", None),
        P("gx", "gy"),
    )
    return jax.shard_map(
        body, mesh=mesh, in_specs=placed, out_specs=P("gx", "gy", None), check_vma=False
    )
```

```python
import functools

import jax
import jax.numpy as jnp
from jax import lax
from jax.experimental import pallas as pl
from jax.experimental.pallas import tpu as pltpu
from jax.sharding import PartitionSpec as P

KA = 7
KS = 3
INFO = 128
NCOL = 8
LANES = 128
WIDE = 256

F32 = jnp.float32
BF16 = jnp.bfloat16
SMEM = pl.BlockSpec(memory_space=pltpu.SMEM)
VMEM = pl.BlockSpec(memory_space=pltpu.VMEM)
HBM = pl.BlockSpec(memory_space=pltpu.HBM)
LONG = pl.CostEstimate(flops=10000000000, bytes_accessed=1000000, transcendentals=0)
MEDIUM = pl.CostEstimate(flops=1000000000, bytes_accessed=1000000, transcendentals=0)
SHORT = pl.CostEstimate(flops=100000000, bytes_accessed=1000000, transcendentals=0)
PARAMS = pltpu.CompilerParams(vmem_limit_bytes=24 * 1024 * 1024)


def spread(value, masks_of, width):
    size = value.shape[0]
    row = lax.broadcasted_iota(jnp.int32, (size, WIDE), 0)
    lane = lax.broadcasted_iota(jnp.int32, (size, WIDE), 1)
    unit = jnp.where(row == lane % size, 1.0, 0.0).astype(BF16)
    tiles = []
    for c in range(width // WIDE):
        moves = jnp.concatenate([unit * mask for mask in masks_of(c * WIDE // size)], axis=0)
        tiles.append(jnp.dot(value, moves, preferred_element_type=F32))
    return tiles


def masks_at(cols, size, dtype):
    slots = (lax.broadcasted_iota(jnp.int32, (1, WIDE), 1) // size).astype(dtype)
    return lambda first: [
        jnp.where(slots == col - first, 1.0, 0.0).astype(BF16) for col in cols
    ]


def multiply(info, a_ref, base, ext_ref, prod_ref):
    rows, size = a_ref.shape[0], a_ref.shape[1]
    ext_ref[ext_ref.shape[0] - 1] = jnp.zeros(ext_ref.shape[1:], BF16)
    none = ext_ref.shape[0] - 1
    for n in range(rows):
        picks = []
        for k in range(KA):
            spot = info[n * INFO + k] - base
            good = (spot >= 0) & (spot < none)
            picks.append(jnp.where(good, spot, none))
        picked = jnp.concatenate([ext_ref[spot] for spot in picks], axis=0)
        value = jnp.dot(a_ref[n], picked, preferred_element_type=F32)
        prod_ref[n * size : (n + 1) * size, :] = value.astype(BF16)


def finish(ownt_ref, prod, keep_ref, send_ref):
    rows = ownt_ref.shape[0] // 2
    sent = jnp.dot(ownt_ref[rows:, :], prod, preferred_element_type=F32)
    send_ref[...] = sent.astype(BF16).reshape(send_ref.shape)
    kept = jnp.dot(ownt_ref[:rows, :], prod, preferred_element_type=F32)
    keep_ref[...] = kept.reshape(keep_ref.shape)


def pack_kernel(
    sends_in, pcol_in, acol_in, mush_in, p_in, first_ref, second_ref, info_out,
    sends, pcol, acol, mush, info, p_ref, packed_ref, sems,
):
    copies = [
        pltpu.make_async_copy(src, dst, sems.at[i])
        for i, (src, dst) in enumerate(
            ((sends_in, sends), (pcol_in, pcol), (acol_in, acol), (mush_in, mush), (p_in, p_ref))
        )
    ]
    for copy in copies:
        copy.start()
    for copy in copies[:4]:
        copy.wait()
    odd = lax.axis_index("gx") % 2
    rows, size = p_ref.shape[0], p_ref.shape[1]
    count = sends.shape[0] // 2
    slots = pcol.shape[0]
    for n in range(rows):
        limit = jnp.where(mush[n] > 0, KA, KS)
        for k in range(KA):
            info[n * INFO + k] = jnp.where(k < limit, acol[k, 0, n], -1)
        for j in range(slots):
            info[n * INFO + KA + j] = pcol[j, n]
    passed = pltpu.make_async_copy(info, info_out, sems.at[0])
    passed.start()
    starts = ((1 - odd) * count, odd * count)
    tail = packed_ref.shape[1] - count * size
    which = lax.broadcasted_iota(jnp.int32, (tail, packed_ref.shape[2]), 0)
    for i, start in enumerate(starts):
        cols = jnp.zeros(which.shape, F32)
        for s in range(count):
            row = sends[start + s]
            for j in range(slots):
                cols = jnp.where(which == s * slots + j, pcol[j, row].astype(F32), cols)
        packed_ref[i, count * size :, :] = cols.astype(BF16)
    copies[4].wait()
    copies = [passed]
    for i, (out_ref, start) in enumerate(zip((first_ref, second_ref), starts)):
        for s in range(count):
            packed_ref[i, s * size : (s + 1) * size, :] = p_ref[sends[start + s]]
        copies.append(pltpu.make_async_copy(packed_ref.at[i], out_ref, sems.at[1 + i]))
        copies[-1].start()
    for copy in copies:
        copy.wait()


def own_kernel(parts, info, a_ref, p_ref, ownt_ref, keep_ref, send_ref, own_ref, prod_ref):
    bit = lax.axis_index("gy") % 2
    rows, size = p_ref.shape[0], p_ref.shape[1]
    width = NCOL * size
    share = width // parts
    for n in range(rows):
        cols = [info[n * INFO + KA + j] for j in range(p_ref.shape[2] // size)]
        masks = masks_at(cols, size, jnp.int32)
        for c, tile in enumerate(spread(p_ref[n], masks, width)):
            own_ref[n, :, c * WIDE : (c + 1) * WIDE] = tile.astype(BF16)
    for c in range(width // LANES):
        column = own_ref[:rows, :, c * LANES : (c + 1) * LANES]
        flipped = column.reshape(rows * size, LANES).T
        for k in range(LANES // share):
            part = c * (LANES // share) + k
            spot = part // 2 + jnp.where(part % 2 == bit, 0, parts // 2)
            at = pl.ds(pl.multiple_of(spot * share, share), share)
            ownt_ref[at, :] = flipped[k * share : (k + 1) * share, :]
    multiply(info, a_ref, 0, own_ref, prod_ref)
    finish(ownt_ref, prod_ref[...], keep_ref, send_ref)


def ghost_kernel(order, info, a_ref, in_ref, ownt_ref, *refs):
    keep_ref, send_ref, high_ref, low_ref, ext_ref, prod_ref = refs[-6:]
    odd = lax.axis_index("gx") % 2
    right = odd if order else 1 - odd
    rows, size = a_ref.shape[0], a_ref.shape[1]
    width = ownt_ref.shape[0]
    slots = in_ref.shape[1] // size
    count = ext_ref.shape[0] // size
    base = rows + right * count
    for n in range(rows):
        at = slice(n * size, (n + 1) * size)
        masks = masks_at([info[n * INFO + k] - base for k in range(KA)], size, jnp.int32)
        for c, tile in enumerate(spread(a_ref[n], masks, count * size)):
            spot = slice(c * WIDE, (c + 1) * WIDE)
            high = tile.astype(BF16)
            high_ref[at, spot] = high
            low_ref[at, spot] = (tile - high.astype(F32)).astype(BF16)
    cols = in_ref[count * size :, :].astype(F32)
    for n in range(count):
        at = slice(n * size, (n + 1) * size)
        masks = masks_at([cols[n * slots + j : n * slots + j + 1, :] for j in range(slots)], size, F32)
        for c, tile in enumerate(spread(in_ref[at, :], masks, width)):
            ext_ref[at, c * WIDE : (c + 1) * WIDE] = tile.astype(BF16)
    ext = ext_ref[...]
    step = prod_ref.shape[0] // 2
    for m in range(2):
        at = slice(m * step, (m + 1) * step)
        value = jnp.dot(high_ref[at, :], ext, preferred_element_type=F32)
        value += jnp.dot(low_ref[at, :], ext, preferred_element_type=F32)
        prod_ref[at, :] = value.astype(BF16)
    finish(ownt_ref, prod_ref[...], keep_ref, send_ref)


def fold_kernel(stage, keep_ref, recv_ref, *refs):
    next_ref, send_ref = refs[-2:]
    bit = (lax.axis_index("gy") >> stage) % 2
    for i in range(next_ref.shape[0]):
        mine, other = 2 * i + bit, 2 * i + 1 - bit
        send_ref[i] = (keep_ref[other] + recv_ref[other].astype(F32)).astype(BF16)
        next_ref[i] = keep_ref[mine] + recv_ref[mine].astype(F32)


def write_kernel(order, keep_ref, recv_ref, *refs):
    out_ref, sum_ref, sem = refs[-3:]
    odd = lax.axis_index("gx") % 2
    third = 1 if order is None else 2 * odd if order else 2 - 2 * odd
    width = sum_ref.shape[1]
    sum_ref[...] = keep_ref[0] + recv_ref[0].astype(F32)
    spot = pl.ds(pl.multiple_of(third * width, width), width)
    copy = pltpu.make_async_copy(sum_ref, out_ref.at[:, spot], sem)
    copy.start()
    copy.wait()


def gate_kernel(recv_ref, token_ref):
    token_ref[...] = jnp.zeros(token_ref.shape, F32)


def swapped(value, axis, step):
    length = lax.axis_size(axis)
    return lax.ppermute(value, axis, [(i, i ^ step) for i in range(length) if i ^ step < length])


def folded(keep, send, parts, after=()):
    left, share, width = keep.shape
    stage = 0
    while left > 1:
        recv = swapped(send, "gy", 1 << stage)
        stage += 1
        left //= 2
        keep, send = pl.pallas_call(
            functools.partial(fold_kernel, stage),
            out_shape=(
                jax.ShapeDtypeStruct((left, share, width), F32),
                jax.ShapeDtypeStruct((left, share, width), BF16),
            ),
            in_specs=[VMEM] * (2 + len(after)),
            out_specs=(VMEM, VMEM),
            compiler_params=PARAMS,
            name="fold",
        )(keep, recv, *after)
        after = ()
    return keep, swapped(send, "gy", 1 << stage), keep


def written(order, keep, recv, result):
    share, width = keep.shape[1:]
    start = order is None
    whole = jax.ShapeDtypeStruct((share, 3 * width), F32)
    return pl.pallas_call(
        functools.partial(write_kernel, order),
        out_shape=whole,
        in_specs=[VMEM, VMEM] if start else [VMEM, VMEM, HBM],
        out_specs=HBM,
        input_output_aliases={} if start else {2: 0},
        scratch_shapes=[pltpu.VMEM((share, width), F32), pltpu.SemaphoreType.DMA],
        compiler_params=PARAMS,
        cost_estimate=SHORT,
        name="write",
    )(keep, recv, *([] if start else [result]))


def body(a_blocks, a_cols, mushy, p_blocks, p_cols, send_rows):
    rows, size, inner = p_blocks.shape[1:]
    acol, pcol = a_cols.transpose(2, 0, 1), p_cols[0].T
    mush, sends = mushy[0], send_rows[0]
    ablk, pblk = a_blocks[0], p_blocks[0]
    count = sends.shape[0] // 2
    width = NCOL * size
    length = lax.axis_size("gx")
    parts = lax.axis_size("gy")
    share = width // parts

    tail = -(-count * pcol.shape[0] // 16) * 16
    packed = jax.ShapeDtypeStruct((count * size + tail, inner), BF16)

    first, second, info = pl.pallas_call(
        pack_kernel,
        out_shape=(packed, packed, jax.ShapeDtypeStruct((rows * INFO,), jnp.int32)),
        in_specs=[HBM] * 5,
        out_specs=(HBM, HBM, HBM),
        scratch_shapes=[
            pltpu.SMEM(sends.shape, sends.dtype),
            pltpu.SMEM(pcol.shape, pcol.dtype),
            pltpu.SMEM(acol.shape, acol.dtype),
            pltpu.SMEM(mush.shape, mush.dtype),
            pltpu.SMEM((rows * INFO,), jnp.int32),
            pltpu.VMEM(pblk.shape, BF16),
            pltpu.VMEM((2,) + packed.shape, BF16),
            pltpu.SemaphoreType.DMA((5,)),
        ],
        compiler_params=pltpu.CompilerParams(vmem_limit_bytes=56 * 1024 * 1024),
        cost_estimate=LONG,
        name="pack",
    )(sends, pcol, acol, mush, pblk)
    even = [(i, i + 1) for i in range(0, length - 1, 2)]
    uneven = [(i, i + 1) for i in range(1, length - 1, 2)]
    first = lax.ppermute(first, "gx", even + [(j, i) for i, j in even])
    second = lax.ppermute(second, "gx", uneven + [(j, i) for i, j in uneven])

    partial = (
        jax.ShapeDtypeStruct((parts // 2, share, width), F32),
        jax.ShapeDtypeStruct((parts // 2, share, width), BF16),
    )
    own_t, keep, send = pl.pallas_call(
        functools.partial(own_kernel, parts),
        out_shape=(jax.ShapeDtypeStruct((width, rows * size), BF16),) + partial,
        in_specs=[SMEM, VMEM, VMEM],
        out_specs=(VMEM, VMEM, VMEM),
        scratch_shapes=[
            pltpu.VMEM((rows + 1, size, width), BF16),
            pltpu.VMEM((rows * size, width), BF16),
        ],
        compiler_params=PARAMS,
        cost_estimate=MEDIUM,
        name="own",
    )(info, ablk, pblk)
    keep, recv, folds = folded(keep, send, parts)
    pieces = []
    for order, ghosts in enumerate((first, second)):
        after = [folds] if order else []
        pieces.append(
            pl.pallas_call(
                functools.partial(ghost_kernel, order),
                out_shape=partial,
                in_specs=[SMEM] + [VMEM] * (3 + len(after)),
                out_specs=(VMEM, VMEM),
                scratch_shapes=[
                    pltpu.VMEM((rows * size, count * size), BF16),
                    pltpu.VMEM((rows * size, count * size), BF16),
                    pltpu.VMEM((count * size, width), BF16),
                    pltpu.VMEM((rows * size, width), BF16),
                ],
                compiler_params=PARAMS,
                cost_estimate=LONG,
                name="ghost",
            )(info, ablk, ghosts, own_t, *after)
        )
    token = pl.pallas_call(
        gate_kernel,
        out_shape=jax.ShapeDtypeStruct((8, LANES), F32),
        in_specs=[HBM],
        out_specs=VMEM,
        compiler_params=PARAMS,
        cost_estimate=LONG,
        name="gate",
    )(recv)
    sides = [folded(*pieces[0], parts), folded(*pieces[1], parts, (token,))]
    result = written(None, keep, recv, None)
    for order, (keep, recv, folds) in enumerate(sides):
        result = written(order, keep, recv, result)
    return result[None]


def solution(mesh):
    placed = (
        P("gx", "gy", None, None),
        P("gx", "gy", None),
        P("gx", "gy"),
        P("gx", "gy", None, None),
        P("gx", "gy", None),
        P("gx", "gy"),
    )
    return jax.shard_map(
        body, mesh=mesh, in_specs=placed, out_specs=P("gx", "gy", None), check_vma=False
    )
```

```python
import functools

import jax
import jax.numpy as jnp
from jax import lax
from jax.experimental import pallas as pl
from jax.experimental.pallas import tpu as pltpu
from jax.sharding import PartitionSpec as P

KA = 7
KS = 3
INFO = 128
NCOL = 8
LANES = 128
WIDE = 256

F32 = jnp.float32
BF16 = jnp.bfloat16
SMEM = pl.BlockSpec(memory_space=pltpu.SMEM)
VMEM = pl.BlockSpec(memory_space=pltpu.VMEM)
HBM = pl.BlockSpec(memory_space=pltpu.HBM)
LONG = pl.CostEstimate(flops=10000000000, bytes_accessed=1000000, transcendentals=0)
MEDIUM = pl.CostEstimate(flops=1000000000, bytes_accessed=1000000, transcendentals=0)
SHORT = pl.CostEstimate(flops=100000000, bytes_accessed=1000000, transcendentals=0)
PARAMS = pltpu.CompilerParams(vmem_limit_bytes=24 * 1024 * 1024)


def spread(value, masks_of, width):
    size = value.shape[0]
    row = lax.broadcasted_iota(jnp.int32, (size, WIDE), 0)
    lane = lax.broadcasted_iota(jnp.int32, (size, WIDE), 1)
    unit = jnp.where(row == lane % size, 1.0, 0.0).astype(BF16)
    tiles = []
    for c in range(width // WIDE):
        moves = jnp.concatenate([unit * mask for mask in masks_of(c * WIDE // size)], axis=0)
        tiles.append(jnp.dot(value, moves, preferred_element_type=F32))
    return tiles


def masks_at(cols, size, dtype):
    slots = (lax.broadcasted_iota(jnp.int32, (1, WIDE), 1) // size).astype(dtype)
    return lambda first: [
        jnp.where(slots == col - first, 1.0, 0.0).astype(BF16) for col in cols
    ]


def widen(a_ref, wide_ref):
    rows, slots, size = wide_ref.shape[:3]
    low = lax.broadcasted_iota(jnp.int32, (size, LANES), 1) < size
    for n in range(rows):
        for q in range(slots // 2):
            tile = a_ref[n, :, q * LANES : (q + 1) * LANES].astype(F32)
            turned = pltpu.roll(tile, size, 1)
            wide_ref[n, 2 * q] = jnp.where(low, tile, turned).astype(BF16)
            wide_ref[n, 2 * q + 1] = jnp.where(low, turned, tile).astype(BF16)
        if slots % 2:
            last = a_ref[n, :, (slots - 1) * size :].astype(F32)
            wide_ref[n, slots - 1] = jnp.concatenate([last, last], axis=1).astype(BF16)


def scatter(info, wide_ref, base, count, laid_ref):
    rows, slots, size = wide_ref.shape[:3]
    half = lax.broadcasted_iota(jnp.int32, (1, LANES), 1) // size
    laid_ref[...] = jnp.zeros(laid_ref.shape, BF16)
    for n in range(rows):
        cols = [info[n * INFO + k] for k in range(slots)]
        for k in range(slots):
            turn = sum(((cols[i] == cols[k]).astype(jnp.int32) for i in range(k)), 0) % 2
            spot = cols[k] - base
            good = (spot >= 0) & (spot < count)
            tile = jnp.where(good, spot // 2, count // 2)
            mask = jnp.where(half == spot % 2, 1.0, 0.0).astype(BF16)
            at = pl.ds(pl.multiple_of(tile * LANES, LANES), LANES)
            place = (turn, slice(n * size, (n + 1) * size), at)
            laid_ref[place] = laid_ref[place] + wide_ref[n, k] * mask


def multiply(laid_ref, ext, prod_ref):
    step = prod_ref.shape[0] // 2
    inner = ext.shape[0]
    for m in range(2):
        at = slice(m * step, (m + 1) * step)
        value = jnp.dot(laid_ref[0, at, :inner], ext, preferred_element_type=F32)
        value += jnp.dot(laid_ref[1, at, :inner], ext, preferred_element_type=F32)
        prod_ref[at, :] = value.astype(BF16)


def finish(ownt_ref, prod, keep_ref, send_ref):
    rows = ownt_ref.shape[0] // 2
    sent = jnp.dot(ownt_ref[rows:, :], prod, preferred_element_type=F32)
    send_ref[...] = sent.astype(BF16).reshape(send_ref.shape)
    kept = jnp.dot(ownt_ref[:rows, :], prod, preferred_element_type=F32)
    keep_ref[...] = kept.reshape(keep_ref.shape)


def pack_kernel(
    sends_in, pcol_in, acol_in, mush_in, p_in, first_ref, second_ref, info_out,
    sends, pcol, acol, mush, info, p_ref, packed_ref, sems,
):
    copies = [
        pltpu.make_async_copy(src, dst, sems.at[i])
        for i, (src, dst) in enumerate(
            ((sends_in, sends), (pcol_in, pcol), (acol_in, acol), (mush_in, mush), (p_in, p_ref))
        )
    ]
    for copy in copies:
        copy.start()
    for copy in copies[:4]:
        copy.wait()
    odd = lax.axis_index("gx") % 2
    rows, size = p_ref.shape[0], p_ref.shape[1]
    count = sends.shape[0] // 2
    slots = pcol.shape[0]
    for n in range(rows):
        limit = jnp.where(mush[n] > 0, KA, KS)
        for k in range(KA):
            info[n * INFO + k] = jnp.where(k < limit, acol[k, 0, n], -1)
        for j in range(slots):
            info[n * INFO + KA + j] = pcol[j, n]
    passed = pltpu.make_async_copy(info, info_out, sems.at[0])
    passed.start()
    starts = ((1 - odd) * count, odd * count)
    tail = packed_ref.shape[1] - count * size
    which = lax.broadcasted_iota(jnp.int32, (tail, packed_ref.shape[2]), 0)
    for i, start in enumerate(starts):
        cols = jnp.zeros(which.shape, F32)
        for s in range(count):
            row = sends[start + s]
            for j in range(slots):
                cols = jnp.where(which == s * slots + j, pcol[j, row].astype(F32), cols)
        packed_ref[i, count * size :, :] = cols.astype(BF16)
    copies[4].wait()
    copies = [passed]
    for i, (out_ref, start) in enumerate(zip((first_ref, second_ref), starts)):
        for s in range(count):
            packed_ref[i, s * size : (s + 1) * size, :] = p_ref[sends[start + s]]
        copies.append(pltpu.make_async_copy(packed_ref.at[i], out_ref, sems.at[1 + i]))
        copies[-1].start()
    for copy in copies:
        copy.wait()


def own_kernel(parts, info, a_ref, p_ref, ownt_ref, wide_ref, keep_ref, send_ref, own_ref, laid_ref, prod_ref):
    bit = lax.axis_index("gy") % 2
    rows, size = p_ref.shape[0], p_ref.shape[1]
    width = NCOL * size
    share = width // parts
    widen(a_ref, wide_ref)
    for n in range(rows):
        cols = [info[n * INFO + KA + j] for j in range(p_ref.shape[2] // size)]
        masks = masks_at(cols, size, jnp.int32)
        for c, tile in enumerate(spread(p_ref[n], masks, width)):
            own_ref[n * size : (n + 1) * size, c * WIDE : (c + 1) * WIDE] = tile.astype(BF16)
    scatter(info, wide_ref, 0, rows, laid_ref)
    for c in range(width // LANES):
        flipped = own_ref[:, c * LANES : (c + 1) * LANES].T
        for k in range(LANES // share):
            part = c * (LANES // share) + k
            spot = part // 2 + jnp.where(part % 2 == bit, 0, parts // 2)
            at = pl.ds(pl.multiple_of(spot * share, share), share)
            ownt_ref[at, :] = flipped[k * share : (k + 1) * share, :]
    multiply(laid_ref, own_ref[...], prod_ref)
    finish(ownt_ref, prod_ref[...], keep_ref, send_ref)


def ghost_kernel(order, info, wide_ref, in_ref, ownt_ref, *refs):
    keep_ref, send_ref, laid_ref, ext_ref, prod_ref = refs[-5:]
    odd = lax.axis_index("gx") % 2
    right = odd if order else 1 - odd
    rows, size = wide_ref.shape[0], wide_ref.shape[2]
    width = ownt_ref.shape[0]
    slots = in_ref.shape[1] // size
    count = ext_ref.shape[0] // size
    cols = in_ref[count * size :, :].astype(F32)
    for n in range(count):
        at = slice(n * size, (n + 1) * size)
        masks = masks_at([cols[n * slots + j : n * slots + j + 1, :] for j in range(slots)], size, F32)
        for c, tile in enumerate(spread(in_ref[at, :], masks, width)):
            ext_ref[at, c * WIDE : (c + 1) * WIDE] = tile.astype(BF16)
    scatter(info, wide_ref, rows + right * count, count, laid_ref)
    multiply(laid_ref, ext_ref[...], prod_ref)
    finish(ownt_ref, prod_ref[...], keep_ref, send_ref)


def fold_kernel(stage, keep_ref, recv_ref, *refs):
    next_ref, send_ref = refs[-2:]
    bit = (lax.axis_index("gy") >> stage) % 2
    for i in range(next_ref.shape[0]):
        mine, other = 2 * i + bit, 2 * i + 1 - bit
        send_ref[i] = (keep_ref[other] + recv_ref[other].astype(F32)).astype(BF16)
        next_ref[i] = keep_ref[mine] + recv_ref[mine].astype(F32)


def write_kernel(order, keep_ref, recv_ref, *refs):
    out_ref, sum_ref, sem = refs[-3:]
    odd = lax.axis_index("gx") % 2
    third = 1 if order is None else 2 * odd if order else 2 - 2 * odd
    width = sum_ref.shape[1]
    sum_ref[...] = keep_ref[0] + recv_ref[0].astype(F32)
    spot = pl.ds(pl.multiple_of(third * width, width), width)
    copy = pltpu.make_async_copy(sum_ref, out_ref.at[:, spot], sem)
    copy.start()
    copy.wait()


def gate_kernel(recv_ref, token_ref):
    token_ref[...] = jnp.zeros(token_ref.shape, F32)


def swapped(value, axis, step):
    length = lax.axis_size(axis)
    return lax.ppermute(value, axis, [(i, i ^ step) for i in range(length) if i ^ step < length])


def folded(keep, send, parts, after=()):
    left, share, width = keep.shape
    stage = 0
    while left > 1:
        recv = swapped(send, "gy", 1 << stage)
        stage += 1
        left //= 2
        keep, send = pl.pallas_call(
            functools.partial(fold_kernel, stage),
            out_shape=(
                jax.ShapeDtypeStruct((left, share, width), F32),
                jax.ShapeDtypeStruct((left, share, width), BF16),
            ),
            in_specs=[VMEM] * (2 + len(after)),
            out_specs=(VMEM, VMEM),
            compiler_params=PARAMS,
            name="fold",
        )(keep, recv, *after)
        after = ()
    return keep, swapped(send, "gy", 1 << stage), keep


def written(order, keep, recv, result):
    share, width = keep.shape[1:]
    start = order is None
    whole = jax.ShapeDtypeStruct((share, 3 * width), F32)
    return pl.pallas_call(
        functools.partial(write_kernel, order),
        out_shape=whole,
        in_specs=[VMEM, VMEM] if start else [VMEM, VMEM, HBM],
        out_specs=HBM,
        input_output_aliases={} if start else {2: 0},
        scratch_shapes=[pltpu.VMEM((share, width), F32), pltpu.SemaphoreType.DMA],
        compiler_params=PARAMS,
        cost_estimate=SHORT,
        name="write",
    )(keep, recv, *([] if start else [result]))


def body(a_blocks, a_cols, mushy, p_blocks, p_cols, send_rows):
    rows, size, inner = p_blocks.shape[1:]
    acol, pcol = a_cols.transpose(2, 0, 1), p_cols[0].T
    mush, sends = mushy[0], send_rows[0]
    ablk, pblk = a_blocks[0], p_blocks[0]
    count = sends.shape[0] // 2
    width = NCOL * size
    length = lax.axis_size("gx")
    parts = lax.axis_size("gy")
    share = width // parts

    tail = -(-count * pcol.shape[0] // 16) * 16
    packed = jax.ShapeDtypeStruct((count * size + tail, inner), BF16)

    first, second, info = pl.pallas_call(
        pack_kernel,
        out_shape=(packed, packed, jax.ShapeDtypeStruct((rows * INFO,), jnp.int32)),
        in_specs=[HBM] * 5,
        out_specs=(HBM, HBM, HBM),
        scratch_shapes=[
            pltpu.SMEM(sends.shape, sends.dtype),
            pltpu.SMEM(pcol.shape, pcol.dtype),
            pltpu.SMEM(acol.shape, acol.dtype),
            pltpu.SMEM(mush.shape, mush.dtype),
            pltpu.SMEM((rows * INFO,), jnp.int32),
            pltpu.VMEM(pblk.shape, BF16),
            pltpu.VMEM((2,) + packed.shape, BF16),
            pltpu.SemaphoreType.DMA((5,)),
        ],
        compiler_params=pltpu.CompilerParams(vmem_limit_bytes=56 * 1024 * 1024),
        cost_estimate=LONG,
        name="pack",
    )(sends, pcol, acol, mush, pblk)
    even = [(i, i + 1) for i in range(0, length - 1, 2)]
    uneven = [(i, i + 1) for i in range(1, length - 1, 2)]
    first = lax.ppermute(first, "gx", even + [(j, i) for i, j in even])
    second = lax.ppermute(second, "gx", uneven + [(j, i) for i, j in uneven])

    partial = (
        jax.ShapeDtypeStruct((parts // 2, share, width), F32),
        jax.ShapeDtypeStruct((parts // 2, share, width), BF16),
    )
    own_t, wide, keep, send = pl.pallas_call(
        functools.partial(own_kernel, parts),
        out_shape=(
            jax.ShapeDtypeStruct((width, rows * size), BF16),
            jax.ShapeDtypeStruct((rows, KA, size, LANES), BF16),
        )
        + partial,
        in_specs=[SMEM, VMEM, VMEM],
        out_specs=(VMEM, VMEM, VMEM, VMEM),
        scratch_shapes=[
            pltpu.VMEM((rows * size, width), BF16),
            pltpu.VMEM((2, rows * size, rows * size + LANES), BF16),
            pltpu.VMEM((rows * size, width), BF16),
        ],
        compiler_params=PARAMS,
        cost_estimate=MEDIUM,
        name="own",
    )(info, ablk, pblk)
    keep, recv, folds = folded(keep, send, parts)
    pieces = []
    for order, ghosts in enumerate((first, second)):
        after = [folds] if order else []
        pieces.append(
            pl.pallas_call(
                functools.partial(ghost_kernel, order),
                out_shape=partial,
                in_specs=[SMEM] + [VMEM] * (3 + len(after)),
                out_specs=(VMEM, VMEM),
                scratch_shapes=[
                    pltpu.VMEM((2, rows * size, count * size + LANES), BF16),
                    pltpu.VMEM((count * size, width), BF16),
                    pltpu.VMEM((rows * size, width), BF16),
                ],
                compiler_params=PARAMS,
                cost_estimate=LONG,
                name="ghost",
            )(info, wide, ghosts, own_t, *after)
        )
    token = pl.pallas_call(
        gate_kernel,
        out_shape=jax.ShapeDtypeStruct((8, LANES), F32),
        in_specs=[HBM],
        out_specs=VMEM,
        compiler_params=PARAMS,
        cost_estimate=LONG,
        name="gate",
    )(recv)
    sides = [folded(*pieces[0], parts), folded(*pieces[1], parts, (token,))]
    result = written(None, keep, recv, None)
    for order, (keep, recv, folds) in enumerate(sides):
        result = written(order, keep, recv, result)
    return result[None]


def solution(mesh):
    placed = (
        P("gx", "gy", None, None),
        P("gx", "gy", None),
        P("gx", "gy"),
        P("gx", "gy", None, None),
        P("gx", "gy", None),
        P("gx", "gy"),
    )
    return jax.shard_map(
        body, mesh=mesh, in_specs=placed, out_specs=P("gx", "gy", None), check_vma=False
    )
```

```python
import functools

import jax
import jax.numpy as jnp
from jax import lax
from jax.experimental import pallas as pl
from jax.experimental.pallas import tpu as pltpu
from jax.sharding import PartitionSpec as P

KA = 7
KS = 3
INFO = 128
NCOL = 8
LANES = 128
WIDE = 256

F32 = jnp.float32
BF16 = jnp.bfloat16
SMEM = pl.BlockSpec(memory_space=pltpu.SMEM)
VMEM = pl.BlockSpec(memory_space=pltpu.VMEM)
HBM = pl.BlockSpec(memory_space=pltpu.HBM)
LONG = pl.CostEstimate(flops=10000000000, bytes_accessed=1000000, transcendentals=0)
MEDIUM = pl.CostEstimate(flops=1000000000, bytes_accessed=1000000, transcendentals=0)
SHORT = pl.CostEstimate(flops=100000000, bytes_accessed=1000000, transcendentals=0)
TINY = pl.CostEstimate(flops=1000000, bytes_accessed=1000000, transcendentals=0)
PARAMS = pltpu.CompilerParams(vmem_limit_bytes=24 * 1024 * 1024)


def spread(value, masks_of, width):
    size = value.shape[0]
    row = lax.broadcasted_iota(jnp.int32, (size, WIDE), 0)
    lane = lax.broadcasted_iota(jnp.int32, (size, WIDE), 1)
    unit = jnp.where(row == lane % size, 1.0, 0.0).astype(BF16)
    tiles = []
    for c in range(width // WIDE):
        moves = jnp.concatenate([unit * mask for mask in masks_of(c * WIDE // size)], axis=0)
        tiles.append(jnp.dot(value, moves, preferred_element_type=F32))
    return tiles


def masks_at(cols, size, dtype):
    slots = (lax.broadcasted_iota(jnp.int32, (1, WIDE), 1) // size).astype(dtype)
    return lambda first: [
        jnp.where(slots == col - first, 1.0, 0.0).astype(BF16) for col in cols
    ]


def multiply(info, a_ref, base, ext_ref, prod_ref):
    rows, size = a_ref.shape[0], a_ref.shape[1]
    ext_ref[ext_ref.shape[0] - 1] = jnp.zeros(ext_ref.shape[1:], BF16)
    none = ext_ref.shape[0] - 1
    for n in range(rows):
        picks = []
        for k in range(KA):
            spot = info[n * INFO + k] - base
            good = (spot >= 0) & (spot < none)
            picks.append(jnp.where(good, spot, none))
        picked = jnp.concatenate([ext_ref[spot] for spot in picks], axis=0)
        value = jnp.dot(a_ref[n], picked, preferred_element_type=F32)
        prod_ref[n * size : (n + 1) * size, :] = value.astype(BF16)


def finish(ownt_ref, prod, keep_ref, send_ref):
    rows = ownt_ref.shape[0] // 2
    sent = jnp.dot(ownt_ref[rows:, :], prod, preferred_element_type=F32)
    send_ref[...] = sent.astype(BF16).reshape(send_ref.shape)
    kept = jnp.dot(ownt_ref[:rows, :], prod, preferred_element_type=F32)
    keep_ref[...] = kept.reshape(keep_ref.shape)


def pack_kernel(
    sends_in, pcol_in, acol_in, mush_in, p_in, first_ref, second_ref, info_out,
    sends, pcol, acol, mush, info, p_ref, packed_ref, sems,
):
    copies = [
        pltpu.make_async_copy(src, dst, sems.at[i])
        for i, (src, dst) in enumerate(
            ((sends_in, sends), (pcol_in, pcol), (acol_in, acol), (mush_in, mush), (p_in, p_ref))
        )
    ]
    for copy in copies:
        copy.start()
    for copy in copies[:4]:
        copy.wait()
    odd = lax.axis_index("gx") % 2
    rows, size = p_ref.shape[0], p_ref.shape[1]
    count = sends.shape[0] // 2
    slots = pcol.shape[0]
    for n in range(rows):
        limit = jnp.where(mush[n] > 0, KA, KS)
        for k in range(KA):
            info[n * INFO + k] = jnp.where(k < limit, acol[k, 0, n], -1)
        for j in range(slots):
            info[n * INFO + KA + j] = pcol[j, n]
    passed = pltpu.make_async_copy(info, info_out, sems.at[0])
    passed.start()
    starts = ((1 - odd) * count, odd * count)
    tail = packed_ref.shape[1] - count * size
    which = lax.broadcasted_iota(jnp.int32, (tail, packed_ref.shape[2]), 0)
    for i, start in enumerate(starts):
        cols = jnp.zeros(which.shape, F32)
        for s in range(count):
            row = sends[start + s]
            for j in range(slots):
                cols = jnp.where(which == s * slots + j, pcol[j, row].astype(F32), cols)
        packed_ref[i, count * size :, :] = cols.astype(BF16)
    copies[4].wait()
    copies = [passed]
    for i, (out_ref, start) in enumerate(zip((first_ref, second_ref), starts)):
        for s in range(count):
            packed_ref[i, s * size : (s + 1) * size, :] = p_ref[sends[start + s]]
        copies.append(pltpu.make_async_copy(packed_ref.at[i], out_ref, sems.at[1 + i]))
        copies[-1].start()
    for copy in copies:
        copy.wait()


def own_kernel(parts, info, a_ref, p_ref, ownt_ref, keep_ref, send_ref, own_ref, prod_ref):
    bit = lax.axis_index("gy") % 2
    rows, size = p_ref.shape[0], p_ref.shape[1]
    width = NCOL * size
    share = width // parts
    for n in range(rows):
        cols = [info[n * INFO + KA + j] for j in range(p_ref.shape[2] // size)]
        masks = masks_at(cols, size, jnp.int32)
        for c, tile in enumerate(spread(p_ref[n], masks, width)):
            own_ref[n, :, c * WIDE : (c + 1) * WIDE] = tile.astype(BF16)
    for c in range(width // LANES):
        column = own_ref[:rows, :, c * LANES : (c + 1) * LANES]
        flipped = column.reshape(rows * size, LANES).T
        for k in range(LANES // share):
            part = c * (LANES // share) + k
            spot = part // 2 + jnp.where(part % 2 == bit, 0, parts // 2)
            at = pl.ds(pl.multiple_of(spot * share, share), share)
            ownt_ref[at, :] = flipped[k * share : (k + 1) * share, :]
    multiply(info, a_ref, 0, own_ref, prod_ref)
    finish(ownt_ref, prod_ref[...], keep_ref, send_ref)


def scatter_kernel(when, info, a_ref, passed, *refs):
    high_ref, low_ref = refs[-3:-1] if when else refs[-2:]
    odd = lax.axis_index("gx") % 2
    rows, size = a_ref.shape[0], a_ref.shape[1]
    width = high_ref.shape[2]

    @pl.when(odd == when)
    def _():
        for n in range(rows):
            at = slice(n * size, (n + 1) * size)
            for order in range(2):
                right = odd if order else 1 - odd
                base = rows + right * (width // size)
                masks = masks_at([info[n * INFO + k] - base for k in range(KA)], size, jnp.int32)
                for c, tile in enumerate(spread(a_ref[n], masks, width)):
                    spot = slice(c * WIDE, (c + 1) * WIDE)
                    high = tile.astype(BF16)
                    high_ref[order, at, spot] = high
                    low_ref[order, at, spot] = (tile - high.astype(F32)).astype(BF16)


def ghost_kernel(order, high_ref, low_ref, in_ref, ownt_ref, *refs):
    keep_ref, send_ref, ext_ref, prod_ref = refs[-4:]
    width = ownt_ref.shape[0]
    size = width // NCOL
    slots = in_ref.shape[1] // size
    count = ext_ref.shape[0] // size
    cols = in_ref[count * size :, :].astype(F32)
    for n in range(count):
        at = slice(n * size, (n + 1) * size)
        masks = masks_at([cols[n * slots + j : n * slots + j + 1, :] for j in range(slots)], size, F32)
        for c, tile in enumerate(spread(in_ref[at, :], masks, width)):
            ext_ref[at, c * WIDE : (c + 1) * WIDE] = tile.astype(BF16)
    ext = ext_ref[...]
    step = prod_ref.shape[0] // 2
    for m in range(2):
        at = slice(m * step, (m + 1) * step)
        value = jnp.dot(high_ref[order, at, :], ext, preferred_element_type=F32)
        value += jnp.dot(low_ref[order, at, :], ext, preferred_element_type=F32)
        prod_ref[at, :] = value.astype(BF16)
    finish(ownt_ref, prod_ref[...], keep_ref, send_ref)


def fold_kernel(stage, keep_ref, recv_ref, *refs):
    next_ref, send_ref = refs[-2:]
    bit = (lax.axis_index("gy") >> stage) % 2
    for i in range(next_ref.shape[0]):
        mine, other = 2 * i + bit, 2 * i + 1 - bit
        send_ref[i] = (keep_ref[other] + recv_ref[other].astype(F32)).astype(BF16)
        next_ref[i] = keep_ref[mine] + recv_ref[mine].astype(F32)


def write_kernel(order, keep_ref, recv_ref, *refs):
    out_ref, sum_ref, sem = refs[-3:]
    odd = lax.axis_index("gx") % 2
    third = 1 if order is None else 2 * odd if order else 2 - 2 * odd
    width = sum_ref.shape[1]
    sum_ref[...] = keep_ref[0] + recv_ref[0].astype(F32)
    spot = pl.ds(pl.multiple_of(third * width, width), width)
    copy = pltpu.make_async_copy(sum_ref, out_ref.at[:, spot], sem)
    copy.start()
    copy.wait()


def gate_kernel(recv_ref, token_ref):
    token_ref[...] = jnp.zeros(token_ref.shape, F32)


def swapped(value, axis, step):
    length = lax.axis_size(axis)
    return lax.ppermute(value, axis, [(i, i ^ step) for i in range(length) if i ^ step < length])


def folded(keep, send, parts, after=()):
    left, share, width = keep.shape
    stage = 0
    while left > 1:
        recv = swapped(send, "gy", 1 << stage)
        stage += 1
        left //= 2
        keep, send = pl.pallas_call(
            functools.partial(fold_kernel, stage),
            out_shape=(
                jax.ShapeDtypeStruct((left, share, width), F32),
                jax.ShapeDtypeStruct((left, share, width), BF16),
            ),
            in_specs=[VMEM] * (2 + len(after)),
            out_specs=(VMEM, VMEM),
            compiler_params=PARAMS,
            name="fold",
        )(keep, recv, *after)
        after = ()
    return keep, swapped(send, "gy", 1 << stage), keep


def written(order, keep, recv, result):
    share, width = keep.shape[1:]
    start = order is None
    whole = jax.ShapeDtypeStruct((share, 3 * width), F32)
    return pl.pallas_call(
        functools.partial(write_kernel, order),
        out_shape=whole,
        in_specs=[VMEM, VMEM] if start else [VMEM, VMEM, HBM],
        out_specs=HBM,
        input_output_aliases={} if start else {2: 0},
        scratch_shapes=[pltpu.VMEM((share, width), F32), pltpu.SemaphoreType.DMA],
        compiler_params=PARAMS,
        cost_estimate=SHORT,
        name="write",
    )(keep, recv, *([] if start else [result]))


def body(a_blocks, a_cols, mushy, p_blocks, p_cols, send_rows):
    rows, size, inner = p_blocks.shape[1:]
    acol, pcol = a_cols.transpose(2, 0, 1), p_cols[0].T
    mush, sends = mushy[0], send_rows[0]
    ablk, pblk = a_blocks[0], p_blocks[0]
    count = sends.shape[0] // 2
    width = NCOL * size
    length = lax.axis_size("gx")
    parts = lax.axis_size("gy")
    share = width // parts

    tail = -(-count * pcol.shape[0] // 16) * 16
    packed = jax.ShapeDtypeStruct((count * size + tail, inner), BF16)

    first, second, info = pl.pallas_call(
        pack_kernel,
        out_shape=(packed, packed, jax.ShapeDtypeStruct((rows * INFO,), jnp.int32)),
        in_specs=[HBM] * 5,
        out_specs=(HBM, HBM, HBM),
        scratch_shapes=[
            pltpu.SMEM(sends.shape, sends.dtype),
            pltpu.SMEM(pcol.shape, pcol.dtype),
            pltpu.SMEM(acol.shape, acol.dtype),
            pltpu.SMEM(mush.shape, mush.dtype),
            pltpu.SMEM((rows * INFO,), jnp.int32),
            pltpu.VMEM(pblk.shape, BF16),
            pltpu.VMEM((2,) + packed.shape, BF16),
            pltpu.SemaphoreType.DMA((5,)),
        ],
        compiler_params=pltpu.CompilerParams(vmem_limit_bytes=56 * 1024 * 1024),
        cost_estimate=LONG,
        name="pack",
    )(sends, pcol, acol, mush, pblk)
    even = [(i, i + 1) for i in range(0, length - 1, 2)]
    uneven = [(i, i + 1) for i in range(1, length - 1, 2)]
    first = lax.ppermute(first, "gx", even + [(j, i) for i, j in even])
    split = jax.ShapeDtypeStruct((2, rows * size, count * size), BF16)
    high, low, second = pl.pallas_call(
        functools.partial(scatter_kernel, 1),
        out_shape=(split, split, packed),
        in_specs=[SMEM, VMEM, HBM],
        out_specs=(VMEM, VMEM, HBM),
        input_output_aliases={2: 2},
        compiler_params=PARAMS,
        cost_estimate=TINY,
        name="scatter",
    )(info, ablk, second)
    second = lax.ppermute(second, "gx", uneven + [(j, i) for i, j in uneven])

    partial = (
        jax.ShapeDtypeStruct((parts // 2, share, width), F32),
        jax.ShapeDtypeStruct((parts // 2, share, width), BF16),
    )
    own_t, keep, send = pl.pallas_call(
        functools.partial(own_kernel, parts),
        out_shape=(jax.ShapeDtypeStruct((width, rows * size), BF16),) + partial,
        in_specs=[SMEM, VMEM, VMEM],
        out_specs=(VMEM, VMEM, VMEM),
        scratch_shapes=[
            pltpu.VMEM((rows + 1, size, width), BF16),
            pltpu.VMEM((rows * size, width), BF16),
        ],
        compiler_params=PARAMS,
        cost_estimate=MEDIUM,
        name="own",
    )(info, ablk, pblk)
    keep, recv, folds = folded(keep, send, parts)
    high, low = pl.pallas_call(
        functools.partial(scatter_kernel, 0),
        out_shape=(split, split),
        in_specs=[SMEM, VMEM, VMEM, VMEM, VMEM],
        out_specs=(VMEM, VMEM),
        input_output_aliases={3: 0, 4: 1},
        compiler_params=PARAMS,
        cost_estimate=TINY,
        name="scatter",
    )(info, ablk, own_t, high, low)
    pieces = []
    for order, ghosts in enumerate((first, second)):
        after = [folds] if order else []
        pieces.append(
            pl.pallas_call(
                functools.partial(ghost_kernel, order),
                out_shape=partial,
                in_specs=[VMEM] * (4 + len(after)),
                out_specs=(VMEM, VMEM),
                scratch_shapes=[
                    pltpu.VMEM((count * size, width), BF16),
                    pltpu.VMEM((rows * size, width), BF16),
                ],
                compiler_params=PARAMS,
                cost_estimate=LONG,
                name="ghost",
            )(high, low, ghosts, own_t, *after)
        )
    token = pl.pallas_call(
        gate_kernel,
        out_shape=jax.ShapeDtypeStruct((8, LANES), F32),
        in_specs=[HBM],
        out_specs=VMEM,
        compiler_params=PARAMS,
        cost_estimate=LONG,
        name="gate",
    )(recv)
    sides = [folded(*pieces[0], parts), folded(*pieces[1], parts, (token,))]
    result = written(None, keep, recv, None)
    for order, (keep, recv, folds) in enumerate(sides):
        result = written(order, keep, recv, result)
    return result[None]


def solution(mesh):
    placed = (
        P("gx", "gy", None, None),
        P("gx", "gy", None),
        P("gx", "gy"),
        P("gx", "gy", None, None),
        P("gx", "gy", None),
        P("gx", "gy"),
    )
    return jax.shard_map(
        body, mesh=mesh, in_specs=placed, out_specs=P("gx", "gy", None), check_vma=False
    )
```

```python
import functools

import jax
import jax.numpy as jnp
from jax import lax
from jax.experimental import pallas as pl
from jax.experimental.pallas import tpu as pltpu
from jax.sharding import PartitionSpec as P

KA = 7
KS = 3
NCOL = 8
LANES = 128
WIDE = 256

F32 = jnp.float32
BF16 = jnp.bfloat16
SMEM = pl.BlockSpec(memory_space=pltpu.SMEM)
VMEM = pl.BlockSpec(memory_space=pltpu.VMEM)
HBM = pl.BlockSpec(memory_space=pltpu.HBM)
LONG = pl.CostEstimate(flops=10000000000, bytes_accessed=1000000, transcendentals=0)
MEDIUM = pl.CostEstimate(flops=1000000000, bytes_accessed=1000000, transcendentals=0)
SHORT = pl.CostEstimate(flops=100000000, bytes_accessed=1000000, transcendentals=0)
TINY = pl.CostEstimate(flops=1000000, bytes_accessed=1000000, transcendentals=0)
PARAMS = pltpu.CompilerParams(vmem_limit_bytes=24 * 1024 * 1024)


def spread(value, masks_of, width):
    size = value.shape[0]
    row = lax.broadcasted_iota(jnp.int32, (size, WIDE), 0)
    lane = lax.broadcasted_iota(jnp.int32, (size, WIDE), 1)
    unit = jnp.where(row == lane % size, 1.0, 0.0).astype(BF16)
    tiles = []
    for c in range(width // WIDE):
        moves = jnp.concatenate([unit * mask for mask in masks_of(c * WIDE // size)], axis=0)
        tiles.append(jnp.dot(value, moves, preferred_element_type=F32))
    return tiles


def masks_at(cols, size):
    slots = (lax.broadcasted_iota(jnp.int32, (1, WIDE), 1) // size).astype(F32)
    return lambda first: [
        jnp.where(slots == col - first, 1.0, 0.0).astype(BF16) for col in cols
    ]


def splats(info_ref, first, count, base):
    info = info_ref[...].astype(F32) - base
    shape = (info.shape[0], WIDE)
    return [jnp.broadcast_to(info[:, first + k : first + k + 1], shape) for k in range(count)]


def multiply(info, a_ref, base, ext_ref, prod_ref):
    rows, size = a_ref.shape[0], a_ref.shape[1]
    ext_ref[ext_ref.shape[0] - 1] = jnp.zeros(ext_ref.shape[1:], BF16)
    none = ext_ref.shape[0] - 1
    for n in range(rows):
        picks = []
        for k in range(KA):
            spot = info[n, k] - base
            good = (spot >= 0) & (spot < none)
            picks.append(jnp.where(good, spot, none))
        picked = jnp.concatenate([ext_ref[spot] for spot in picks], axis=0)
        value = jnp.dot(a_ref[n], picked, preferred_element_type=F32)
        prod_ref[n * size : (n + 1) * size, :] = value.astype(BF16)


def finish(ownt_ref, prod, keep_ref, send_ref):
    rows = ownt_ref.shape[0] // 2
    sent = jnp.dot(ownt_ref[rows:, :], prod, preferred_element_type=F32)
    send_ref[...] = sent.astype(BF16).reshape(send_ref.shape)
    kept = jnp.dot(ownt_ref[:rows, :], prod, preferred_element_type=F32)
    keep_ref[...] = kept.reshape(keep_ref.shape)


def pack_kernel(
    sends_in, pcol_in, acol_in, mush_in, p_in, first_ref, second_ref, info_out,
    sends, pcol, acol, mush, info, p_ref, packed_ref, sems,
):
    copies = [
        pltpu.make_async_copy(src, dst, sems.at[i])
        for i, (src, dst) in enumerate(
            ((sends_in, sends), (pcol_in, pcol), (acol_in, acol), (mush_in, mush), (p_in, p_ref))
        )
    ]
    for copy in copies:
        copy.start()
    for copy in copies[:4]:
        copy.wait()
    odd = lax.axis_index("gx") % 2
    rows, size = p_ref.shape[0], p_ref.shape[1]
    count = sends.shape[0] // 2
    slots = pcol.shape[0]
    for n in range(rows):
        limit = jnp.where(mush[n] > 0, KA, KS)
        for k in range(KA):
            info[n, k] = jnp.where(k < limit, acol[k, 0, n], -1)
        for j in range(slots):
            info[n, KA + j] = pcol[j, n]
    passed = pltpu.make_async_copy(info, info_out, sems.at[0])
    passed.start()
    starts = ((1 - odd) * count, odd * count)
    tail = packed_ref.shape[1] - count * size
    which = lax.broadcasted_iota(jnp.int32, (tail, packed_ref.shape[2]), 0)
    for i, start in enumerate(starts):
        cols = jnp.zeros(which.shape, F32)
        for s in range(count):
            row = sends[start + s]
            for j in range(slots):
                cols = jnp.where(which == s * slots + j, pcol[j, row].astype(F32), cols)
        packed_ref[i, count * size :, :] = cols.astype(BF16)
    copies[4].wait()
    copies = [passed]
    for i, (out_ref, start) in enumerate(zip((first_ref, second_ref), starts)):
        for s in range(count):
            packed_ref[i, s * size : (s + 1) * size, :] = p_ref[sends[start + s]]
        copies.append(pltpu.make_async_copy(packed_ref.at[i], out_ref, sems.at[1 + i]))
        copies[-1].start()
    for copy in copies:
        copy.wait()


def own_kernel(parts, info_ref, a_ref, p_ref, ownt_ref, keep_ref, send_ref, own_ref, prod_ref, info, sem):
    bit = lax.axis_index("gy") % 2
    rows, size = p_ref.shape[0], p_ref.shape[1]
    width = NCOL * size
    share = width // parts
    copy = pltpu.make_async_copy(info_ref, info, sem)
    copy.start()
    cols = splats(info_ref, KA, p_ref.shape[2] // size, 0)
    for n in range(rows):
        masks = masks_at([col[n : n + 1, :] for col in cols], size)
        for c, tile in enumerate(spread(p_ref[n], masks, width)):
            own_ref[n, :, c * WIDE : (c + 1) * WIDE] = tile.astype(BF16)
    for c in range(width // LANES):
        column = own_ref[:rows, :, c * LANES : (c + 1) * LANES]
        flipped = column.reshape(rows * size, LANES).T
        for k in range(LANES // share):
            part = c * (LANES // share) + k
            spot = part // 2 + jnp.where(part % 2 == bit, 0, parts // 2)
            at = pl.ds(pl.multiple_of(spot * share, share), share)
            ownt_ref[at, :] = flipped[k * share : (k + 1) * share, :]
    copy.wait()
    multiply(info, a_ref, 0, own_ref, prod_ref)
    finish(ownt_ref, prod_ref[...], keep_ref, send_ref)


def scatter_kernel(when, info_ref, a_ref, passed, *refs):
    high_ref, low_ref = refs[-3:-1] if when else refs[-2:]
    odd = lax.axis_index("gx") % 2
    rows, size = a_ref.shape[0], a_ref.shape[1]
    width = high_ref.shape[2]

    @pl.when(odd == when)
    def _():
        for order in range(2):
            right = odd if order else 1 - odd
            base = rows + right * (width // size)
            cols = splats(info_ref, 0, KA, base.astype(F32))
            for n in range(rows):
                at = slice(n * size, (n + 1) * size)
                masks = masks_at([col[n : n + 1, :] for col in cols], size)
                for c, tile in enumerate(spread(a_ref[n], masks, width)):
                    spot = slice(c * WIDE, (c + 1) * WIDE)
                    high = tile.astype(BF16)
                    high_ref[order, at, spot] = high
                    low_ref[order, at, spot] = (tile - high.astype(F32)).astype(BF16)


def ghost_kernel(order, high_ref, low_ref, in_ref, ownt_ref, *refs):
    keep_ref, send_ref, ext_ref, prod_ref = refs[-4:]
    width = ownt_ref.shape[0]
    size = width // NCOL
    slots = in_ref.shape[1] // size
    count = ext_ref.shape[0] // size
    cols = in_ref[count * size :, :].astype(F32)
    for n in range(count):
        at = slice(n * size, (n + 1) * size)
        masks = masks_at([cols[n * slots + j : n * slots + j + 1, :] for j in range(slots)], size)
        for c, tile in enumerate(spread(in_ref[at, :], masks, width)):
            ext_ref[at, c * WIDE : (c + 1) * WIDE] = tile.astype(BF16)
    ext = ext_ref[...]
    step = prod_ref.shape[0] // 2
    for m in range(2):
        at = slice(m * step, (m + 1) * step)
        value = jnp.dot(high_ref[order, at, :], ext, preferred_element_type=F32)
        value += jnp.dot(low_ref[order, at, :], ext, preferred_element_type=F32)
        prod_ref[at, :] = value.astype(BF16)
    finish(ownt_ref, prod_ref[...], keep_ref, send_ref)


def fold_kernel(stage, keep_ref, recv_ref, *refs):
    next_ref, send_ref = refs[-2:]
    bit = (lax.axis_index("gy") >> stage) % 2
    for i in range(next_ref.shape[0]):
        mine, other = 2 * i + bit, 2 * i + 1 - bit
        send_ref[i] = (keep_ref[other] + recv_ref[other].astype(F32)).astype(BF16)
        next_ref[i] = keep_ref[mine] + recv_ref[mine].astype(F32)


def write_kernel(order, keep_ref, recv_ref, *refs):
    out_ref, sum_ref, sem = refs[-3:]
    odd = lax.axis_index("gx") % 2
    third = 1 if order is None else 2 * odd if order else 2 - 2 * odd
    width = sum_ref.shape[1]
    sum_ref[...] = keep_ref[0] + recv_ref[0].astype(F32)
    spot = pl.ds(pl.multiple_of(third * width, width), width)
    copy = pltpu.make_async_copy(sum_ref, out_ref.at[:, spot], sem)
    copy.start()
    copy.wait()


def gate_kernel(recv_ref, token_ref):
    token_ref[...] = jnp.zeros(token_ref.shape, F32)


def swapped(value, axis, step):
    length = lax.axis_size(axis)
    return lax.ppermute(value, axis, [(i, i ^ step) for i in range(length) if i ^ step < length])


def folded(keep, send, parts, after=()):
    left, share, width = keep.shape
    stage = 0
    while left > 1:
        recv = swapped(send, "gy", 1 << stage)
        stage += 1
        left //= 2
        keep, send = pl.pallas_call(
            functools.partial(fold_kernel, stage),
            out_shape=(
                jax.ShapeDtypeStruct((left, share, width), F32),
                jax.ShapeDtypeStruct((left, share, width), BF16),
            ),
            in_specs=[VMEM] * (2 + len(after)),
            out_specs=(VMEM, VMEM),
            compiler_params=PARAMS,
            name="fold",
        )(keep, recv, *after)
        after = ()
    return keep, swapped(send, "gy", 1 << stage), keep


def written(order, keep, recv, result):
    share, width = keep.shape[1:]
    start = order is None
    whole = jax.ShapeDtypeStruct((share, 3 * width), F32)
    return pl.pallas_call(
        functools.partial(write_kernel, order),
        out_shape=whole,
        in_specs=[VMEM, VMEM] if start else [VMEM, VMEM, HBM],
        out_specs=HBM,
        input_output_aliases={} if start else {2: 0},
        scratch_shapes=[pltpu.VMEM((share, width), F32), pltpu.SemaphoreType.DMA],
        compiler_params=PARAMS,
        cost_estimate=SHORT,
        name="write",
    )(keep, recv, *([] if start else [result]))


def body(a_blocks, a_cols, mushy, p_blocks, p_cols, send_rows):
    rows, size, inner = p_blocks.shape[1:]
    acol, pcol = a_cols.transpose(2, 0, 1), p_cols[0].T
    mush, sends = mushy[0], send_rows[0]
    ablk, pblk = a_blocks[0], p_blocks[0]
    count = sends.shape[0] // 2
    width = NCOL * size
    length = lax.axis_size("gx")
    parts = lax.axis_size("gy")
    share = width // parts

    tail = -(-count * pcol.shape[0] // 16) * 16
    packed = jax.ShapeDtypeStruct((count * size + tail, inner), BF16)

    first, second, info = pl.pallas_call(
        pack_kernel,
        out_shape=(packed, packed, jax.ShapeDtypeStruct((rows, LANES), jnp.int32)),
        in_specs=[HBM] * 5,
        out_specs=(HBM, HBM, HBM),
        scratch_shapes=[
            pltpu.SMEM(sends.shape, sends.dtype),
            pltpu.SMEM(pcol.shape, pcol.dtype),
            pltpu.SMEM(acol.shape, acol.dtype),
            pltpu.SMEM(mush.shape, mush.dtype),
            pltpu.SMEM((rows, LANES), jnp.int32),
            pltpu.VMEM(pblk.shape, BF16),
            pltpu.VMEM((2,) + packed.shape, BF16),
            pltpu.SemaphoreType.DMA((5,)),
        ],
        compiler_params=pltpu.CompilerParams(vmem_limit_bytes=56 * 1024 * 1024),
        cost_estimate=LONG,
        name="pack",
    )(sends, pcol, acol, mush, pblk)
    even = [(i, i + 1) for i in range(0, length - 1, 2)]
    uneven = [(i, i + 1) for i in range(1, length - 1, 2)]
    first = lax.ppermute(first, "gx", even + [(j, i) for i, j in even])
    split = jax.ShapeDtypeStruct((2, rows * size, count * size), BF16)
    high, low, second = pl.pallas_call(
        functools.partial(scatter_kernel, 1),
        out_shape=(split, split, packed),
        in_specs=[VMEM, VMEM, HBM],
        out_specs=(VMEM, VMEM, HBM),
        input_output_aliases={2: 2},
        compiler_params=PARAMS,
        cost_estimate=TINY,
        name="scatter",
    )(info, ablk, second)
    second = lax.ppermute(second, "gx", uneven + [(j, i) for i, j in uneven])

    partial = (
        jax.ShapeDtypeStruct((parts // 2, share, width), F32),
        jax.ShapeDtypeStruct((parts // 2, share, width), BF16),
    )
    own_t, keep, send = pl.pallas_call(
        functools.partial(own_kernel, parts),
        out_shape=(jax.ShapeDtypeStruct((width, rows * size), BF16),) + partial,
        in_specs=[VMEM, VMEM, VMEM],
        out_specs=(VMEM, VMEM, VMEM),
        scratch_shapes=[
            pltpu.VMEM((rows + 1, size, width), BF16),
            pltpu.VMEM((rows * size, width), BF16),
            pltpu.SMEM((rows, LANES), jnp.int32),
            pltpu.SemaphoreType.DMA,
        ],
        compiler_params=PARAMS,
        cost_estimate=MEDIUM,
        name="own",
    )(info, ablk, pblk)
    keep, recv, folds = folded(keep, send, parts)
    high, low = pl.pallas_call(
        functools.partial(scatter_kernel, 0),
        out_shape=(split, split),
        in_specs=[VMEM, VMEM, VMEM, VMEM, VMEM],
        out_specs=(VMEM, VMEM),
        input_output_aliases={3: 0, 4: 1},
        compiler_params=PARAMS,
        cost_estimate=TINY,
        name="scatter",
    )(info, ablk, own_t, high, low)
    pieces = []
    for order, ghosts in enumerate((first, second)):
        after = [folds] if order else []
        pieces.append(
            pl.pallas_call(
                functools.partial(ghost_kernel, order),
                out_shape=partial,
                in_specs=[VMEM] * (4 + len(after)),
                out_specs=(VMEM, VMEM),
                scratch_shapes=[
                    pltpu.VMEM((count * size, width), BF16),
                    pltpu.VMEM((rows * size, width), BF16),
                ],
                compiler_params=PARAMS,
                cost_estimate=LONG,
                name="ghost",
            )(high, low, ghosts, own_t, *after)
        )
    token = pl.pallas_call(
        gate_kernel,
        out_shape=jax.ShapeDtypeStruct((8, LANES), F32),
        in_specs=[HBM],
        out_specs=VMEM,
        compiler_params=PARAMS,
        cost_estimate=LONG,
        name="gate",
    )(recv)
    sides = [folded(*pieces[0], parts), folded(*pieces[1], parts, (token,))]
    result = written(None, keep, recv, None)
    for order, (keep, recv, folds) in enumerate(sides):
        result = written(order, keep, recv, result)
    return result[None]


def solution(mesh):
    placed = (
        P("gx", "gy", None, None),
        P("gx", "gy", None),
        P("gx", "gy"),
        P("gx", "gy", None, None),
        P("gx", "gy", None),
        P("gx", "gy"),
    )
    return jax.shard_map(
        body, mesh=mesh, in_specs=placed, out_specs=P("gx", "gy", None), check_vma=False
    )
```

```python
import functools

import jax
import jax.numpy as jnp
from jax import lax
from jax.experimental import pallas as pl
from jax.experimental.pallas import tpu as pltpu
from jax.sharding import PartitionSpec as P

KA = 7
KS = 3
NCOL = 8
LANES = 128
WIDE = 256

F32 = jnp.float32
BF16 = jnp.bfloat16
SMEM = pl.BlockSpec(memory_space=pltpu.SMEM)
VMEM = pl.BlockSpec(memory_space=pltpu.VMEM)
HBM = pl.BlockSpec(memory_space=pltpu.HBM)
LONG = pl.CostEstimate(flops=10000000000, bytes_accessed=1000000, transcendentals=0)
MEDIUM = pl.CostEstimate(flops=1000000000, bytes_accessed=1000000, transcendentals=0)
SHORT = pl.CostEstimate(flops=100000000, bytes_accessed=1000000, transcendentals=0)
TINY = pl.CostEstimate(flops=1000000, bytes_accessed=1000000, transcendentals=0)
PARAMS = pltpu.CompilerParams(vmem_limit_bytes=24 * 1024 * 1024)


def spread(value, masks_of, width):
    size = value.shape[0]
    row = lax.broadcasted_iota(jnp.int32, (size, WIDE), 0)
    lane = lax.broadcasted_iota(jnp.int32, (size, WIDE), 1)
    unit = jnp.where(row == lane % size, 1.0, 0.0).astype(BF16)
    tiles = []
    for c in range(width // WIDE):
        moves = jnp.concatenate([unit * mask for mask in masks_of(c * WIDE // size)], axis=0)
        tiles.append(jnp.dot(value, moves, preferred_element_type=F32))
    return tiles


def masks_at(cols, size):
    slots = (lax.broadcasted_iota(jnp.int32, (1, WIDE), 1) // size).astype(F32)
    return lambda first: [
        jnp.where(slots == col - first, 1.0, 0.0).astype(BF16) for col in cols
    ]


def splats(info_ref, first, count, base):
    info = info_ref[...].astype(F32) - base
    shape = (info.shape[0], WIDE)
    return [jnp.broadcast_to(info[:, first + k : first + k + 1], shape) for k in range(count)]


def multiply(info, a_ref, base, ext_ref, prod_ref):
    rows, size = a_ref.shape[0], a_ref.shape[1]
    ext_ref[ext_ref.shape[0] - 1] = jnp.zeros(ext_ref.shape[1:], BF16)
    none = ext_ref.shape[0] - 1
    for n in range(rows):
        picks = []
        for k in range(KA):
            spot = info[n, k] - base
            good = (spot >= 0) & (spot < none)
            picks.append(jnp.where(good, spot, none))
        picked = jnp.concatenate([ext_ref[spot] for spot in picks], axis=0)
        value = jnp.dot(a_ref[n], picked, preferred_element_type=F32)
        prod_ref[n * size : (n + 1) * size, :] = value.astype(BF16)


def finish(ownt_ref, prod, keep_ref, send_ref):
    rows = ownt_ref.shape[0] // 2
    sent = jnp.dot(ownt_ref[rows:, :], prod, preferred_element_type=F32)
    send_ref[...] = sent.astype(BF16).reshape(send_ref.shape)
    kept = jnp.dot(ownt_ref[:rows, :], prod, preferred_element_type=F32)
    keep_ref[...] = kept.reshape(keep_ref.shape)


def pack_kernel(
    sends_in, pcol_in, acol_in, mush_in, p_in, first_ref, second_ref, info_out,
    sends, pcol, acol, mush, info, p_ref, packed_ref, sems,
):
    copies = [
        pltpu.make_async_copy(src, dst, sems.at[i])
        for i, (src, dst) in enumerate(
            ((sends_in, sends), (pcol_in, pcol), (acol_in, acol), (mush_in, mush), (p_in, p_ref))
        )
    ]
    for copy in copies:
        copy.start()
    for copy in copies[:4]:
        copy.wait()
    odd = lax.axis_index("gx") % 2
    rows, size = p_ref.shape[0], p_ref.shape[1]
    count = sends.shape[0] // 2
    slots = pcol.shape[0]
    for n in range(rows):
        limit = jnp.where(mush[n] > 0, KA, KS)
        for k in range(KA):
            info[n, k] = jnp.where(k < limit, acol[k, 0, n], -1)
        for j in range(slots):
            info[n, KA + j] = pcol[j, n]
    passed = pltpu.make_async_copy(info, info_out, sems.at[0])
    passed.start()
    starts = ((1 - odd) * count, odd * count)
    tail = packed_ref.shape[1] - count * size
    which = lax.broadcasted_iota(jnp.int32, (tail, packed_ref.shape[2]), 0)
    for i, start in enumerate(starts):
        cols = jnp.zeros(which.shape, F32)
        for s in range(count):
            row = sends[start + s]
            for j in range(slots):
                cols = jnp.where(which == s * slots + j, pcol[j, row].astype(F32), cols)
        packed_ref[i, count * size :, :] = cols.astype(BF16)
    copies[4].wait()
    copies = [passed]
    for i, (out_ref, start) in enumerate(zip((first_ref, second_ref), starts)):
        for s in range(count):
            packed_ref[i, s * size : (s + 1) * size, :] = p_ref[sends[start + s]]
        copies.append(pltpu.make_async_copy(packed_ref.at[i], out_ref, sems.at[1 + i]))
        copies[-1].start()
    for copy in copies:
        copy.wait()


def own_kernel(parts, info_ref, a_ref, p_ref, ownt_ref, keep_ref, send_ref, own_ref, prod_ref, info, sem):
    bit = lax.axis_index("gy") % 2
    rows, size = p_ref.shape[0], p_ref.shape[1]
    width = NCOL * size
    share = width // parts
    copy = pltpu.make_async_copy(info_ref, info, sem)
    copy.start()
    cols = splats(info_ref, KA, p_ref.shape[2] // size, 0)
    for n in range(rows):
        masks = masks_at([col[n : n + 1, :] for col in cols], size)
        for c, tile in enumerate(spread(p_ref[n], masks, width)):
            own_ref[n, :, c * WIDE : (c + 1) * WIDE] = tile.astype(BF16)
    copy.wait()
    multiply(info, a_ref, 0, own_ref, prod_ref)
    for c in range(width // LANES):
        column = own_ref[:rows, :, c * LANES : (c + 1) * LANES]
        flipped = column.reshape(rows * size, LANES).T
        for k in range(LANES // share):
            part = c * (LANES // share) + k
            spot = part // 2 + jnp.where(part % 2 == bit, 0, parts // 2)
            at = pl.ds(pl.multiple_of(spot * share, share), share)
            ownt_ref[at, :] = flipped[k * share : (k + 1) * share, :]
    finish(ownt_ref, prod_ref[...], keep_ref, send_ref)


def scatter(order, info_ref, a_ref, high_ref, low_ref):
    odd = lax.axis_index("gx") % 2
    right = odd if order else 1 - odd
    rows, size = a_ref.shape[0], a_ref.shape[1]
    width = high_ref.shape[1]
    base = rows + right * (width // size)
    cols = splats(info_ref, 0, KA, base.astype(F32))
    for n in range(rows):
        at = slice(n * size, (n + 1) * size)
        masks = masks_at([col[n : n + 1, :] for col in cols], size)
        for c, tile in enumerate(spread(a_ref[n], masks, width)):
            spot = slice(c * WIDE, (c + 1) * WIDE)
            high = tile.astype(BF16)
            high_ref[at, spot] = high
            low_ref[at, spot] = (tile - high.astype(F32)).astype(BF16)


def scatter_kernel(when, info_ref, a_ref, passed, *refs):
    high_ref, low_ref = refs[-3:-1] if when else refs[-2:]

    @pl.when(lax.axis_index("gx") % 2 == when)
    def _():
        for order in range(1 + when):
            scatter(order, info_ref, a_ref, high_ref.at[order], low_ref.at[order])


def ghost_kernel(order, high_ref, low_ref, in_ref, ownt_ref, *refs):
    if order:
        info_ref, a_ref, after, keep_ref, send_ref, ext_ref, prod_ref, mine_high, mine_low = refs
    else:
        keep_ref, send_ref, ext_ref, prod_ref = refs
    width = ownt_ref.shape[0]
    size = width // NCOL
    slots = in_ref.shape[1] // size
    count = ext_ref.shape[0] // size
    cols = in_ref[count * size :, :].astype(F32)
    for n in range(count):
        at = slice(n * size, (n + 1) * size)
        masks = masks_at([cols[n * slots + j : n * slots + j + 1, :] for j in range(slots)], size)
        for c, tile in enumerate(spread(in_ref[at, :], masks, width)):
            ext_ref[at, c * WIDE : (c + 1) * WIDE] = tile.astype(BF16)

    def product(high, low):
        ext = ext_ref[...]
        step = prod_ref.shape[0] // 2
        for m in range(2):
            at = slice(m * step, (m + 1) * step)
            value = jnp.dot(high[at, :], ext, preferred_element_type=F32)
            value += jnp.dot(low[at, :], ext, preferred_element_type=F32)
            prod_ref[at, :] = value.astype(BF16)

    if order:
        odd = lax.axis_index("gx") % 2

        @pl.when(odd == 0)
        def _():
            scatter(1, info_ref, a_ref, mine_high, mine_low)
            product(mine_high, mine_low)

        @pl.when(odd == 1)
        def _():
            product(high_ref.at[1], low_ref.at[1])

    else:
        product(high_ref.at[0], low_ref.at[0])
    finish(ownt_ref, prod_ref[...], keep_ref, send_ref)


def fold_kernel(stage, keep_ref, recv_ref, *refs):
    next_ref, send_ref = refs[-2:]
    bit = (lax.axis_index("gy") >> stage) % 2
    for i in range(next_ref.shape[0]):
        mine, other = 2 * i + bit, 2 * i + 1 - bit
        send_ref[i] = (keep_ref[other] + recv_ref[other].astype(F32)).astype(BF16)
        next_ref[i] = keep_ref[mine] + recv_ref[mine].astype(F32)


def write_kernel(order, keep_ref, recv_ref, *refs):
    out_ref, sum_ref, sem = refs[-3:]
    odd = lax.axis_index("gx") % 2
    third = 1 if order is None else 2 * odd if order else 2 - 2 * odd
    width = sum_ref.shape[1]
    sum_ref[...] = keep_ref[0] + recv_ref[0].astype(F32)
    spot = pl.ds(pl.multiple_of(third * width, width), width)
    copy = pltpu.make_async_copy(sum_ref, out_ref.at[:, spot], sem)
    copy.start()
    copy.wait()


def gate_kernel(recv_ref, token_ref):
    token_ref[...] = jnp.zeros(token_ref.shape, F32)


def swapped(value, axis, step):
    length = lax.axis_size(axis)
    return lax.ppermute(value, axis, [(i, i ^ step) for i in range(length) if i ^ step < length])


def folded(keep, send, parts, after=()):
    left, share, width = keep.shape
    stage = 0
    while left > 1:
        recv = swapped(send, "gy", 1 << stage)
        stage += 1
        left //= 2
        keep, send = pl.pallas_call(
            functools.partial(fold_kernel, stage),
            out_shape=(
                jax.ShapeDtypeStruct((left, share, width), F32),
                jax.ShapeDtypeStruct((left, share, width), BF16),
            ),
            in_specs=[VMEM] * (2 + len(after)),
            out_specs=(VMEM, VMEM),
            compiler_params=PARAMS,
            name="fold",
        )(keep, recv, *after)
        after = ()
    return keep, swapped(send, "gy", 1 << stage), keep


def written(order, keep, recv, result):
    share, width = keep.shape[1:]
    start = order is None
    whole = jax.ShapeDtypeStruct((share, 3 * width), F32)
    return pl.pallas_call(
        functools.partial(write_kernel, order),
        out_shape=whole,
        in_specs=[VMEM, VMEM] if start else [VMEM, VMEM, HBM],
        out_specs=HBM,
        input_output_aliases={} if start else {2: 0},
        scratch_shapes=[pltpu.VMEM((share, width), F32), pltpu.SemaphoreType.DMA],
        compiler_params=PARAMS,
        cost_estimate=SHORT,
        name="write",
    )(keep, recv, *([] if start else [result]))


def body(a_blocks, a_cols, mushy, p_blocks, p_cols, send_rows):
    rows, size, inner = p_blocks.shape[1:]
    acol, pcol = a_cols.transpose(2, 0, 1), p_cols[0].T
    mush, sends = mushy[0], send_rows[0]
    ablk, pblk = a_blocks[0], p_blocks[0]
    count = sends.shape[0] // 2
    width = NCOL * size
    length = lax.axis_size("gx")
    parts = lax.axis_size("gy")
    share = width // parts

    tail = -(-count * pcol.shape[0] // 16) * 16
    packed = jax.ShapeDtypeStruct((count * size + tail, inner), BF16)

    first, second, info = pl.pallas_call(
        pack_kernel,
        out_shape=(packed, packed, jax.ShapeDtypeStruct((rows, LANES), jnp.int32)),
        in_specs=[HBM] * 5,
        out_specs=(HBM, HBM, HBM),
        scratch_shapes=[
            pltpu.SMEM(sends.shape, sends.dtype),
            pltpu.SMEM(pcol.shape, pcol.dtype),
            pltpu.SMEM(acol.shape, acol.dtype),
            pltpu.SMEM(mush.shape, mush.dtype),
            pltpu.SMEM((rows, LANES), jnp.int32),
            pltpu.VMEM(pblk.shape, BF16),
            pltpu.VMEM((2,) + packed.shape, BF16),
            pltpu.SemaphoreType.DMA((5,)),
        ],
        compiler_params=pltpu.CompilerParams(vmem_limit_bytes=56 * 1024 * 1024),
        cost_estimate=LONG,
        name="pack",
    )(sends, pcol, acol, mush, pblk)
    even = [(i, i + 1) for i in range(0, length - 1, 2)]
    uneven = [(i, i + 1) for i in range(1, length - 1, 2)]
    first = lax.ppermute(first, "gx", even + [(j, i) for i, j in even])
    split = jax.ShapeDtypeStruct((2, rows * size, count * size), BF16)
    high, low, second = pl.pallas_call(
        functools.partial(scatter_kernel, 1),
        out_shape=(split, split, packed),
        in_specs=[VMEM, VMEM, HBM],
        out_specs=(VMEM, VMEM, HBM),
        input_output_aliases={2: 2},
        compiler_params=PARAMS,
        cost_estimate=TINY,
        name="scatter",
    )(info, ablk, second)
    second = lax.ppermute(second, "gx", uneven + [(j, i) for i, j in uneven])

    partial = (
        jax.ShapeDtypeStruct((parts // 2, share, width), F32),
        jax.ShapeDtypeStruct((parts // 2, share, width), BF16),
    )
    own_t, keep, send = pl.pallas_call(
        functools.partial(own_kernel, parts),
        out_shape=(jax.ShapeDtypeStruct((width, rows * size), BF16),) + partial,
        in_specs=[VMEM, VMEM, VMEM],
        out_specs=(VMEM, VMEM, VMEM),
        scratch_shapes=[
            pltpu.VMEM((rows + 1, size, width), BF16),
            pltpu.VMEM((rows * size, width), BF16),
            pltpu.SMEM((rows, LANES), jnp.int32),
            pltpu.SemaphoreType.DMA,
        ],
        compiler_params=PARAMS,
        cost_estimate=MEDIUM,
        name="own",
    )(info, ablk, pblk)
    keep, recv, folds = folded(keep, send, parts)
    high, low = pl.pallas_call(
        functools.partial(scatter_kernel, 0),
        out_shape=(split, split),
        in_specs=[VMEM, VMEM, VMEM, VMEM, VMEM],
        out_specs=(VMEM, VMEM),
        input_output_aliases={3: 0, 4: 1},
        compiler_params=PARAMS,
        cost_estimate=TINY,
        name="scatter",
    )(info, ablk, own_t, high, low)
    pieces = []
    for order, ghosts in enumerate((first, second)):
        more = [info, ablk, folds] if order else []
        pieces.append(
            pl.pallas_call(
                functools.partial(ghost_kernel, order),
                out_shape=partial,
                in_specs=[VMEM] * (4 + len(more)),
                out_specs=(VMEM, VMEM),
                scratch_shapes=[
                    pltpu.VMEM((count * size, width), BF16),
                    pltpu.VMEM((rows * size, width), BF16),
                ]
                + [pltpu.VMEM((rows * size, count * size), BF16)] * (2 * order),
                compiler_params=PARAMS,
                cost_estimate=LONG,
                name="ghost",
            )(high, low, ghosts, own_t, *more)
        )
    token = pl.pallas_call(
        gate_kernel,
        out_shape=jax.ShapeDtypeStruct((8, LANES), F32),
        in_specs=[HBM],
        out_specs=VMEM,
        compiler_params=PARAMS,
        cost_estimate=LONG,
        name="gate",
    )(recv)
    sides = [folded(*pieces[0], parts), folded(*pieces[1], parts, (token,))]
    result = written(None, keep, recv, None)
    for order, (keep, recv, folds) in enumerate(sides):
        result = written(order, keep, recv, result)
    return result[None]


def solution(mesh):
    placed = (
        P("gx", "gy", None, None),
        P("gx", "gy", None),
        P("gx", "gy"),
        P("gx", "gy", None, None),
        P("gx", "gy", None),
        P("gx", "gy"),
    )
    return jax.shard_map(
        body, mesh=mesh, in_specs=placed, out_specs=P("gx", "gy", None), check_vma=False
    )
```

```python
import functools

import jax
import jax.numpy as jnp
from jax import lax
from jax.experimental import pallas as pl
from jax.experimental.pallas import tpu as pltpu
from jax.sharding import PartitionSpec as P

KA = 7
KS = 3
NCOL = 8
LANES = 128
WIDE = 256

F32 = jnp.float32
BF16 = jnp.bfloat16
SMEM = pl.BlockSpec(memory_space=pltpu.SMEM)
VMEM = pl.BlockSpec(memory_space=pltpu.VMEM)
HBM = pl.BlockSpec(memory_space=pltpu.HBM)
LONG = pl.CostEstimate(flops=10000000000, bytes_accessed=1000000, transcendentals=0)
MEDIUM = pl.CostEstimate(flops=1000000000, bytes_accessed=1000000, transcendentals=0)
SHORT = pl.CostEstimate(flops=100000000, bytes_accessed=1000000, transcendentals=0)
TINY = pl.CostEstimate(flops=1000000, bytes_accessed=1000000, transcendentals=0)
PARAMS = pltpu.CompilerParams(vmem_limit_bytes=24 * 1024 * 1024)


def spread(value, masks_of, width):
    size = value.shape[0]
    row = lax.broadcasted_iota(jnp.int32, (size, WIDE), 0)
    lane = lax.broadcasted_iota(jnp.int32, (size, WIDE), 1)
    unit = jnp.where(row == lane % size, 1.0, 0.0).astype(BF16)
    tiles = []
    for c in range(width // WIDE):
        moves = jnp.concatenate([unit * mask for mask in masks_of(c * WIDE // size)], axis=0)
        tiles.append(jnp.dot(value, moves, preferred_element_type=F32))
    return tiles


def masks_at(cols, size):
    slots = (lax.broadcasted_iota(jnp.int32, (1, WIDE), 1) // size).astype(F32)
    return lambda first: [
        jnp.where(slots == col - first, 1.0, 0.0).astype(BF16) for col in cols
    ]


def splats(info_ref, first, count, base):
    info = info_ref[...].astype(F32) - base
    shape = (info.shape[0], WIDE)
    return [jnp.broadcast_to(info[:, first + k : first + k + 1], shape) for k in range(count)]


def multiply(info, a_ref, base, ext_ref, prod_ref):
    rows, size = a_ref.shape[0], a_ref.shape[1]
    ext_ref[ext_ref.shape[0] - 1] = jnp.zeros(ext_ref.shape[1:], BF16)
    none = ext_ref.shape[0] - 1
    for n in range(rows):
        picks = []
        for k in range(KA):
            spot = info[n, k] - base
            good = (spot >= 0) & (spot < none)
            picks.append(jnp.where(good, spot, none))
        picked = jnp.concatenate([ext_ref[spot] for spot in picks], axis=0)
        value = jnp.dot(a_ref[n], picked, preferred_element_type=F32)
        prod_ref[n * size : (n + 1) * size, :] = value.astype(BF16)


def finish(ownt_ref, prod, keep_ref, send_ref):
    rows = ownt_ref.shape[0] // 2
    sent = jnp.dot(ownt_ref[rows:, :], prod, preferred_element_type=F32)
    send_ref[...] = sent.astype(BF16).reshape(send_ref.shape)
    kept = jnp.dot(ownt_ref[:rows, :], prod, preferred_element_type=F32)
    keep_ref[...] = kept.reshape(keep_ref.shape)


def pack_kernel(
    sends_in, pcol_in, acol_in, mush_in, p_in, first_ref, second_ref, info_out,
    sends, pcol, acol, mush, info, p_ref, packed_ref, sems,
):
    copies = [
        pltpu.make_async_copy(src, dst, sems.at[i])
        for i, (src, dst) in enumerate(
            ((sends_in, sends), (pcol_in, pcol), (acol_in, acol), (mush_in, mush), (p_in, p_ref))
        )
    ]
    for copy in copies:
        copy.start()
    for copy in copies[:4]:
        copy.wait()
    odd = lax.axis_index("gx") % 2
    rows, size = p_ref.shape[0], p_ref.shape[1]
    count = sends.shape[0] // 2
    slots = pcol.shape[0]
    starts = ((1 - odd) * count, odd * count)
    tail = packed_ref.shape[1] - count * size
    which = lax.broadcasted_iota(jnp.int32, (tail, packed_ref.shape[2]), 0)
    for i, start in enumerate(starts):
        cols = jnp.zeros(which.shape, F32)
        for s in range(count):
            row = sends[start + s]
            for j in range(slots):
                cols = jnp.where(which == s * slots + j, pcol[j, row].astype(F32), cols)
        packed_ref[i, count * size :, :] = cols.astype(BF16)
    copies[4].wait()
    copies = []
    for i, (out_ref, start) in enumerate(zip((first_ref, second_ref), starts)):
        for s in range(count):
            packed_ref[i, s * size : (s + 1) * size, :] = p_ref[sends[start + s]]
        copies.append(pltpu.make_async_copy(packed_ref.at[i], out_ref, sems.at[1 + i]))
        copies[-1].start()
    for n in range(rows):
        limit = jnp.where(mush[n] > 0, KA, KS)
        for k in range(KA):
            info[n, k] = jnp.where(k < limit, acol[k, 0, n], -1)
        for j in range(slots):
            info[n, KA + j] = pcol[j, n]
    passed = pltpu.make_async_copy(info, info_out, sems.at[0])
    passed.start()
    for copy in copies + [passed]:
        copy.wait()


def own_kernel(parts, info_ref, a_ref, p_ref, ownt_ref, keep_ref, send_ref, own_ref, prod_ref, info, sem):
    bit = lax.axis_index("gy") % 2
    rows, size = p_ref.shape[0], p_ref.shape[1]
    width = NCOL * size
    share = width // parts
    copy = pltpu.make_async_copy(info_ref, info, sem)
    copy.start()
    cols = splats(info_ref, KA, p_ref.shape[2] // size, 0)
    for n in range(rows):
        masks = masks_at([col[n : n + 1, :] for col in cols], size)
        for c, tile in enumerate(spread(p_ref[n], masks, width)):
            own_ref[n, :, c * WIDE : (c + 1) * WIDE] = tile.astype(BF16)
    copy.wait()
    multiply(info, a_ref, 0, own_ref, prod_ref)
    for c in range(width // LANES):
        column = own_ref[:rows, :, c * LANES : (c + 1) * LANES]
        flipped = column.reshape(rows * size, LANES).T
        for k in range(LANES // share):
            part = c * (LANES // share) + k
            spot = part // 2 + jnp.where(part % 2 == bit, 0, parts // 2)
            at = pl.ds(pl.multiple_of(spot * share, share), share)
            ownt_ref[at, :] = flipped[k * share : (k + 1) * share, :]
    finish(ownt_ref, prod_ref[...], keep_ref, send_ref)


def scatter(order, info_ref, a_ref, high_ref, low_ref):
    odd = lax.axis_index("gx") % 2
    right = odd if order else 1 - odd
    rows, size = a_ref.shape[0], a_ref.shape[1]
    width = high_ref.shape[1]
    base = rows + right * (width // size)
    cols = splats(info_ref, 0, KA, base.astype(F32))
    for n in range(rows):
        at = slice(n * size, (n + 1) * size)
        masks = masks_at([col[n : n + 1, :] for col in cols], size)
        for c, tile in enumerate(spread(a_ref[n], masks, width)):
            spot = slice(c * WIDE, (c + 1) * WIDE)
            high = tile.astype(BF16)
            high_ref[at, spot] = high
            low_ref[at, spot] = (tile - high.astype(F32)).astype(BF16)


def scatter_kernel(when, info_ref, a_ref, passed, *refs):
    high_ref, low_ref = refs[-3:-1] if when else refs[-2:]

    @pl.when(lax.axis_index("gx") % 2 == when)
    def _():
        for order in range(1 + when):
            scatter(order, info_ref, a_ref, high_ref.at[order], low_ref.at[order])


def ghost_kernel(order, high_ref, low_ref, in_ref, ownt_ref, *refs):
    if order:
        info_ref, a_ref, after, keep_ref, send_ref, ext_ref, prod_ref, mine_high, mine_low = refs
    else:
        keep_ref, send_ref, ext_ref, prod_ref = refs
    width = ownt_ref.shape[0]
    size = width // NCOL
    slots = in_ref.shape[1] // size
    count = ext_ref.shape[0] // size
    cols = in_ref[count * size :, :].astype(F32)
    for n in range(count):
        at = slice(n * size, (n + 1) * size)
        masks = masks_at([cols[n * slots + j : n * slots + j + 1, :] for j in range(slots)], size)
        for c, tile in enumerate(spread(in_ref[at, :], masks, width)):
            ext_ref[at, c * WIDE : (c + 1) * WIDE] = tile.astype(BF16)

    def product(high, low):
        ext = ext_ref[...]
        step = prod_ref.shape[0] // 2
        for m in range(2):
            at = slice(m * step, (m + 1) * step)
            value = jnp.dot(high[at, :], ext, preferred_element_type=F32)
            value += jnp.dot(low[at, :], ext, preferred_element_type=F32)
            prod_ref[at, :] = value.astype(BF16)

    if order:
        odd = lax.axis_index("gx") % 2

        @pl.when(odd == 0)
        def _():
            scatter(1, info_ref, a_ref, mine_high, mine_low)
            product(mine_high, mine_low)

        @pl.when(odd == 1)
        def _():
            product(high_ref.at[1], low_ref.at[1])

    else:
        product(high_ref.at[0], low_ref.at[0])
    finish(ownt_ref, prod_ref[...], keep_ref, send_ref)


def fold_kernel(stage, count, keep_ref, recv_ref, *refs):
    next_ref, send_ref = refs[count : count + 2]
    bit = (lax.axis_index("gy") >> stage) % 2
    for i in range(next_ref.shape[0]):
        mine, other = 2 * i + bit, 2 * i + 1 - bit
        send_ref[i] = (keep_ref[other] + recv_ref[other].astype(F32)).astype(BF16)
        next_ref[i] = keep_ref[mine] + recv_ref[mine].astype(F32)


def write_kernel(order, keep_ref, recv_ref, *refs):
    out_ref, sum_ref, sem = refs[-3:]
    odd = lax.axis_index("gx") % 2
    third = 1 if order is None else 2 * odd if order else 2 - 2 * odd
    width = sum_ref.shape[1]
    sum_ref[...] = keep_ref[0] + recv_ref[0].astype(F32)
    spot = pl.ds(pl.multiple_of(third * width, width), width)
    copy = pltpu.make_async_copy(sum_ref, out_ref.at[:, spot], sem)
    copy.start()
    copy.wait()


def gate_kernel(recv_ref, token_ref):
    token_ref[...] = jnp.zeros(token_ref.shape, F32)


def swapped(value, axis, step):
    length = lax.axis_size(axis)
    return lax.ppermute(value, axis, [(i, i ^ step) for i in range(length) if i ^ step < length])


def folded(keep, send, parts, *passed):
    left, share, width = keep.shape
    stage = 0
    later = ()
    while left > 1:
        recv = swapped(send, "gy", 1 << stage)
        stage += 1
        left //= 2
        through = passed if stage == 1 else ()
        count = len(through)
        keep, send, *through = pl.pallas_call(
            functools.partial(fold_kernel, stage, count),
            out_shape=(
                jax.ShapeDtypeStruct((left, share, width), F32),
                jax.ShapeDtypeStruct((left, share, width), BF16),
            )
            + tuple(jax.ShapeDtypeStruct(value.shape, value.dtype) for value in through),
            in_specs=[VMEM] * (2 + count),
            out_specs=(VMEM,) * (2 + count),
            input_output_aliases={2 + i: 2 + i for i in range(count)},
            compiler_params=PARAMS,
            name="fold",
        )(keep, recv, *through)
        if stage == 1:
            later, folds = through, keep
    return keep, swapped(send, "gy", 1 << stage), folds, later


def written(order, keep, recv, result):
    share, width = keep.shape[1:]
    start = order is None
    whole = jax.ShapeDtypeStruct((share, 3 * width), F32)
    return pl.pallas_call(
        functools.partial(write_kernel, order),
        out_shape=whole,
        in_specs=[VMEM, VMEM] if start else [VMEM, VMEM, HBM],
        out_specs=HBM,
        input_output_aliases={} if start else {2: 0},
        scratch_shapes=[pltpu.VMEM((share, width), F32), pltpu.SemaphoreType.DMA],
        compiler_params=PARAMS,
        cost_estimate=SHORT,
        name="write",
    )(keep, recv, *([] if start else [result]))


def body(a_blocks, a_cols, mushy, p_blocks, p_cols, send_rows):
    rows, size, inner = p_blocks.shape[1:]
    acol, pcol = a_cols.transpose(2, 0, 1), p_cols[0].T
    mush, sends = mushy[0], send_rows[0]
    ablk, pblk = a_blocks[0], p_blocks[0]
    count = sends.shape[0] // 2
    width = NCOL * size
    length = lax.axis_size("gx")
    parts = lax.axis_size("gy")
    share = width // parts

    tail = -(-count * pcol.shape[0] // 16) * 16
    packed = jax.ShapeDtypeStruct((count * size + tail, inner), BF16)

    first, second, info = pl.pallas_call(
        pack_kernel,
        out_shape=(packed, packed, jax.ShapeDtypeStruct((rows, LANES), jnp.int32)),
        in_specs=[HBM] * 5,
        out_specs=(HBM, HBM, HBM),
        scratch_shapes=[
            pltpu.SMEM(sends.shape, sends.dtype),
            pltpu.SMEM(pcol.shape, pcol.dtype),
            pltpu.SMEM(acol.shape, acol.dtype),
            pltpu.SMEM(mush.shape, mush.dtype),
            pltpu.SMEM((rows, LANES), jnp.int32),
            pltpu.VMEM(pblk.shape, BF16),
            pltpu.VMEM((2,) + packed.shape, BF16),
            pltpu.SemaphoreType.DMA((5,)),
        ],
        compiler_params=pltpu.CompilerParams(vmem_limit_bytes=56 * 1024 * 1024),
        cost_estimate=LONG,
        name="pack",
    )(sends, pcol, acol, mush, pblk)
    even = [(i, i + 1) for i in range(0, length - 1, 2)]
    uneven = [(i, i + 1) for i in range(1, length - 1, 2)]
    first = lax.ppermute(first, "gx", even + [(j, i) for i, j in even])
    split = jax.ShapeDtypeStruct((2, rows * size, count * size), BF16)
    high, low, second = pl.pallas_call(
        functools.partial(scatter_kernel, 1),
        out_shape=(split, split, packed),
        in_specs=[VMEM, VMEM, HBM],
        out_specs=(VMEM, VMEM, HBM),
        input_output_aliases={2: 2},
        compiler_params=PARAMS,
        cost_estimate=TINY,
        name="scatter",
    )(info, ablk, second)
    second = lax.ppermute(second, "gx", uneven + [(j, i) for i, j in uneven])

    partial = (
        jax.ShapeDtypeStruct((parts // 2, share, width), F32),
        jax.ShapeDtypeStruct((parts // 2, share, width), BF16),
    )
    own_t, keep, send = pl.pallas_call(
        functools.partial(own_kernel, parts),
        out_shape=(jax.ShapeDtypeStruct((width, rows * size), BF16),) + partial,
        in_specs=[VMEM, VMEM, VMEM],
        out_specs=(VMEM, VMEM, VMEM),
        scratch_shapes=[
            pltpu.VMEM((rows + 1, size, width), BF16),
            pltpu.VMEM((rows * size, width), BF16),
            pltpu.SMEM((rows, LANES), jnp.int32),
            pltpu.SemaphoreType.DMA,
        ],
        compiler_params=PARAMS,
        cost_estimate=MEDIUM,
        name="own",
    )(info, ablk, pblk)
    high, low = pl.pallas_call(
        functools.partial(scatter_kernel, 0),
        out_shape=(split, split),
        in_specs=[VMEM, VMEM, VMEM, VMEM, VMEM],
        out_specs=(VMEM, VMEM),
        input_output_aliases={3: 0, 4: 1},
        compiler_params=PARAMS,
        cost_estimate=TINY,
        name="scatter",
    )(info, ablk, own_t, high, low)

    def ghost(order, ghosts, *more):
        return pl.pallas_call(
            functools.partial(ghost_kernel, order),
            out_shape=partial,
            in_specs=[VMEM] * (4 + len(more)),
            out_specs=(VMEM, VMEM),
            scratch_shapes=[
                pltpu.VMEM((count * size, width), BF16),
                pltpu.VMEM((rows * size, width), BF16),
            ]
            + [pltpu.VMEM((rows * size, count * size), BF16)] * (2 * order),
            compiler_params=PARAMS,
            cost_estimate=LONG,
            name="ghost",
        )(high, low, ghosts, own_t, *more)

    side_keep, side_send = ghost(0, first)
    keep, recv, folds, (side_send,) = folded(keep, send, parts, side_send)
    last = ghost(1, second, info, ablk, folds)
    token = pl.pallas_call(
        gate_kernel,
        out_shape=jax.ShapeDtypeStruct((8, LANES), F32),
        in_specs=[HBM],
        out_specs=VMEM,
        compiler_params=PARAMS,
        cost_estimate=LONG,
        name="gate",
    )(recv)
    sides = [folded(side_keep, side_send, parts), folded(*last, parts, token)]
    result = written(None, keep, recv, None)
    for order, (keep, recv, folds, later) in enumerate(sides):
        result = written(order, keep, recv, result)
    return result[None]


def solution(mesh):
    placed = (
        P("gx", "gy", None, None),
        P("gx", "gy", None),
        P("gx", "gy"),
        P("gx", "gy", None, None),
        P("gx", "gy", None),
        P("gx", "gy"),
    )
    return jax.shard_map(
        body, mesh=mesh, in_specs=placed, out_specs=P("gx", "gy", None), check_vma=False
    )
```

```python
import functools

import jax
import jax.numpy as jnp
from jax import lax
from jax.experimental import pallas as pl
from jax.experimental.pallas import tpu as pltpu
from jax.sharding import PartitionSpec as P

KA = 7
KS = 3
NCOL = 8
LANES = 128
WIDE = 256

F32 = jnp.float32
BF16 = jnp.bfloat16
SMEM = pl.BlockSpec(memory_space=pltpu.SMEM)
VMEM = pl.BlockSpec(memory_space=pltpu.VMEM)
HBM = pl.BlockSpec(memory_space=pltpu.HBM)
LONG = pl.CostEstimate(flops=10000000000, bytes_accessed=1000000, transcendentals=0)
MEDIUM = pl.CostEstimate(flops=1000000000, bytes_accessed=1000000, transcendentals=0)
SHORT = pl.CostEstimate(flops=100000000, bytes_accessed=1000000, transcendentals=0)
TINY = pl.CostEstimate(flops=1000000, bytes_accessed=1000000, transcendentals=0)
PARAMS = pltpu.CompilerParams(vmem_limit_bytes=24 * 1024 * 1024)


def spread(value, masks_of, width):
    size = value.shape[0]
    row = lax.broadcasted_iota(jnp.int32, (size, WIDE), 0)
    lane = lax.broadcasted_iota(jnp.int32, (size, WIDE), 1)
    unit = jnp.where(row == lane % size, 1.0, 0.0).astype(BF16)
    tiles = []
    for c in range(width // WIDE):
        moves = jnp.concatenate([unit * mask for mask in masks_of(c * WIDE // size)], axis=0)
        tiles.append(jnp.dot(value, moves, preferred_element_type=F32))
    return tiles


def masks_at(cols, size):
    slots = (lax.broadcasted_iota(jnp.int32, (1, WIDE), 1) // size).astype(F32)
    return lambda first: [
        jnp.where(slots == col - first, 1.0, 0.0).astype(BF16) for col in cols
    ]


def splats(info_ref, first, count, base):
    info = info_ref[...].astype(F32) - base
    shape = (info.shape[0], WIDE)
    return [jnp.broadcast_to(info[:, first + k : first + k + 1], shape) for k in range(count)]


def multiply(info, a_ref, base, ext_ref, prod_ref):
    rows, size = a_ref.shape[0], a_ref.shape[1]
    ext_ref[ext_ref.shape[0] - 1] = jnp.zeros(ext_ref.shape[1:], BF16)
    none = ext_ref.shape[0] - 1
    for n in range(rows):
        picks = []
        for k in range(KA):
            spot = info[n, k] - base
            good = (spot >= 0) & (spot < none)
            picks.append(jnp.where(good, spot, none))
        picked = jnp.concatenate([ext_ref[spot] for spot in picks], axis=0)
        value = jnp.dot(a_ref[n], picked, preferred_element_type=F32)
        prod_ref[n * size : (n + 1) * size, :] = value.astype(BF16)


def finish(ownt_ref, prod, keep_ref, send_ref):
    rows = ownt_ref.shape[0] // 2
    sent = jnp.dot(ownt_ref[rows:, :], prod, preferred_element_type=F32)
    send_ref[...] = sent.astype(BF16).reshape(send_ref.shape)
    kept = jnp.dot(ownt_ref[:rows, :], prod, preferred_element_type=F32)
    keep_ref[...] = kept.reshape(keep_ref.shape)


def pack_kernel(
    sends_in, pcol_in, acol_in, mush_in, p_in, first_ref, second_ref, info_out,
    sends, pcol, acol, mush, info, p_ref, packed_ref, sems,
):
    copies = [
        pltpu.make_async_copy(src, dst, sems.at[i])
        for i, (src, dst) in enumerate(
            ((sends_in, sends), (pcol_in, pcol), (acol_in, acol), (mush_in, mush), (p_in, p_ref))
        )
    ]
    for copy in copies:
        copy.start()
    for copy in copies[:4]:
        copy.wait()
    odd = lax.axis_index("gx") % 2
    rows, size = p_ref.shape[0], p_ref.shape[1]
    count = sends.shape[0] // 2
    slots = pcol.shape[0]
    starts = ((1 - odd) * count, odd * count)
    tail = packed_ref.shape[1] - count * size
    which = lax.broadcasted_iota(jnp.int32, (tail, packed_ref.shape[2]), 0)
    for i, start in enumerate(starts):
        cols = jnp.zeros(which.shape, F32)
        for s in range(count):
            row = sends[start + s]
            for j in range(slots):
                cols = jnp.where(which == s * slots + j, pcol[j, row].astype(F32), cols)
        packed_ref[i, count * size :, :] = cols.astype(BF16)
    copies[4].wait()
    copies = []
    for i, (out_ref, start) in enumerate(zip((first_ref, second_ref), starts)):
        for s in range(count):
            packed_ref[i, s * size : (s + 1) * size, :] = p_ref[sends[start + s]]
        copies.append(pltpu.make_async_copy(packed_ref.at[i], out_ref, sems.at[1 + i]))
        copies[-1].start()
    for n in range(rows):
        limit = jnp.where(mush[n] > 0, KA, KS)
        for k in range(KA):
            info[n, k] = jnp.where(k < limit, acol[k, 0, n], -1)
        for j in range(slots):
            info[n, KA + j] = pcol[j, n]
    passed = pltpu.make_async_copy(info, info_out, sems.at[0])
    passed.start()
    for copy in copies + [passed]:
        copy.wait()


def own_kernel(parts, info_ref, a_ref, p_ref, ownt_ref, keep_ref, send_ref, own_ref, prod_ref, info, sem):
    bit = lax.axis_index("gy") % 2
    rows, size = p_ref.shape[0], p_ref.shape[1]
    width = NCOL * size
    share = width // parts
    copy = pltpu.make_async_copy(info_ref, info, sem)
    copy.start()
    cols = splats(info_ref, KA, p_ref.shape[2] // size, 0)
    for n in range(rows):
        masks = masks_at([col[n : n + 1, :] for col in cols], size)
        for c, tile in enumerate(spread(p_ref[n], masks, width)):
            own_ref[n, :, c * WIDE : (c + 1) * WIDE] = tile.astype(BF16)
    copy.wait()
    multiply(info, a_ref, 0, own_ref, prod_ref)
    for c in range(width // LANES):
        column = own_ref[:rows, :, c * LANES : (c + 1) * LANES]
        flipped = column.reshape(rows * size, LANES).T
        for k in range(LANES // share):
            part = c * (LANES // share) + k
            spot = part // 2 + jnp.where(part % 2 == bit, 0, parts // 2)
            at = pl.ds(pl.multiple_of(spot * share, share), share)
            ownt_ref[at, :] = flipped[k * share : (k + 1) * share, :]
    finish(ownt_ref, prod_ref[...], keep_ref, send_ref)


def scatter(order, info_ref, a_ref, high_ref, low_ref):
    odd = lax.axis_index("gx") % 2
    right = odd if order else 1 - odd
    rows, size = a_ref.shape[0], a_ref.shape[1]
    width = high_ref.shape[1]
    base = rows + right * (width // size)
    cols = splats(info_ref, 0, KA, base.astype(F32))
    for n in range(rows):
        at = slice(n * size, (n + 1) * size)
        masks = masks_at([col[n : n + 1, :] for col in cols], size)
        for c, tile in enumerate(spread(a_ref[n], masks, width)):
            spot = slice(c * WIDE, (c + 1) * WIDE)
            high = tile.astype(BF16)
            high_ref[at, spot] = high
            low_ref[at, spot] = (tile - high.astype(F32)).astype(BF16)


def scatter_kernel(late, info_ref, a_ref, passed, *refs):
    high_ref, low_ref = refs[-2:] if late else refs[-3:-1]
    place = lax.axis_index("gx")

    def side(order):
        scatter(order, info_ref, a_ref, high_ref.at[order], low_ref.at[order])

    if late:
        pl.when(place % 2 == 0)(lambda: side(0))
        pl.when((place % 2 == 1) | (place == 0))(lambda: side(1))
    else:
        pl.when(place % 2 == 1)(lambda: side(0))


def ghost_kernel(order, high_ref, low_ref, in_ref, ownt_ref, *refs):
    if order:
        info_ref, a_ref, after, keep_ref, send_ref, ext_ref, prod_ref, mine_high, mine_low = refs
    else:
        keep_ref, send_ref, ext_ref, prod_ref = refs
    width = ownt_ref.shape[0]
    size = width // NCOL
    slots = in_ref.shape[1] // size
    count = ext_ref.shape[0] // size
    cols = in_ref[count * size :, :].astype(F32)
    for n in range(count):
        at = slice(n * size, (n + 1) * size)
        masks = masks_at([cols[n * slots + j : n * slots + j + 1, :] for j in range(slots)], size)
        for c, tile in enumerate(spread(in_ref[at, :], masks, width)):
            ext_ref[at, c * WIDE : (c + 1) * WIDE] = tile.astype(BF16)

    def product(high, low):
        ext = ext_ref[...]
        step = prod_ref.shape[0] // 2
        for m in range(2):
            at = slice(m * step, (m + 1) * step)
            value = jnp.dot(high[at, :], ext, preferred_element_type=F32)
            value += jnp.dot(low[at, :], ext, preferred_element_type=F32)
            prod_ref[at, :] = value.astype(BF16)

    if order:
        place = lax.axis_index("gx")
        open_side = (place % 2 == 0) & (place > 0)

        @pl.when(open_side)
        def _():
            scatter(1, info_ref, a_ref, mine_high, mine_low)
            product(mine_high, mine_low)

        @pl.when(jnp.logical_not(open_side))
        def _():
            product(high_ref.at[1], low_ref.at[1])

    else:
        product(high_ref.at[0], low_ref.at[0])
    finish(ownt_ref, prod_ref[...], keep_ref, send_ref)


def fold_kernel(stage, count, keep_ref, recv_ref, *refs):
    next_ref, send_ref = refs[count : count + 2]
    bit = (lax.axis_index("gy") >> stage) % 2
    for i in range(next_ref.shape[0]):
        mine, other = 2 * i + bit, 2 * i + 1 - bit
        send_ref[i] = (keep_ref[other] + recv_ref[other].astype(F32)).astype(BF16)
        next_ref[i] = keep_ref[mine] + recv_ref[mine].astype(F32)


def write_kernel(order, keep_ref, recv_ref, *refs):
    out_ref, sum_ref, sems = refs[-3:]
    odd = lax.axis_index("gx") % 2
    third = 1 if order is None else 2 * odd if order else 2 - 2 * odd
    share, width = sum_ref.shape
    spot = pl.ds(pl.multiple_of(third * width, width), width)
    count = sems.shape[0]
    copies = []
    for i in range(count):
        at = slice(i * share // count, (i + 1) * share // count)
        sum_ref[at, :] = keep_ref[0, at, :] + recv_ref[0, at, :].astype(F32)
        copies.append(pltpu.make_async_copy(sum_ref.at[at], out_ref.at[at, spot], sems.at[i]))
        copies[-1].start()
    for copy in copies:
        copy.wait()


def gate_kernel(recv_ref, token_ref):
    token_ref[...] = jnp.zeros(token_ref.shape, F32)


def swapped(value, axis, step):
    length = lax.axis_size(axis)
    return lax.ppermute(value, axis, [(i, i ^ step) for i in range(length) if i ^ step < length])


def folded(keep, send, parts, *passed):
    left, share, width = keep.shape
    stage = 0
    later = ()
    while left > 1:
        recv = swapped(send, "gy", 1 << stage)
        stage += 1
        left //= 2
        through = passed if stage == 1 else ()
        count = len(through)
        keep, send, *through = pl.pallas_call(
            functools.partial(fold_kernel, stage, count),
            out_shape=(
                jax.ShapeDtypeStruct((left, share, width), F32),
                jax.ShapeDtypeStruct((left, share, width), BF16),
            )
            + tuple(jax.ShapeDtypeStruct(value.shape, value.dtype) for value in through),
            in_specs=[VMEM] * (2 + count),
            out_specs=(VMEM,) * (2 + count),
            input_output_aliases={2 + i: 2 + i for i in range(count)},
            compiler_params=PARAMS,
            name="fold",
        )(keep, recv, *through)
        if stage == 1:
            later, folds = through, keep
    return keep, swapped(send, "gy", 1 << stage), folds, later


def written(order, keep, recv, result):
    share, width = keep.shape[1:]
    start = order is None
    whole = jax.ShapeDtypeStruct((share, 3 * width), F32)
    return pl.pallas_call(
        functools.partial(write_kernel, order),
        out_shape=whole,
        in_specs=[VMEM, VMEM] if start else [VMEM, VMEM, HBM],
        out_specs=HBM,
        input_output_aliases={} if start else {2: 0},
        scratch_shapes=[
            pltpu.VMEM((share, width), F32),
            pltpu.SemaphoreType.DMA((max(1, min(4, share // 16)),)),
        ],
        compiler_params=PARAMS,
        cost_estimate=SHORT,
        name="write",
    )(keep, recv, *([] if start else [result]))


def body(a_blocks, a_cols, mushy, p_blocks, p_cols, send_rows):
    rows, size, inner = p_blocks.shape[1:]
    acol, pcol = a_cols.transpose(2, 0, 1), p_cols[0].T
    mush, sends = mushy[0], send_rows[0]
    ablk, pblk = a_blocks[0], p_blocks[0]
    count = sends.shape[0] // 2
    width = NCOL * size
    length = lax.axis_size("gx")
    parts = lax.axis_size("gy")
    share = width // parts

    tail = -(-count * pcol.shape[0] // 16) * 16
    packed = jax.ShapeDtypeStruct((count * size + tail, inner), BF16)

    first, second, info = pl.pallas_call(
        pack_kernel,
        out_shape=(packed, packed, jax.ShapeDtypeStruct((rows, LANES), jnp.int32)),
        in_specs=[HBM] * 5,
        out_specs=(HBM, HBM, HBM),
        scratch_shapes=[
            pltpu.SMEM(sends.shape, sends.dtype),
            pltpu.SMEM(pcol.shape, pcol.dtype),
            pltpu.SMEM(acol.shape, acol.dtype),
            pltpu.SMEM(mush.shape, mush.dtype),
            pltpu.SMEM((rows, LANES), jnp.int32),
            pltpu.VMEM(pblk.shape, BF16),
            pltpu.VMEM((2,) + packed.shape, BF16),
            pltpu.SemaphoreType.DMA((5,)),
        ],
        compiler_params=pltpu.CompilerParams(vmem_limit_bytes=56 * 1024 * 1024),
        cost_estimate=LONG,
        name="pack",
    )(sends, pcol, acol, mush, pblk)
    even = [(i, i + 1) for i in range(0, length - 1, 2)]
    uneven = [(i, i + 1) for i in range(1, length - 1, 2)]
    first = lax.ppermute(first, "gx", even + [(j, i) for i, j in even])
    split = jax.ShapeDtypeStruct((2, rows * size, count * size), BF16)
    high, low, second = pl.pallas_call(
        functools.partial(scatter_kernel, False),
        out_shape=(split, split, packed),
        in_specs=[VMEM, VMEM, HBM],
        out_specs=(VMEM, VMEM, HBM),
        input_output_aliases={2: 2},
        compiler_params=PARAMS,
        cost_estimate=TINY,
        name="scatter",
    )(info, ablk, second)
    second = lax.ppermute(second, "gx", uneven + [(j, i) for i, j in uneven])

    partial = (
        jax.ShapeDtypeStruct((parts // 2, share, width), F32),
        jax.ShapeDtypeStruct((parts // 2, share, width), BF16),
    )
    own_t, keep, send = pl.pallas_call(
        functools.partial(own_kernel, parts),
        out_shape=(jax.ShapeDtypeStruct((width, rows * size), BF16),) + partial,
        in_specs=[VMEM, VMEM, VMEM],
        out_specs=(VMEM, VMEM, VMEM),
        scratch_shapes=[
            pltpu.VMEM((rows + 1, size, width), BF16),
            pltpu.VMEM((rows * size, width), BF16),
            pltpu.SMEM((rows, LANES), jnp.int32),
            pltpu.SemaphoreType.DMA,
        ],
        compiler_params=PARAMS,
        cost_estimate=MEDIUM,
        name="own",
    )(info, ablk, pblk)
    high, low = pl.pallas_call(
        functools.partial(scatter_kernel, True),
        out_shape=(split, split),
        in_specs=[VMEM, VMEM, VMEM, VMEM, VMEM],
        out_specs=(VMEM, VMEM),
        input_output_aliases={3: 0, 4: 1},
        compiler_params=PARAMS,
        cost_estimate=TINY,
        name="scatter",
    )(info, ablk, own_t, high, low)

    def ghost(order, ghosts, *more):
        return pl.pallas_call(
            functools.partial(ghost_kernel, order),
            out_shape=partial,
            in_specs=[VMEM] * (4 + len(more)),
            out_specs=(VMEM, VMEM),
            scratch_shapes=[
                pltpu.VMEM((count * size, width), BF16),
                pltpu.VMEM((rows * size, width), BF16),
            ]
            + [pltpu.VMEM((rows * size, count * size), BF16)] * (2 * order),
            compiler_params=PARAMS,
            cost_estimate=LONG,
            name="ghost",
        )(high, low, ghosts, own_t, *more)

    side_keep, side_send = ghost(0, first)
    keep, recv, folds, (side_send,) = folded(keep, send, parts, side_send)
    last = ghost(1, second, info, ablk, folds)
    token = pl.pallas_call(
        gate_kernel,
        out_shape=jax.ShapeDtypeStruct((8, LANES), F32),
        in_specs=[HBM],
        out_specs=VMEM,
        compiler_params=PARAMS,
        cost_estimate=LONG,
        name="gate",
    )(recv)
    sides = [folded(side_keep, side_send, parts), folded(*last, parts, token)]
    result = written(None, keep, recv, None)
    for order, (keep, recv, folds, later) in enumerate(sides):
        result = written(order, keep, recv, result)
    return result[None]


def solution(mesh):
    placed = (
        P("gx", "gy", None, None),
        P("gx", "gy", None),
        P("gx", "gy"),
        P("gx", "gy", None, None),
        P("gx", "gy", None),
        P("gx", "gy"),
    )
    return jax.shard_map(
        body, mesh=mesh, in_specs=placed, out_specs=P("gx", "gy", None), check_vma=False
    )
```

```python
import functools

import jax
import jax.numpy as jnp
from jax import lax
from jax.experimental import pallas as pl
from jax.experimental.pallas import tpu as pltpu
from jax.sharding import PartitionSpec as P

KA = 7
KS = 3
NCOL = 8
LANES = 128
WIDE = 256

F32 = jnp.float32
BF16 = jnp.bfloat16
SMEM = pl.BlockSpec(memory_space=pltpu.SMEM)
VMEM = pl.BlockSpec(memory_space=pltpu.VMEM)
HBM = pl.BlockSpec(memory_space=pltpu.HBM)
LONG = pl.CostEstimate(flops=10000000000, bytes_accessed=1000000, transcendentals=0)
MEDIUM = pl.CostEstimate(flops=1000000000, bytes_accessed=1000000, transcendentals=0)
SHORT = pl.CostEstimate(flops=100000000, bytes_accessed=1000000, transcendentals=0)
TINY = pl.CostEstimate(flops=1000000, bytes_accessed=1000000, transcendentals=0)
PARAMS = pltpu.CompilerParams(vmem_limit_bytes=24 * 1024 * 1024)


def spread(value, masks_of, width):
    size = value.shape[0]
    row = lax.broadcasted_iota(jnp.int32, (size, WIDE), 0)
    lane = lax.broadcasted_iota(jnp.int32, (size, WIDE), 1)
    unit = jnp.where(row == lane % size, 1.0, 0.0).astype(BF16)
    tiles = []
    for c in range(width // WIDE):
        moves = jnp.concatenate([unit * mask for mask in masks_of(c * WIDE // size)], axis=0)
        tiles.append(jnp.dot(value, moves, preferred_element_type=F32))
    return tiles


def masks_at(cols, size):
    slots = (lax.broadcasted_iota(jnp.int32, (1, WIDE), 1) // size).astype(F32)
    return lambda first: [
        jnp.where(slots == col - first, 1.0, 0.0).astype(BF16) for col in cols
    ]


def splats(info_ref, first, count, base):
    info = info_ref[...].astype(F32) - base
    shape = (info.shape[0], WIDE)
    return [jnp.broadcast_to(info[:, first + k : first + k + 1], shape) for k in range(count)]


def multiply(info, a_ref, base, ext_ref, prod_ref):
    rows, size = a_ref.shape[0], a_ref.shape[1]
    ext_ref[ext_ref.shape[0] - 1] = jnp.zeros(ext_ref.shape[1:], BF16)
    none = ext_ref.shape[0] - 1
    for n in range(rows):
        picks = []
        for k in range(KA):
            spot = info[n, k] - base
            good = (spot >= 0) & (spot < none)
            picks.append(jnp.where(good, spot, none))
        picked = jnp.concatenate([ext_ref[spot] for spot in picks], axis=0)
        value = jnp.dot(a_ref[n], picked, preferred_element_type=F32)
        prod_ref[n * size : (n + 1) * size, :] = value.astype(BF16)


def finish(ownt_ref, prod, keep_ref, send_ref):
    rows = ownt_ref.shape[0] // 2
    sent = jnp.dot(ownt_ref[rows:, :], prod, preferred_element_type=F32)
    send_ref[...] = sent.astype(BF16).reshape(send_ref.shape)
    kept = jnp.dot(ownt_ref[:rows, :], prod, preferred_element_type=F32)
    keep_ref[...] = kept.reshape(keep_ref.shape)


def pack_kernel(
    sends_in, pcol_in, acol_in, mush_in, p_in, first_ref, second_ref, info_out,
    sends, pcol, acol, mush, info, p_ref, packed_ref, sems,
):
    copies = [
        pltpu.make_async_copy(src, dst, sems.at[i])
        for i, (src, dst) in enumerate(
            ((sends_in, sends), (pcol_in, pcol), (acol_in, acol), (mush_in, mush), (p_in, p_ref))
        )
    ]
    for copy in copies:
        copy.start()
    for copy in copies[:4]:
        copy.wait()
    odd = lax.axis_index("gx") % 2
    rows, size = p_ref.shape[0], p_ref.shape[1]
    count = sends.shape[0] // 2
    slots = pcol.shape[0]
    starts = ((1 - odd) * count, odd * count)
    tail = packed_ref.shape[1] - count * size
    which = lax.broadcasted_iota(jnp.int32, (tail, packed_ref.shape[2]), 0)
    for i, start in enumerate(starts):
        cols = jnp.zeros(which.shape, F32)
        for s in range(count):
            row = sends[start + s]
            for j in range(slots):
                cols = jnp.where(which == s * slots + j, pcol[j, row].astype(F32), cols)
        packed_ref[i, count * size :, :] = cols.astype(BF16)
    copies[4].wait()
    copies = []
    for i, (out_ref, start) in enumerate(zip((first_ref, second_ref), starts)):
        for s in range(count):
            packed_ref[i, s * size : (s + 1) * size, :] = p_ref[sends[start + s]]
        copies.append(pltpu.make_async_copy(packed_ref.at[i], out_ref, sems.at[1 + i]))
        copies[-1].start()
    for n in range(rows):
        limit = jnp.where(mush[n] > 0, KA, KS)
        for k in range(KA):
            info[n, k] = jnp.where(k < limit, acol[k, 0, n], -1)
        for j in range(slots):
            info[n, KA + j] = pcol[j, n]
    passed = pltpu.make_async_copy(info, info_out, sems.at[0])
    passed.start()
    for copy in copies + [passed]:
        copy.wait()


def own_kernel(parts, info_ref, a_ref, p_ref, ownt_ref, keep_ref, send_ref, own_ref, prod_ref, info, sem):
    bit = lax.axis_index("gy") % 2
    rows, size = p_ref.shape[0], p_ref.shape[1]
    width = NCOL * size
    share = width // parts
    copy = pltpu.make_async_copy(info_ref, info, sem)
    copy.start()
    cols = splats(info_ref, KA, p_ref.shape[2] // size, 0)
    for n in range(rows):
        masks = masks_at([col[n : n + 1, :] for col in cols], size)
        for c, tile in enumerate(spread(p_ref[n], masks, width)):
            own_ref[n, :, c * WIDE : (c + 1) * WIDE] = tile.astype(BF16)
    copy.wait()
    multiply(info, a_ref, 0, own_ref, prod_ref)
    for c in range(width // LANES):
        column = own_ref[:rows, :, c * LANES : (c + 1) * LANES]
        flipped = column.reshape(rows * size, LANES).T
        for k in range(LANES // share):
            part = c * (LANES // share) + k
            spot = part // 2 + jnp.where(part % 2 == bit, 0, parts // 2)
            at = pl.ds(pl.multiple_of(spot * share, share), share)
            ownt_ref[at, :] = flipped[k * share : (k + 1) * share, :]
    finish(ownt_ref, prod_ref[...], keep_ref, send_ref)


def scatter(order, info_ref, a_ref, high_ref, low_ref):
    odd = lax.axis_index("gx") % 2
    right = odd if order else 1 - odd
    rows, size = a_ref.shape[0], a_ref.shape[1]
    width = high_ref.shape[1]
    base = rows + right * (width // size)
    cols = splats(info_ref, 0, KA, base.astype(F32))
    for n in range(rows):
        at = slice(n * size, (n + 1) * size)
        masks = masks_at([col[n : n + 1, :] for col in cols], size)
        for c, tile in enumerate(spread(a_ref[n], masks, width)):
            spot = slice(c * WIDE, (c + 1) * WIDE)
            high = tile.astype(BF16)
            high_ref[at, spot] = high
            low_ref[at, spot] = (tile - high.astype(F32)).astype(BF16)


def scatter_kernel(late, info_ref, a_ref, passed, *refs):
    laid = refs[-4:] if late else refs[-5:-1]
    place = lax.axis_index("gx")

    def side(order):
        scatter(order, info_ref, a_ref, *laid[2 * order : 2 * order + 2])

    if late:
        pl.when(place % 2 == 0)(lambda: side(0))
        pl.when((place % 2 == 1) | (place == 0))(lambda: side(1))
    else:
        pl.when(place % 2 == 1)(lambda: side(0))


def second_kernel(info_ref, a_ref, after, *refs):
    place = lax.axis_index("gx")
    pl.when((place % 2 == 0) & (place > 0))(lambda: scatter(1, info_ref, a_ref, *refs[-2:]))


def ghost_kernel(high_ref, low_ref, in_ref, ownt_ref, keep_ref, send_ref, ext_ref, prod_ref):
    width = ownt_ref.shape[0]
    size = width // NCOL
    slots = in_ref.shape[1] // size
    count = ext_ref.shape[0] // size
    cols = in_ref[count * size :, :].astype(F32)
    for n in range(count):
        at = slice(n * size, (n + 1) * size)
        masks = masks_at([cols[n * slots + j : n * slots + j + 1, :] for j in range(slots)], size)
        for c, tile in enumerate(spread(in_ref[at, :], masks, width)):
            ext_ref[at, c * WIDE : (c + 1) * WIDE] = tile.astype(BF16)

    ext = ext_ref[...]
    step = prod_ref.shape[0] // 2
    for m in range(2):
        at = slice(m * step, (m + 1) * step)
        value = jnp.dot(high_ref[at, :], ext, preferred_element_type=F32)
        value += jnp.dot(low_ref[at, :], ext, preferred_element_type=F32)
        prod_ref[at, :] = value.astype(BF16)
    finish(ownt_ref, prod_ref[...], keep_ref, send_ref)


def fold_kernel(stage, count, keep_ref, recv_ref, *refs):
    next_ref, send_ref = refs[count : count + 2]
    bit = (lax.axis_index("gy") >> stage) % 2
    for i in range(next_ref.shape[0]):
        mine, other = 2 * i + bit, 2 * i + 1 - bit
        send_ref[i] = (keep_ref[other] + recv_ref[other].astype(F32)).astype(BF16)
        next_ref[i] = keep_ref[mine] + recv_ref[mine].astype(F32)


def write_kernel(order, keep_ref, recv_ref, *refs):
    out_ref, sum_ref, sems = refs[-3:]
    odd = lax.axis_index("gx") % 2
    third = 1 if order is None else 2 * odd if order else 2 - 2 * odd
    share, width = sum_ref.shape
    spot = pl.ds(pl.multiple_of(third * width, width), width)
    count = sems.shape[0]
    copies = []
    for i in range(count):
        at = slice(i * share // count, (i + 1) * share // count)
        sum_ref[at, :] = keep_ref[0, at, :] + recv_ref[0, at, :].astype(F32)
        copies.append(pltpu.make_async_copy(sum_ref.at[at], out_ref.at[at, spot], sems.at[i]))
        copies[-1].start()
    for copy in copies:
        copy.wait()


def gate_kernel(recv_ref, token_ref):
    token_ref[...] = jnp.zeros(token_ref.shape, F32)


def swapped(value, axis, step):
    length = lax.axis_size(axis)
    return lax.ppermute(value, axis, [(i, i ^ step) for i in range(length) if i ^ step < length])


def folded(keep, send, parts, *passed):
    left, share, width = keep.shape
    stage = 0
    later = ()
    while left > 1:
        recv = swapped(send, "gy", 1 << stage)
        stage += 1
        left //= 2
        through = passed if stage == 1 else ()
        count = len(through)
        keep, send, *through = pl.pallas_call(
            functools.partial(fold_kernel, stage, count),
            out_shape=(
                jax.ShapeDtypeStruct((left, share, width), F32),
                jax.ShapeDtypeStruct((left, share, width), BF16),
            )
            + tuple(jax.ShapeDtypeStruct(value.shape, value.dtype) for value in through),
            in_specs=[VMEM] * (2 + count),
            out_specs=(VMEM,) * (2 + count),
            input_output_aliases={2 + i: 2 + i for i in range(count)},
            compiler_params=PARAMS,
            name="fold",
        )(keep, recv, *through)
        if stage == 1:
            later, folds = through, keep
    return keep, swapped(send, "gy", 1 << stage), folds, later


def written(order, keep, recv, result):
    share, width = keep.shape[1:]
    start = order is None
    whole = jax.ShapeDtypeStruct((share, 3 * width), F32)
    return pl.pallas_call(
        functools.partial(write_kernel, order),
        out_shape=whole,
        in_specs=[VMEM, VMEM] if start else [VMEM, VMEM, HBM],
        out_specs=HBM,
        input_output_aliases={} if start else {2: 0},
        scratch_shapes=[
            pltpu.VMEM((share, width), F32),
            pltpu.SemaphoreType.DMA((max(1, min(4, share // 16)),)),
        ],
        compiler_params=PARAMS,
        cost_estimate=SHORT,
        name="write",
    )(keep, recv, *([] if start else [result]))


def body(a_blocks, a_cols, mushy, p_blocks, p_cols, send_rows):
    rows, size, inner = p_blocks.shape[1:]
    acol, pcol = a_cols.transpose(2, 0, 1), p_cols[0].T
    mush, sends = mushy[0], send_rows[0]
    ablk, pblk = a_blocks[0], p_blocks[0]
    count = sends.shape[0] // 2
    width = NCOL * size
    length = lax.axis_size("gx")
    parts = lax.axis_size("gy")
    share = width // parts

    tail = -(-count * pcol.shape[0] // 16) * 16
    packed = jax.ShapeDtypeStruct((count * size + tail, inner), BF16)

    first, second, info = pl.pallas_call(
        pack_kernel,
        out_shape=(packed, packed, jax.ShapeDtypeStruct((rows, LANES), jnp.int32)),
        in_specs=[HBM] * 5,
        out_specs=(HBM, HBM, HBM),
        scratch_shapes=[
            pltpu.SMEM(sends.shape, sends.dtype),
            pltpu.SMEM(pcol.shape, pcol.dtype),
            pltpu.SMEM(acol.shape, acol.dtype),
            pltpu.SMEM(mush.shape, mush.dtype),
            pltpu.SMEM((rows, LANES), jnp.int32),
            pltpu.VMEM(pblk.shape, BF16),
            pltpu.VMEM((2,) + packed.shape, BF16),
            pltpu.SemaphoreType.DMA((5,)),
        ],
        compiler_params=pltpu.CompilerParams(vmem_limit_bytes=56 * 1024 * 1024),
        cost_estimate=LONG,
        name="pack",
    )(sends, pcol, acol, mush, pblk)
    even = [(i, i + 1) for i in range(0, length - 1, 2)]
    uneven = [(i, i + 1) for i in range(1, length - 1, 2)]
    first = lax.ppermute(first, "gx", even + [(j, i) for i, j in even])
    split = jax.ShapeDtypeStruct((rows * size, count * size), BF16)
    *laid, second = pl.pallas_call(
        functools.partial(scatter_kernel, False),
        out_shape=(split,) * 4 + (packed,),
        in_specs=[VMEM, VMEM, HBM],
        out_specs=(VMEM,) * 4 + (HBM,),
        input_output_aliases={2: 4},
        compiler_params=PARAMS,
        cost_estimate=TINY,
        name="scatter",
    )(info, ablk, second)
    second = lax.ppermute(second, "gx", uneven + [(j, i) for i, j in uneven])

    partial = (
        jax.ShapeDtypeStruct((parts // 2, share, width), F32),
        jax.ShapeDtypeStruct((parts // 2, share, width), BF16),
    )
    own_t, keep, send = pl.pallas_call(
        functools.partial(own_kernel, parts),
        out_shape=(jax.ShapeDtypeStruct((width, rows * size), BF16),) + partial,
        in_specs=[VMEM, VMEM, VMEM],
        out_specs=(VMEM, VMEM, VMEM),
        scratch_shapes=[
            pltpu.VMEM((rows + 1, size, width), BF16),
            pltpu.VMEM((rows * size, width), BF16),
            pltpu.SMEM((rows, LANES), jnp.int32),
            pltpu.SemaphoreType.DMA,
        ],
        compiler_params=PARAMS,
        cost_estimate=MEDIUM,
        name="own",
    )(info, ablk, pblk)
    laid = pl.pallas_call(
        functools.partial(scatter_kernel, True),
        out_shape=(split,) * 4,
        in_specs=[VMEM] * 7,
        out_specs=(VMEM,) * 4,
        input_output_aliases={3: 0, 4: 1, 5: 2, 6: 3},
        compiler_params=PARAMS,
        cost_estimate=TINY,
        name="scatter",
    )(info, ablk, own_t, *laid)

    def ghost(order, high, low, ghosts):
        return pl.pallas_call(
            ghost_kernel,
            out_shape=partial,
            in_specs=[VMEM] * 4,
            out_specs=(VMEM, VMEM),
            scratch_shapes=[
                pltpu.VMEM((count * size, width), BF16),
                pltpu.VMEM((rows * size, width), BF16),
            ],
            compiler_params=PARAMS,
            cost_estimate=LONG,
            name="ghost",
        )(high, low, ghosts, own_t)

    side_keep, side_send = ghost(0, *laid[:2], first)
    keep, recv, folds, (side_send,) = folded(keep, send, parts, side_send)
    more = pl.pallas_call(
        second_kernel,
        out_shape=(split, split),
        in_specs=[VMEM] * 5,
        out_specs=(VMEM, VMEM),
        input_output_aliases={3: 0, 4: 1},
        compiler_params=PARAMS,
        cost_estimate=TINY,
        name="scatter",
    )(info, ablk, folds, *laid[2:])
    last = ghost(1, *more, second)
    token = pl.pallas_call(
        gate_kernel,
        out_shape=jax.ShapeDtypeStruct((8, LANES), F32),
        in_specs=[HBM],
        out_specs=VMEM,
        compiler_params=PARAMS,
        cost_estimate=LONG,
        name="gate",
    )(recv)
    sides = [folded(side_keep, side_send, parts), folded(*last, parts, token)]
    result = written(None, keep, recv, None)
    for order, (keep, recv, folds, later) in enumerate(sides):
        result = written(order, keep, recv, result)
    return result[None]


def solution(mesh):
    placed = (
        P("gx", "gy", None, None),
        P("gx", "gy", None),
        P("gx", "gy"),
        P("gx", "gy", None, None),
        P("gx", "gy", None),
        P("gx", "gy"),
    )
    return jax.shard_map(
        body, mesh=mesh, in_specs=placed, out_specs=P("gx", "gy", None), check_vma=False
    )
```

```python
import functools

import jax
import jax.numpy as jnp
from jax import lax
from jax.experimental import pallas as pl
from jax.experimental.pallas import tpu as pltpu
from jax.sharding import PartitionSpec as P

KA = 7
KS = 3
NCOL = 8
LANES = 128
SPLIT = 2
WIDE = 256

F32 = jnp.float32
BF16 = jnp.bfloat16
SMEM = pl.BlockSpec(memory_space=pltpu.SMEM)
VMEM = pl.BlockSpec(memory_space=pltpu.VMEM)
HBM = pl.BlockSpec(memory_space=pltpu.HBM)
LONG = pl.CostEstimate(flops=10000000000, bytes_accessed=1000000, transcendentals=0)
MEDIUM = pl.CostEstimate(flops=1000000000, bytes_accessed=1000000, transcendentals=0)
SHORT = pl.CostEstimate(flops=100000000, bytes_accessed=1000000, transcendentals=0)
TINY = pl.CostEstimate(flops=1000000, bytes_accessed=1000000, transcendentals=0)
PARAMS = pltpu.CompilerParams(vmem_limit_bytes=24 * 1024 * 1024)


def spread(value, masks_of, width):
    size = value.shape[0]
    row = lax.broadcasted_iota(jnp.int32, (size, WIDE), 0)
    lane = lax.broadcasted_iota(jnp.int32, (size, WIDE), 1)
    unit = jnp.where(row == lane % size, 1.0, 0.0).astype(BF16)
    tiles = []
    for c in range(width // WIDE):
        moves = jnp.concatenate([unit * mask for mask in masks_of(c * WIDE // size)], axis=0)
        tiles.append(jnp.dot(value, moves, preferred_element_type=F32))
    return tiles


def masks_at(cols, size):
    slots = (lax.broadcasted_iota(jnp.int32, (1, WIDE), 1) // size).astype(F32)
    return lambda first: [
        jnp.where(slots == col - first, 1.0, 0.0).astype(BF16) for col in cols
    ]


def splats(info_ref, first, count, base):
    info = info_ref[...].astype(F32) - base
    shape = (info.shape[0], WIDE)
    return [jnp.broadcast_to(info[:, first + k : first + k + 1], shape) for k in range(count)]


def multiply(info, a_ref, base, ext_ref, prod_ref):
    rows, size = a_ref.shape[0], a_ref.shape[1]
    ext_ref[ext_ref.shape[0] - 1] = jnp.zeros(ext_ref.shape[1:], BF16)
    none = ext_ref.shape[0] - 1
    for n in range(rows):
        picks = []
        for k in range(KA):
            spot = info[n, k] - base
            good = (spot >= 0) & (spot < none)
            picks.append(jnp.where(good, spot, none))
        picked = jnp.concatenate([ext_ref[spot] for spot in picks], axis=0)
        value = jnp.dot(a_ref[n], picked, preferred_element_type=F32)
        prod_ref[n * size : (n + 1) * size, :] = value.astype(BF16)


def finish(ownt_ref, prod, keep_ref, *send_refs):
    rows = ownt_ref.shape[0] // 2
    sent = jnp.dot(ownt_ref[rows:, :], prod, preferred_element_type=F32).astype(BF16)
    wide = sent.shape[1] // len(send_refs)
    for i, send_ref in enumerate(send_refs):
        send_ref[...] = sent[:, i * wide : (i + 1) * wide].reshape(send_ref.shape)
    kept = jnp.dot(ownt_ref[:rows, :], prod, preferred_element_type=F32)
    keep_ref[...] = kept.reshape(keep_ref.shape)


def pack_kernel(
    sends_in, pcol_in, acol_in, mush_in, p_in, first_ref, second_ref, info_out,
    sends, pcol, acol, mush, info, p_ref, packed_ref, sems,
):
    copies = [
        pltpu.make_async_copy(src, dst, sems.at[i])
        for i, (src, dst) in enumerate(
            ((sends_in, sends), (pcol_in, pcol), (acol_in, acol), (mush_in, mush), (p_in, p_ref))
        )
    ]
    for copy in copies:
        copy.start()
    for copy in copies[:4]:
        copy.wait()
    odd = lax.axis_index("gx") % 2
    rows, size = p_ref.shape[0], p_ref.shape[1]
    count = sends.shape[0] // 2
    slots = pcol.shape[0]
    starts = ((1 - odd) * count, odd * count)
    tail = packed_ref.shape[1] - count * size
    which = lax.broadcasted_iota(jnp.int32, (tail, packed_ref.shape[2]), 0)
    for i, start in enumerate(starts):
        cols = jnp.zeros(which.shape, F32)
        for s in range(count):
            row = sends[start + s]
            for j in range(slots):
                cols = jnp.where(which == s * slots + j, pcol[j, row].astype(F32), cols)
        packed_ref[i, count * size :, :] = cols.astype(BF16)
    copies[4].wait()
    copies = []
    for i, (out_ref, start) in enumerate(zip((first_ref, second_ref), starts)):
        for s in range(count):
            packed_ref[i, s * size : (s + 1) * size, :] = p_ref[sends[start + s]]
        copies.append(pltpu.make_async_copy(packed_ref.at[i], out_ref, sems.at[1 + i]))
        copies[-1].start()
    for n in range(rows):
        limit = jnp.where(mush[n] > 0, KA, KS)
        for k in range(KA):
            info[n, k] = jnp.where(k < limit, acol[k, 0, n], -1)
        for j in range(slots):
            info[n, KA + j] = pcol[j, n]
    passed = pltpu.make_async_copy(info, info_out, sems.at[0])
    passed.start()
    for copy in copies + [passed]:
        copy.wait()


def own_kernel(parts, info_ref, a_ref, p_ref, ownt_ref, keep_ref, send_ref, own_ref, prod_ref, info, sem):
    bit = lax.axis_index("gy") % 2
    rows, size = p_ref.shape[0], p_ref.shape[1]
    width = NCOL * size
    share = width // parts
    copy = pltpu.make_async_copy(info_ref, info, sem)
    copy.start()
    cols = splats(info_ref, KA, p_ref.shape[2] // size, 0)
    for n in range(rows):
        masks = masks_at([col[n : n + 1, :] for col in cols], size)
        for c, tile in enumerate(spread(p_ref[n], masks, width)):
            own_ref[n, :, c * WIDE : (c + 1) * WIDE] = tile.astype(BF16)
    copy.wait()
    multiply(info, a_ref, 0, own_ref, prod_ref)
    for c in range(width // LANES):
        column = own_ref[:rows, :, c * LANES : (c + 1) * LANES]
        flipped = column.reshape(rows * size, LANES).T
        for k in range(LANES // share):
            part = c * (LANES // share) + k
            spot = part // 2 + jnp.where(part % 2 == bit, 0, parts // 2)
            at = pl.ds(pl.multiple_of(spot * share, share), share)
            ownt_ref[at, :] = flipped[k * share : (k + 1) * share, :]
    finish(ownt_ref, prod_ref[...], keep_ref, send_ref)


def scatter(order, info_ref, a_ref, high_ref, low_ref):
    odd = lax.axis_index("gx") % 2
    right = odd if order else 1 - odd
    rows, size = a_ref.shape[0], a_ref.shape[1]
    width = high_ref.shape[1]
    base = rows + right * (width // size)
    cols = splats(info_ref, 0, KA, base.astype(F32))
    for n in range(rows):
        at = slice(n * size, (n + 1) * size)
        masks = masks_at([col[n : n + 1, :] for col in cols], size)
        for c, tile in enumerate(spread(a_ref[n], masks, width)):
            spot = slice(c * WIDE, (c + 1) * WIDE)
            high = tile.astype(BF16)
            high_ref[at, spot] = high
            low_ref[at, spot] = (tile - high.astype(F32)).astype(BF16)


def scatter_kernel(late, info_ref, a_ref, passed, *refs):
    laid = refs[-4:] if late else refs[-5:-1]
    place = lax.axis_index("gx")

    def side(order):
        scatter(order, info_ref, a_ref, *laid[2 * order : 2 * order + 2])

    if late:
        pl.when(place % 2 == 0)(lambda: side(0))
        pl.when((place % 2 == 1) | (place == 0))(lambda: side(1))
    else:
        pl.when(place % 2 == 1)(lambda: side(0))


def second_kernel(info_ref, a_ref, after, *refs):
    place = lax.axis_index("gx")
    pl.when((place % 2 == 0) & (place > 0))(lambda: scatter(1, info_ref, a_ref, *refs[-2:]))


def ghost_kernel(high_ref, low_ref, in_ref, ownt_ref, keep_ref, *refs):
    *send_refs, ext_ref, prod_ref = refs
    width = ownt_ref.shape[0]
    size = width // NCOL
    slots = in_ref.shape[1] // size
    count = ext_ref.shape[0] // size
    cols = in_ref[count * size :, :].astype(F32)
    for n in range(count):
        at = slice(n * size, (n + 1) * size)
        masks = masks_at([cols[n * slots + j : n * slots + j + 1, :] for j in range(slots)], size)
        for c, tile in enumerate(spread(in_ref[at, :], masks, width)):
            ext_ref[at, c * WIDE : (c + 1) * WIDE] = tile.astype(BF16)

    ext = ext_ref[...]
    step = prod_ref.shape[0] // 2
    for m in range(2):
        at = slice(m * step, (m + 1) * step)
        value = jnp.dot(high_ref[at, :], ext, preferred_element_type=F32)
        value += jnp.dot(low_ref[at, :], ext, preferred_element_type=F32)
        prod_ref[at, :] = value.astype(BF16)
    finish(ownt_ref, prod_ref[...], keep_ref, *send_refs)


def fold_kernel(stage, pieces, count, keep_ref, *refs):
    recv_refs = refs[:pieces]
    next_ref, send_ref = refs[pieces + count : pieces + count + 2]
    bit = (lax.axis_index("gy") >> stage) % 2
    wide = keep_ref.shape[2] // pieces
    share = keep_ref.shape[1]
    if send_ref.shape[1] > share:
        send_ref[:, share:, :] = jnp.zeros_like(send_ref[:, share:, :])
    for c, recv_ref in enumerate(recv_refs):
        at = slice(c * wide, (c + 1) * wide)
        for i in range(next_ref.shape[0]):
            mine, other = 2 * i + bit, 2 * i + 1 - bit
            sent = keep_ref[other, :, at] + recv_ref[other].astype(F32)
            send_ref[i, : sent.shape[0], at] = sent.astype(BF16)
            next_ref[i, :, at] = keep_ref[mine, :, at] + recv_ref[mine].astype(F32)


def write_kernel(order, keep_ref, recv_ref, *refs):
    out_ref, sum_ref, sems = refs[-3:]
    odd = lax.axis_index("gx") % 2
    third = 1 if order is None else 2 * odd if order else 2 - 2 * odd
    share, width = sum_ref.shape
    spot = pl.ds(pl.multiple_of(third * width, width), width)
    count = sems.shape[0]
    copies = []
    for i in range(count):
        at = slice(i * share // count, (i + 1) * share // count)
        sum_ref[at, :] = keep_ref[0, at, :] + recv_ref[0, at, :].astype(F32)
        copies.append(pltpu.make_async_copy(sum_ref.at[at], out_ref.at[at, spot], sems.at[i]))
        copies[-1].start()
    for copy in copies:
        copy.wait()


def swapped(value, axis, step):
    length = lax.axis_size(axis)
    return lax.ppermute(value, axis, [(i, i ^ step) for i in range(length) if i ^ step < length])


def folded(keep, sends, parts, *passed, extra=0):
    left, share, width = keep.shape
    stage = 0
    later = ()
    while left > 1:
        recvs = [swapped(send, "gy", 1 << stage) for send in sends]
        stage += 1
        left //= 2
        through = passed if stage == 1 else ()
        count = len(through)
        keep, send, *through = pl.pallas_call(
            functools.partial(fold_kernel, stage, len(recvs), count),
            out_shape=(
                jax.ShapeDtypeStruct((left, share, width), F32),
                jax.ShapeDtypeStruct((left, share + (extra if left == 1 else 0), width), BF16),
            )
            + tuple(jax.ShapeDtypeStruct(value.shape, value.dtype) for value in through),
            in_specs=[VMEM] * (1 + len(recvs) + count),
            out_specs=(VMEM,) * (2 + count),
            input_output_aliases={1 + len(recvs) + i: 2 + i for i in range(count)},
            compiler_params=PARAMS,
            name="fold",
        )(keep, *recvs, *through)
        sends = [send]
        if stage == 1:
            later, folds = through, keep
    return keep, swapped(sends[0], "gy", 1 << stage), folds, later


def written(order, keep, recv, result, *after):
    share, width = keep.shape[1:]
    start = order is None
    whole = jax.ShapeDtypeStruct((share, 3 * width), F32)
    return pl.pallas_call(
        functools.partial(write_kernel, order),
        out_shape=whole,
        in_specs=[VMEM, VMEM] + ([VMEM] * len(after) if start else [HBM]),
        out_specs=HBM,
        input_output_aliases={} if start else {2: 0},
        scratch_shapes=[
            pltpu.VMEM((share, width), F32),
            pltpu.SemaphoreType.DMA((max(1, min(4, share // 16)),)),
        ],
        compiler_params=PARAMS,
        cost_estimate=TINY if start else LONG,
        name="write",
    )(keep, recv, *(after if start else [result]))


def body(a_blocks, a_cols, mushy, p_blocks, p_cols, send_rows):
    rows, size, inner = p_blocks.shape[1:]
    acol, pcol = a_cols.transpose(2, 0, 1), p_cols[0].T
    mush, sends = mushy[0], send_rows[0]
    ablk, pblk = a_blocks[0], p_blocks[0]
    count = sends.shape[0] // 2
    width = NCOL * size
    length = lax.axis_size("gx")
    parts = lax.axis_size("gy")
    share = width // parts

    tail = -(-count * pcol.shape[0] // 16) * 16
    packed = jax.ShapeDtypeStruct((count * size + tail, inner), BF16)

    first, second, info = pl.pallas_call(
        pack_kernel,
        out_shape=(packed, packed, jax.ShapeDtypeStruct((rows, LANES), jnp.int32)),
        in_specs=[HBM] * 5,
        out_specs=(HBM, HBM, HBM),
        scratch_shapes=[
            pltpu.SMEM(sends.shape, sends.dtype),
            pltpu.SMEM(pcol.shape, pcol.dtype),
            pltpu.SMEM(acol.shape, acol.dtype),
            pltpu.SMEM(mush.shape, mush.dtype),
            pltpu.SMEM((rows, LANES), jnp.int32),
            pltpu.VMEM(pblk.shape, BF16),
            pltpu.VMEM((2,) + packed.shape, BF16),
            pltpu.SemaphoreType.DMA((5,)),
        ],
        compiler_params=pltpu.CompilerParams(vmem_limit_bytes=56 * 1024 * 1024),
        cost_estimate=LONG,
        name="pack",
    )(sends, pcol, acol, mush, pblk)
    even = [(i, i + 1) for i in range(0, length - 1, 2)]
    uneven = [(i, i + 1) for i in range(1, length - 1, 2)]
    first = lax.ppermute(first, "gx", even + [(j, i) for i, j in even])
    split = jax.ShapeDtypeStruct((rows * size, count * size), BF16)
    *laid, second = pl.pallas_call(
        functools.partial(scatter_kernel, False),
        out_shape=(split,) * 4 + (packed,),
        in_specs=[VMEM, VMEM, HBM],
        out_specs=(VMEM,) * 4 + (HBM,),
        input_output_aliases={2: 4},
        compiler_params=PARAMS,
        cost_estimate=TINY,
        name="scatter",
    )(info, ablk, second)
    second = lax.ppermute(second, "gx", uneven + [(j, i) for i, j in uneven])

    partial = (
        jax.ShapeDtypeStruct((parts // 2, share, width), F32),
        jax.ShapeDtypeStruct((parts // 2, share, width), BF16),
    )
    own_t, keep, send = pl.pallas_call(
        functools.partial(own_kernel, parts),
        out_shape=(jax.ShapeDtypeStruct((width, rows * size), BF16),) + partial,
        in_specs=[VMEM, VMEM, VMEM],
        out_specs=(VMEM, VMEM, VMEM),
        scratch_shapes=[
            pltpu.VMEM((rows + 1, size, width), BF16),
            pltpu.VMEM((rows * size, width), BF16),
            pltpu.SMEM((rows, LANES), jnp.int32),
            pltpu.SemaphoreType.DMA,
        ],
        compiler_params=PARAMS,
        cost_estimate=MEDIUM,
        name="own",
    )(info, ablk, pblk)
    laid = pl.pallas_call(
        functools.partial(scatter_kernel, True),
        out_shape=(split,) * 4,
        in_specs=[VMEM] * 7,
        out_specs=(VMEM,) * 4,
        input_output_aliases={3: 0, 4: 1, 5: 2, 6: 3},
        compiler_params=PARAMS,
        cost_estimate=TINY,
        name="scatter",
    )(info, ablk, own_t, *laid)

    small = jax.ShapeDtypeStruct((parts // 2, share, width // SPLIT), BF16)

    def ghost(order, high, low, ghosts):
        return pl.pallas_call(
            ghost_kernel,
            out_shape=(partial[0],) + (small,) * SPLIT if order else partial,
            in_specs=[VMEM] * 4,
            out_specs=(VMEM,) * (1 + (SPLIT if order else 1)),
            scratch_shapes=[
                pltpu.VMEM((count * size, width), BF16),
                pltpu.VMEM((rows * size, width), BF16),
            ],
            compiler_params=PARAMS,
            cost_estimate=LONG,
            name="ghost",
        )(high, low, ghosts, own_t)

    side_keep, side_send = ghost(0, *laid[:2], first)
    keep, recv, folds, (side_send,) = folded(keep, [send], parts, side_send, extra=16)
    more = pl.pallas_call(
        second_kernel,
        out_shape=(split, split),
        in_specs=[VMEM] * 5,
        out_specs=(VMEM, VMEM),
        input_output_aliases={3: 0, 4: 1},
        compiler_params=PARAMS,
        cost_estimate=TINY,
        name="scatter",
    )(info, ablk, folds, *laid[2:])
    last_keep, *last_sends = ghost(1, *more, second)
    side_keep, side_recv, _, _ = folded(side_keep, [side_send], parts)
    last_keep, last_recv, _, (side_keep,) = folded(last_keep, last_sends, parts, side_keep)
    sides = [(side_keep, side_recv), (last_keep, last_recv)]
    result = written(None, keep, recv, None, last_keep)
    for order, (keep, recv) in enumerate(sides):
        result = written(order, keep, recv, result)
    return result[None]


def solution(mesh):
    placed = (
        P("gx", "gy", None, None),
        P("gx", "gy", None),
        P("gx", "gy"),
        P("gx", "gy", None, None),
        P("gx", "gy", None),
        P("gx", "gy"),
    )
    return jax.shard_map(
        body, mesh=mesh, in_specs=placed, out_specs=P("gx", "gy", None), check_vma=False
    )
```

```python
import functools

import jax
import jax.numpy as jnp
from jax import lax
from jax.experimental import pallas as pl
from jax.experimental.pallas import tpu as pltpu
from jax.sharding import PartitionSpec as P

KA = 7
KS = 3
NCOL = 8
LANES = 128
WIDE = 256

F32 = jnp.float32
BF16 = jnp.bfloat16
SMEM = pl.BlockSpec(memory_space=pltpu.SMEM)
VMEM = pl.BlockSpec(memory_space=pltpu.VMEM)
HBM = pl.BlockSpec(memory_space=pltpu.HBM)
LONG = pl.CostEstimate(flops=10000000000, bytes_accessed=1000000, transcendentals=0)
MEDIUM = pl.CostEstimate(flops=1000000000, bytes_accessed=1000000, transcendentals=0)
SHORT = pl.CostEstimate(flops=100000000, bytes_accessed=1000000, transcendentals=0)
TINY = pl.CostEstimate(flops=1000000, bytes_accessed=1000000, transcendentals=0)
PARAMS = pltpu.CompilerParams(vmem_limit_bytes=24 * 1024 * 1024)


def spread(value, masks_of, width):
    size = value.shape[0]
    row = lax.broadcasted_iota(jnp.int32, (size, WIDE), 0)
    lane = lax.broadcasted_iota(jnp.int32, (size, WIDE), 1)
    unit = jnp.where(row == lane % size, 1.0, 0.0).astype(BF16)
    tiles = []
    for c in range(width // WIDE):
        moves = jnp.concatenate([unit * mask for mask in masks_of(c * WIDE // size)], axis=0)
        tiles.append(jnp.dot(value, moves, preferred_element_type=F32))
    return tiles


def masks_at(cols, size):
    slots = (lax.broadcasted_iota(jnp.int32, (1, WIDE), 1) // size).astype(F32)
    return lambda first: [
        jnp.where(slots == col - first, 1.0, 0.0).astype(BF16) for col in cols
    ]


def splats(info_ref, first, count, base):
    info = info_ref[...].astype(F32) - base
    shape = (info.shape[0], WIDE)
    return [jnp.broadcast_to(info[:, first + k : first + k + 1], shape) for k in range(count)]


def multiply(info, a_ref, base, ext_ref, prod_ref):
    rows, size = a_ref.shape[0], a_ref.shape[1]
    ext_ref[ext_ref.shape[0] - 1] = jnp.zeros(ext_ref.shape[1:], BF16)
    none = ext_ref.shape[0] - 1
    for n in range(rows):
        picks = []
        for k in range(KA):
            spot = info[n, k] - base
            good = (spot >= 0) & (spot < none)
            picks.append(jnp.where(good, spot, none))
        picked = jnp.concatenate([ext_ref[spot] for spot in picks], axis=0)
        value = jnp.dot(a_ref[n], picked, preferred_element_type=F32)
        prod_ref[n * size : (n + 1) * size, :] = value.astype(BF16)


def finish(ownt_ref, prod, keep_ref, send_ref):
    rows = ownt_ref.shape[0] // 2
    sent = jnp.dot(ownt_ref[rows:, :], prod, preferred_element_type=F32)
    send_ref[...] = sent.astype(BF16).reshape(send_ref.shape)
    kept = jnp.dot(ownt_ref[:rows, :], prod, preferred_element_type=F32)
    keep_ref[...] = kept.reshape(keep_ref.shape)


def pack_kernel(
    sends_in, pcol_in, acol_in, mush_in, p_in, first_ref, second_ref, info_out,
    sends, pcol, acol, mush, info, p_ref, packed_ref, sems,
):
    copies = [
        pltpu.make_async_copy(src, dst, sems.at[i])
        for i, (src, dst) in enumerate(
            ((sends_in, sends), (pcol_in, pcol), (acol_in, acol), (mush_in, mush), (p_in, p_ref))
        )
    ]
    for copy in copies:
        copy.start()
    for copy in copies[:4]:
        copy.wait()
    odd = lax.axis_index("gx") % 2
    rows, size = p_ref.shape[0], p_ref.shape[1]
    count = sends.shape[0] // 2
    slots = pcol.shape[0]
    starts = ((1 - odd) * count, odd * count)
    tail = packed_ref.shape[1] - count * size
    which = lax.broadcasted_iota(jnp.int32, (tail, packed_ref.shape[2]), 0)
    for i, start in enumerate(starts):
        cols = jnp.zeros(which.shape, F32)
        for s in range(count):
            row = sends[start + s]
            for j in range(slots):
                cols = jnp.where(which == s * slots + j, pcol[j, row].astype(F32), cols)
        packed_ref[i, count * size :, :] = cols.astype(BF16)
    copies[4].wait()
    copies = []
    for i, (out_ref, start) in enumerate(zip((first_ref, second_ref), starts)):
        for s in range(count):
            packed_ref[i, s * size : (s + 1) * size, :] = p_ref[sends[start + s]]
        copies.append(pltpu.make_async_copy(packed_ref.at[i], out_ref, sems.at[1 + i]))
        copies[-1].start()
    for n in range(rows):
        limit = jnp.where(mush[n] > 0, KA, KS)
        for k in range(KA):
            info[n, k] = jnp.where(k < limit, acol[k, 0, n], -1)
        for j in range(slots):
            info[n, KA + j] = pcol[j, n]
    passed = pltpu.make_async_copy(info, info_out, sems.at[0])
    passed.start()
    for copy in copies + [passed]:
        copy.wait()


def own_kernel(parts, info_ref, a_ref, p_ref, ownt_ref, keep_ref, send_ref, own_ref, prod_ref, info, sem):
    bit = lax.axis_index("gy") % 2
    rows, size = p_ref.shape[0], p_ref.shape[1]
    width = NCOL * size
    share = width // parts
    copy = pltpu.make_async_copy(info_ref, info, sem)
    copy.start()
    cols = splats(info_ref, KA, p_ref.shape[2] // size, 0)
    for n in range(rows):
        masks = masks_at([col[n : n + 1, :] for col in cols], size)
        for c, tile in enumerate(spread(p_ref[n], masks, width)):
            own_ref[n, :, c * WIDE : (c + 1) * WIDE] = tile.astype(BF16)
    copy.wait()
    multiply(info, a_ref, 0, own_ref, prod_ref)
    for c in range(width // LANES):
        column = own_ref[:rows, :, c * LANES : (c + 1) * LANES]
        flipped = column.reshape(rows * size, LANES).T
        for k in range(LANES // share):
            part = c * (LANES // share) + k
            spot = part // 2 + jnp.where(part % 2 == bit, 0, parts // 2)
            at = pl.ds(pl.multiple_of(spot * share, share), share)
            ownt_ref[at, :] = flipped[k * share : (k + 1) * share, :]
    finish(ownt_ref, prod_ref[...], keep_ref, send_ref)


def scatter(order, info_ref, a_ref, high_ref, low_ref):
    odd = lax.axis_index("gx") % 2
    right = odd if order else 1 - odd
    rows, size = a_ref.shape[0], a_ref.shape[1]
    width = high_ref.shape[1]
    base = rows + right * (width // size)
    cols = splats(info_ref, 0, KA, base.astype(F32))
    for n in range(rows):
        at = slice(n * size, (n + 1) * size)
        masks = masks_at([col[n : n + 1, :] for col in cols], size)
        for c, tile in enumerate(spread(a_ref[n], masks, width)):
            spot = slice(c * WIDE, (c + 1) * WIDE)
            high = tile.astype(BF16)
            high_ref[at, spot] = high
            low_ref[at, spot] = (tile - high.astype(F32)).astype(BF16)


def early_kernel(info_ref, a_ref, passed, *refs):
    place = lax.axis_index("gx")
    pl.when(place % 2 == 1)(lambda: scatter(0, info_ref, a_ref, *refs[:2]))


def first_kernel(info_ref, a_ref, *refs):
    in_ref, ownt_ref, keep_ref, send_ref = refs[4:8]
    laid = refs[8:12]
    place = lax.axis_index("gx")
    pl.when(place % 2 == 0)(lambda: scatter(0, info_ref, a_ref, *laid[:2]))
    pl.when((place % 2 == 1) | (place == 0))(lambda: scatter(1, info_ref, a_ref, *laid[2:]))
    ghost_kernel(*laid[:2], in_ref, ownt_ref, keep_ref, send_ref, *refs[12:])


def second_kernel(info_ref, a_ref, after, *refs):
    place = lax.axis_index("gx")
    pl.when((place % 2 == 0) & (place > 0))(lambda: scatter(1, info_ref, a_ref, *refs[-2:]))


def ghost_kernel(high_ref, low_ref, in_ref, ownt_ref, keep_ref, send_ref, ext_ref, prod_ref):
    width = ownt_ref.shape[0]
    size = width // NCOL
    slots = in_ref.shape[1] // size
    count = ext_ref.shape[0] // size
    cols = in_ref[count * size :, :].astype(F32)
    for n in range(count):
        at = slice(n * size, (n + 1) * size)
        masks = masks_at([cols[n * slots + j : n * slots + j + 1, :] for j in range(slots)], size)
        for c, tile in enumerate(spread(in_ref[at, :], masks, width)):
            ext_ref[at, c * WIDE : (c + 1) * WIDE] = tile.astype(BF16)

    ext = ext_ref[...]
    step = prod_ref.shape[0] // 2
    for m in range(2):
        at = slice(m * step, (m + 1) * step)
        value = jnp.dot(high_ref[at, :], ext, preferred_element_type=F32)
        value += jnp.dot(low_ref[at, :], ext, preferred_element_type=F32)
        prod_ref[at, :] = value.astype(BF16)
    finish(ownt_ref, prod_ref[...], keep_ref, send_ref)


def fold_kernel(stage, count, keep_ref, recv_ref, *refs):
    next_ref, send_ref = refs[count : count + 2]
    bit = (lax.axis_index("gy") >> stage) % 2
    for i in range(next_ref.shape[0]):
        mine, other = 2 * i + bit, 2 * i + 1 - bit
        send_ref[i] = (keep_ref[other] + recv_ref[other].astype(F32)).astype(BF16)
        next_ref[i] = keep_ref[mine] + recv_ref[mine].astype(F32)


def write_kernel(order, keep_ref, recv_ref, *refs):
    out_ref, sum_ref, sems = refs[-3:]
    odd = lax.axis_index("gx") % 2
    third = 1 if order is None else 2 * odd if order else 2 - 2 * odd
    share, width = sum_ref.shape
    spot = pl.ds(pl.multiple_of(third * width, width), width)
    count = sems.shape[0]
    copies = []
    for i in range(count):
        at = slice(i * share // count, (i + 1) * share // count)
        sum_ref[at, :] = keep_ref[0, at, :] + recv_ref[0, at, :].astype(F32)
        copies.append(pltpu.make_async_copy(sum_ref.at[at], out_ref.at[at, spot], sems.at[i]))
        copies[-1].start()
    for copy in copies:
        copy.wait()


def gate_kernel(recv_ref, token_ref):
    token_ref[...] = jnp.zeros(token_ref.shape, F32)


def swapped(value, axis, step):
    length = lax.axis_size(axis)
    return lax.ppermute(value, axis, [(i, i ^ step) for i in range(length) if i ^ step < length])


def folded(keep, send, parts, *passed):
    left, share, width = keep.shape
    stage = 0
    later = ()
    while left > 1:
        recv = swapped(send, "gy", 1 << stage)
        stage += 1
        left //= 2
        through = passed if stage == 1 else ()
        count = len(through)
        keep, send, *through = pl.pallas_call(
            functools.partial(fold_kernel, stage, count),
            out_shape=(
                jax.ShapeDtypeStruct((left, share, width), F32),
                jax.ShapeDtypeStruct((left, share, width), BF16),
            )
            + tuple(jax.ShapeDtypeStruct(value.shape, value.dtype) for value in through),
            in_specs=[VMEM] * (2 + count),
            out_specs=(VMEM,) * (2 + count),
            input_output_aliases={2 + i: 2 + i for i in range(count)},
            compiler_params=PARAMS,
            name="fold",
        )(keep, recv, *through)
        if stage == 1:
            later, folds = through, keep
    return keep, swapped(send, "gy", 1 << stage), folds, later


def written(order, keep, recv, result):
    share, width = keep.shape[1:]
    start = order is None
    whole = jax.ShapeDtypeStruct((share, 3 * width), F32)
    return pl.pallas_call(
        functools.partial(write_kernel, order),
        out_shape=whole,
        in_specs=[VMEM, VMEM] if start else [VMEM, VMEM, HBM],
        out_specs=HBM,
        input_output_aliases={} if start else {2: 0},
        scratch_shapes=[
            pltpu.VMEM((share, width), F32),
            pltpu.SemaphoreType.DMA((max(1, min(4, share // 16)),)),
        ],
        compiler_params=PARAMS,
        cost_estimate=SHORT,
        name="write",
    )(keep, recv, *([] if start else [result]))


def body(a_blocks, a_cols, mushy, p_blocks, p_cols, send_rows):
    rows, size, inner = p_blocks.shape[1:]
    acol, pcol = a_cols.transpose(2, 0, 1), p_cols[0].T
    mush, sends = mushy[0], send_rows[0]
    ablk, pblk = a_blocks[0], p_blocks[0]
    count = sends.shape[0] // 2
    width = NCOL * size
    length = lax.axis_size("gx")
    parts = lax.axis_size("gy")
    share = width // parts

    tail = -(-count * pcol.shape[0] // 16) * 16
    packed = jax.ShapeDtypeStruct((count * size + tail, inner), BF16)

    first, second, info = pl.pallas_call(
        pack_kernel,
        out_shape=(packed, packed, jax.ShapeDtypeStruct((rows, LANES), jnp.int32)),
        in_specs=[HBM] * 5,
        out_specs=(HBM, HBM, HBM),
        scratch_shapes=[
            pltpu.SMEM(sends.shape, sends.dtype),
            pltpu.SMEM(pcol.shape, pcol.dtype),
            pltpu.SMEM(acol.shape, acol.dtype),
            pltpu.SMEM(mush.shape, mush.dtype),
            pltpu.SMEM((rows, LANES), jnp.int32),
            pltpu.VMEM(pblk.shape, BF16),
            pltpu.VMEM((2,) + packed.shape, BF16),
            pltpu.SemaphoreType.DMA((5,)),
        ],
        compiler_params=pltpu.CompilerParams(vmem_limit_bytes=56 * 1024 * 1024),
        cost_estimate=LONG,
        name="pack",
    )(sends, pcol, acol, mush, pblk)
    even = [(i, i + 1) for i in range(0, length - 1, 2)]
    uneven = [(i, i + 1) for i in range(1, length - 1, 2)]
    first = lax.ppermute(first, "gx", even + [(j, i) for i, j in even])
    split = jax.ShapeDtypeStruct((rows * size, count * size), BF16)
    *laid, second = pl.pallas_call(
        early_kernel,
        out_shape=(split,) * 4 + (packed,),
        in_specs=[VMEM, VMEM, HBM],
        out_specs=(VMEM,) * 4 + (HBM,),
        input_output_aliases={2: 4},
        compiler_params=PARAMS,
        cost_estimate=TINY,
        name="scatter",
    )(info, ablk, second)
    second = lax.ppermute(second, "gx", uneven + [(j, i) for i, j in uneven])

    partial = (
        jax.ShapeDtypeStruct((parts // 2, share, width), F32),
        jax.ShapeDtypeStruct((parts // 2, share, width), BF16),
    )
    own_t, keep, send = pl.pallas_call(
        functools.partial(own_kernel, parts),
        out_shape=(jax.ShapeDtypeStruct((width, rows * size), BF16),) + partial,
        in_specs=[VMEM, VMEM, VMEM],
        out_specs=(VMEM, VMEM, VMEM),
        scratch_shapes=[
            pltpu.VMEM((rows + 1, size, width), BF16),
            pltpu.VMEM((rows * size, width), BF16),
            pltpu.SMEM((rows, LANES), jnp.int32),
            pltpu.SemaphoreType.DMA,
        ],
        compiler_params=PARAMS,
        cost_estimate=MEDIUM,
        name="own",
    )(info, ablk, pblk)
    scratch = [
        pltpu.VMEM((count * size, width), BF16),
        pltpu.VMEM((rows * size, width), BF16),
    ]
    side_keep, side_send, *laid = pl.pallas_call(
        first_kernel,
        out_shape=partial + (split,) * 4,
        in_specs=[VMEM] * 8,
        out_specs=(VMEM,) * 6,
        input_output_aliases={2 + i: 2 + i for i in range(4)},
        scratch_shapes=scratch,
        compiler_params=PARAMS,
        cost_estimate=LONG,
        name="ghost",
    )(info, ablk, *laid, first, own_t)
    keep, recv, folds, (side_send,) = folded(keep, send, parts, side_send)
    more = pl.pallas_call(
        second_kernel,
        out_shape=(split, split),
        in_specs=[VMEM] * 5,
        out_specs=(VMEM, VMEM),
        input_output_aliases={3: 0, 4: 1},
        compiler_params=PARAMS,
        cost_estimate=TINY,
        name="scatter",
    )(info, ablk, folds, *laid[2:])
    last = pl.pallas_call(
        ghost_kernel,
        out_shape=partial,
        in_specs=[VMEM] * 4,
        out_specs=(VMEM, VMEM),
        scratch_shapes=scratch,
        compiler_params=PARAMS,
        cost_estimate=LONG,
        name="ghost",
    )(*more, second, own_t)
    token = pl.pallas_call(
        gate_kernel,
        out_shape=jax.ShapeDtypeStruct((8, LANES), F32),
        in_specs=[HBM],
        out_specs=VMEM,
        compiler_params=PARAMS,
        cost_estimate=LONG,
        name="gate",
    )(recv)
    sides = [folded(side_keep, side_send, parts), folded(*last, parts, token)]
    result = written(None, keep, recv, None)
    for order, (keep, recv, folds, later) in enumerate(sides):
        result = written(order, keep, recv, result)
    return result[None]


def solution(mesh):
    placed = (
        P("gx", "gy", None, None),
        P("gx", "gy", None),
        P("gx", "gy"),
        P("gx", "gy", None, None),
        P("gx", "gy", None),
        P("gx", "gy"),
    )
    return jax.shard_map(
        body, mesh=mesh, in_specs=placed, out_specs=P("gx", "gy", None), check_vma=False
    )
```

```python
import functools

import jax
import jax.numpy as jnp
from jax import lax
from jax.experimental import pallas as pl
from jax.experimental.pallas import tpu as pltpu
from jax.sharding import PartitionSpec as P

KA = 7
KS = 3
NCOL = 8
LANES = 128
WIDE = 256

F32 = jnp.float32
BF16 = jnp.bfloat16
SMEM = pl.BlockSpec(memory_space=pltpu.SMEM)
VMEM = pl.BlockSpec(memory_space=pltpu.VMEM)
HBM = pl.BlockSpec(memory_space=pltpu.HBM)
LONG = pl.CostEstimate(flops=10000000000, bytes_accessed=1000000, transcendentals=0)
MEDIUM = pl.CostEstimate(flops=1000000000, bytes_accessed=1000000, transcendentals=0)
SHORT = pl.CostEstimate(flops=100000000, bytes_accessed=1000000, transcendentals=0)
TINY = pl.CostEstimate(flops=1000000, bytes_accessed=1000000, transcendentals=0)
PARAMS = pltpu.CompilerParams(vmem_limit_bytes=24 * 1024 * 1024)


def spread(value, masks_of, width):
    size = value.shape[0]
    row = lax.broadcasted_iota(jnp.int32, (size, WIDE), 0)
    lane = lax.broadcasted_iota(jnp.int32, (size, WIDE), 1)
    unit = jnp.where(row == lane % size, 1.0, 0.0).astype(BF16)
    tiles = []
    for c in range(width // WIDE):
        moves = jnp.concatenate([unit * mask for mask in masks_of(c * WIDE // size)], axis=0)
        tiles.append(jnp.dot(value, moves, preferred_element_type=F32))
    return tiles


def masks_at(cols, size):
    slots = (lax.broadcasted_iota(jnp.int32, (1, WIDE), 1) // size).astype(F32)
    return lambda first: [
        jnp.where(slots == col - first, 1.0, 0.0).astype(BF16) for col in cols
    ]


def splats(info_ref, first, count, base):
    info = info_ref[...].astype(F32) - base
    shape = (info.shape[0], WIDE)
    return [jnp.broadcast_to(info[:, first + k : first + k + 1], shape) for k in range(count)]


def multiply(info, a_ref, base, ext_ref, prod_ref):
    rows, size = a_ref.shape[0], a_ref.shape[1]
    ext_ref[ext_ref.shape[0] - 1] = jnp.zeros(ext_ref.shape[1:], BF16)
    none = ext_ref.shape[0] - 1
    for n in range(rows):
        picks = []
        for k in range(KA):
            spot = info[n, k] - base
            good = (spot >= 0) & (spot < none)
            picks.append(jnp.where(good, spot, none))
        picked = jnp.concatenate([ext_ref[spot] for spot in picks], axis=0)
        value = jnp.dot(a_ref[n], picked, preferred_element_type=F32)
        prod_ref[n * size : (n + 1) * size, :] = value.astype(BF16)


def finish(ownt_ref, prod, keep_ref, send_ref):
    rows = ownt_ref.shape[0] // 2
    sent = jnp.dot(ownt_ref[rows:, :], prod, preferred_element_type=F32)
    send_ref[...] = sent.astype(BF16).reshape(send_ref.shape)
    kept = jnp.dot(ownt_ref[:rows, :], prod, preferred_element_type=F32)
    keep_ref[...] = kept.reshape(keep_ref.shape)


def pack_kernel(
    sends_in, pcol_in, acol_in, mush_in, p_in, first_ref, second_ref, info_out,
    sends, pcol, acol, mush, info, p_ref, packed_ref, sems,
):
    copies = [
        pltpu.make_async_copy(src, dst, sems.at[i])
        for i, (src, dst) in enumerate(
            ((sends_in, sends), (pcol_in, pcol), (acol_in, acol), (mush_in, mush), (p_in, p_ref))
        )
    ]
    for copy in copies:
        copy.start()
    for copy in copies[:4]:
        copy.wait()
    odd = lax.axis_index("gx") % 2
    rows, size = p_ref.shape[0], p_ref.shape[1]
    count = sends.shape[0] // 2
    slots = pcol.shape[0]
    starts = ((1 - odd) * count, odd * count)
    tail = packed_ref.shape[1] - count * size
    which = lax.broadcasted_iota(jnp.int32, (tail, packed_ref.shape[2]), 0)
    for i, start in enumerate(starts):
        cols = jnp.zeros(which.shape, F32)
        for s in range(count):
            row = sends[start + s]
            for j in range(slots):
                cols = jnp.where(which == s * slots + j, pcol[j, row].astype(F32), cols)
        packed_ref[i, count * size :, :] = cols.astype(BF16)
    copies[4].wait()
    copies = []
    for i, (out_ref, start) in enumerate(zip((first_ref, second_ref), starts)):
        for s in range(count):
            packed_ref[i, s * size : (s + 1) * size, :] = p_ref[sends[start + s]]
        copies.append(pltpu.make_async_copy(packed_ref.at[i], out_ref, sems.at[1 + i]))
        copies[-1].start()
    for n in range(rows):
        limit = jnp.where(mush[n] > 0, KA, KS)
        for k in range(KA):
            info[n, k] = jnp.where(k < limit, acol[k, 0, n], -1)
        for j in range(slots):
            info[n, KA + j] = pcol[j, n]
    passed = pltpu.make_async_copy(info, info_out, sems.at[0])
    passed.start()
    for copy in copies + [passed]:
        copy.wait()


def own_kernel(parts, info_ref, a_ref, p_ref, ownt_ref, keep_ref, send_ref, own_ref, prod_ref, info, sem):
    bit = lax.axis_index("gy") % 2
    rows, size = p_ref.shape[0], p_ref.shape[1]
    width = NCOL * size
    share = width // parts
    copy = pltpu.make_async_copy(info_ref, info, sem)
    copy.start()
    cols = splats(info_ref, KA, p_ref.shape[2] // size, 0)
    for n in range(rows):
        masks = masks_at([col[n : n + 1, :] for col in cols], size)
        for c, tile in enumerate(spread(p_ref[n], masks, width)):
            own_ref[n, :, c * WIDE : (c + 1) * WIDE] = tile.astype(BF16)
    copy.wait()
    multiply(info, a_ref, 0, own_ref, prod_ref)
    for c in range(width // LANES):
        column = own_ref[:rows, :, c * LANES : (c + 1) * LANES]
        flipped = column.reshape(rows * size, LANES).T
        for k in range(LANES // share):
            part = c * (LANES // share) + k
            spot = part // 2 + jnp.where(part % 2 == bit, 0, parts // 2)
            at = pl.ds(pl.multiple_of(spot * share, share), share)
            ownt_ref[at, :] = flipped[k * share : (k + 1) * share, :]
    finish(ownt_ref, prod_ref[...], keep_ref, send_ref)


def scatter(order, info_ref, a_ref, high_ref, low_ref):
    odd = lax.axis_index("gx") % 2
    right = odd if order else 1 - odd
    rows, size = a_ref.shape[0], a_ref.shape[1]
    width = high_ref.shape[1]
    base = rows + right * (width // size)
    cols = splats(info_ref, 0, KA, base.astype(F32))
    for n in range(rows):
        at = slice(n * size, (n + 1) * size)
        masks = masks_at([col[n : n + 1, :] for col in cols], size)
        for c, tile in enumerate(spread(a_ref[n], masks, width)):
            spot = slice(c * WIDE, (c + 1) * WIDE)
            high = tile.astype(BF16)
            high_ref[at, spot] = high
            low_ref[at, spot] = (tile - high.astype(F32)).astype(BF16)


def early_kernel(info_ref, a_ref, passed, *refs):
    place = lax.axis_index("gx")
    pl.when((place % 2 == 1) | (place == 0))(lambda: scatter(0, info_ref, a_ref, *refs[:2]))
    pl.when(place == 0)(lambda: scatter(1, info_ref, a_ref, *refs[2:4]))


def first_kernel(info_ref, a_ref, *refs):
    in_ref, ownt_ref, keep_ref, send_ref = refs[4:8]
    laid = refs[8:12]
    place = lax.axis_index("gx")
    pl.when((place % 2 == 0) & (place > 0))(lambda: scatter(0, info_ref, a_ref, *laid[:2]))
    pl.when(place % 2 == 1)(lambda: scatter(1, info_ref, a_ref, *laid[2:]))
    ghost_kernel(*laid[:2], in_ref, ownt_ref, keep_ref, send_ref, *refs[12:])


def second_kernel(info_ref, a_ref, after, *refs):
    place = lax.axis_index("gx")
    pl.when((place % 2 == 0) & (place > 0))(lambda: scatter(1, info_ref, a_ref, *refs[-2:]))


def ghost_kernel(high_ref, low_ref, in_ref, ownt_ref, keep_ref, send_ref, ext_ref, prod_ref):
    width = ownt_ref.shape[0]
    size = width // NCOL
    slots = in_ref.shape[1] // size
    count = ext_ref.shape[0] // size
    cols = in_ref[count * size :, :].astype(F32)
    for n in range(count):
        at = slice(n * size, (n + 1) * size)
        masks = masks_at([cols[n * slots + j : n * slots + j + 1, :] for j in range(slots)], size)
        for c, tile in enumerate(spread(in_ref[at, :], masks, width)):
            ext_ref[at, c * WIDE : (c + 1) * WIDE] = tile.astype(BF16)

    ext = ext_ref[...]
    step = prod_ref.shape[0] // 2
    for m in range(2):
        at = slice(m * step, (m + 1) * step)
        value = jnp.dot(high_ref[at, :], ext, preferred_element_type=F32)
        value += jnp.dot(low_ref[at, :], ext, preferred_element_type=F32)
        prod_ref[at, :] = value.astype(BF16)
    finish(ownt_ref, prod_ref[...], keep_ref, send_ref)


def fold_kernel(stage, count, keep_ref, recv_ref, *refs):
    next_ref, send_ref = refs[count : count + 2]
    bit = (lax.axis_index("gy") >> stage) % 2
    for i in range(next_ref.shape[0]):
        mine, other = 2 * i + bit, 2 * i + 1 - bit
        send_ref[i] = (keep_ref[other] + recv_ref[other].astype(F32)).astype(BF16)
        next_ref[i] = keep_ref[mine] + recv_ref[mine].astype(F32)


def write_kernel(order, keep_ref, recv_ref, *refs):
    out_ref, sum_ref, sems = refs[-3:]
    odd = lax.axis_index("gx") % 2
    third = 1 if order is None else 2 * odd if order else 2 - 2 * odd
    share, width = sum_ref.shape
    spot = pl.ds(pl.multiple_of(third * width, width), width)
    count = sems.shape[0]
    copies = []
    for i in range(count):
        at = slice(i * share // count, (i + 1) * share // count)
        sum_ref[at, :] = keep_ref[0, at, :] + recv_ref[0, at, :].astype(F32)
        copies.append(pltpu.make_async_copy(sum_ref.at[at], out_ref.at[at, spot], sems.at[i]))
        copies[-1].start()
    for copy in copies:
        copy.wait()


def gate_kernel(recv_ref, token_ref):
    token_ref[...] = jnp.zeros(token_ref.shape, F32)


def swapped(value, axis, step):
    length = lax.axis_size(axis)
    return lax.ppermute(value, axis, [(i, i ^ step) for i in range(length) if i ^ step < length])


def folded(keep, send, parts, *passed):
    left, share, width = keep.shape
    stage = 0
    later = ()
    while left > 1:
        recv = swapped(send, "gy", 1 << stage)
        stage += 1
        left //= 2
        through = passed if stage == 1 else ()
        count = len(through)
        keep, send, *through = pl.pallas_call(
            functools.partial(fold_kernel, stage, count),
            out_shape=(
                jax.ShapeDtypeStruct((left, share, width), F32),
                jax.ShapeDtypeStruct((left, share, width), BF16),
            )
            + tuple(jax.ShapeDtypeStruct(value.shape, value.dtype) for value in through),
            in_specs=[VMEM] * (2 + count),
            out_specs=(VMEM,) * (2 + count),
            input_output_aliases={2 + i: 2 + i for i in range(count)},
            compiler_params=PARAMS,
            name="fold",
        )(keep, recv, *through)
        if stage == 1:
            later, folds = through, keep
    return keep, swapped(send, "gy", 1 << stage), folds, later


def written(order, keep, recv, result):
    share, width = keep.shape[1:]
    start = order is None
    whole = jax.ShapeDtypeStruct((share, 3 * width), F32)
    return pl.pallas_call(
        functools.partial(write_kernel, order),
        out_shape=whole,
        in_specs=[VMEM, VMEM] if start else [VMEM, VMEM, HBM],
        out_specs=HBM,
        input_output_aliases={} if start else {2: 0},
        scratch_shapes=[
            pltpu.VMEM((share, width), F32),
            pltpu.SemaphoreType.DMA((max(1, min(4, share // 16)),)),
        ],
        compiler_params=PARAMS,
        cost_estimate=SHORT,
        name="write",
    )(keep, recv, *([] if start else [result]))


def body(a_blocks, a_cols, mushy, p_blocks, p_cols, send_rows):
    rows, size, inner = p_blocks.shape[1:]
    acol, pcol = a_cols.transpose(2, 0, 1), p_cols[0].T
    mush, sends = mushy[0], send_rows[0]
    ablk, pblk = a_blocks[0], p_blocks[0]
    count = sends.shape[0] // 2
    width = NCOL * size
    length = lax.axis_size("gx")
    parts = lax.axis_size("gy")
    share = width // parts

    tail = -(-count * pcol.shape[0] // 16) * 16
    packed = jax.ShapeDtypeStruct((count * size + tail, inner), BF16)

    first, second, info = pl.pallas_call(
        pack_kernel,
        out_shape=(packed, packed, jax.ShapeDtypeStruct((rows, LANES), jnp.int32)),
        in_specs=[HBM] * 5,
        out_specs=(HBM, HBM, HBM),
        scratch_shapes=[
            pltpu.SMEM(sends.shape, sends.dtype),
            pltpu.SMEM(pcol.shape, pcol.dtype),
            pltpu.SMEM(acol.shape, acol.dtype),
            pltpu.SMEM(mush.shape, mush.dtype),
            pltpu.SMEM((rows, LANES), jnp.int32),
            pltpu.VMEM(pblk.shape, BF16),
            pltpu.VMEM((2,) + packed.shape, BF16),
            pltpu.SemaphoreType.DMA((5,)),
        ],
        compiler_params=pltpu.CompilerParams(vmem_limit_bytes=56 * 1024 * 1024),
        cost_estimate=LONG,
        name="pack",
    )(sends, pcol, acol, mush, pblk)
    even = [(i, i + 1) for i in range(0, length - 1, 2)]
    uneven = [(i, i + 1) for i in range(1, length - 1, 2)]
    first = lax.ppermute(first, "gx", even + [(j, i) for i, j in even])
    split = jax.ShapeDtypeStruct((rows * size, count * size), BF16)
    *laid, second = pl.pallas_call(
        early_kernel,
        out_shape=(split,) * 4 + (packed,),
        in_specs=[VMEM, VMEM, HBM],
        out_specs=(VMEM,) * 4 + (HBM,),
        input_output_aliases={2: 4},
        compiler_params=PARAMS,
        cost_estimate=TINY,
        name="scatter",
    )(info, ablk, second)
    second = lax.ppermute(second, "gx", uneven + [(j, i) for i, j in uneven])

    partial = (
        jax.ShapeDtypeStruct((parts // 2, share, width), F32),
        jax.ShapeDtypeStruct((parts // 2, share, width), BF16),
    )
    own_t, keep, send = pl.pallas_call(
        functools.partial(own_kernel, parts),
        out_shape=(jax.ShapeDtypeStruct((width, rows * size), BF16),) + partial,
        in_specs=[VMEM, VMEM, VMEM],
        out_specs=(VMEM, VMEM, VMEM),
        scratch_shapes=[
            pltpu.VMEM((rows + 1, size, width), BF16),
            pltpu.VMEM((rows * size, width), BF16),
            pltpu.SMEM((rows, LANES), jnp.int32),
            pltpu.SemaphoreType.DMA,
        ],
        compiler_params=PARAMS,
        cost_estimate=MEDIUM,
        name="own",
    )(info, ablk, pblk)
    scratch = [
        pltpu.VMEM((count * size, width), BF16),
        pltpu.VMEM((rows * size, width), BF16),
    ]
    side_keep, side_send, *laid = pl.pallas_call(
        first_kernel,
        out_shape=partial + (split,) * 4,
        in_specs=[VMEM] * 8,
        out_specs=(VMEM,) * 6,
        input_output_aliases={2 + i: 2 + i for i in range(4)},
        scratch_shapes=scratch,
        compiler_params=PARAMS,
        cost_estimate=LONG,
        name="ghost",
    )(info, ablk, *laid, first, own_t)
    keep, recv, folds, (side_send,) = folded(keep, send, parts, side_send)
    more = pl.pallas_call(
        second_kernel,
        out_shape=(split, split),
        in_specs=[VMEM] * 5,
        out_specs=(VMEM, VMEM),
        input_output_aliases={3: 0, 4: 1},
        compiler_params=PARAMS,
        cost_estimate=TINY,
        name="scatter",
    )(info, ablk, folds, *laid[2:])
    last = pl.pallas_call(
        ghost_kernel,
        out_shape=partial,
        in_specs=[VMEM] * 4,
        out_specs=(VMEM, VMEM),
        scratch_shapes=scratch,
        compiler_params=PARAMS,
        cost_estimate=LONG,
        name="ghost",
    )(*more, second, own_t)
    token = pl.pallas_call(
        gate_kernel,
        out_shape=jax.ShapeDtypeStruct((8, LANES), F32),
        in_specs=[HBM],
        out_specs=VMEM,
        compiler_params=PARAMS,
        cost_estimate=LONG,
        name="gate",
    )(recv)
    sides = [folded(side_keep, side_send, parts), folded(*last, parts, token)]
    result = written(None, keep, recv, None)
    for order, (keep, recv, folds, later) in enumerate(sides):
        result = written(order, keep, recv, result)
    return result[None]


def solution(mesh):
    placed = (
        P("gx", "gy", None, None),
        P("gx", "gy", None),
        P("gx", "gy"),
        P("gx", "gy", None, None),
        P("gx", "gy", None),
        P("gx", "gy"),
    )
    return jax.shard_map(
        body, mesh=mesh, in_specs=placed, out_specs=P("gx", "gy", None), check_vma=False
    )
```
